32 devices in a mesh: frame: 4 (over x, core), clip: 8 (over z, y).
Axes of the slice: x: 2, y: 2, z: 4, core: 2. Of those that a mesh axis runs over, the one named last changes fastest.
Arguments:
- tokens: bfloat16 [96, 320, 768], P('clip', 'frame'), may hold values from -6 to 6
- cotangent: bfloat16 [96, 320, 768], P('clip', 'frame'), may hold values from -6 to 6
- frame_count: int32 [96], P('clip'), may hold values from 1 to 8, as said below
- image_group: int32 [96, 8], P('clip', 'frame'), may hold values from 0 to 3
- keep_mask: int32 [96, 320], P('clip', 'frame'), may hold values from 0 to 1, as said below
- attn_norm_gain: bfloat16 [768], P(('frame', 'clip')), may hold values from 0.5 to 1.5
- attn_norm_bias: bfloat16 [768], P(('frame', 'clip')), may hold values from -1.5 to 1.5
- w_qkv: bfloat16 [768, 2304], P(('frame', 'clip')), may hold values from -0.21875 to 0.21875
- query_bias: bfloat16 [768], P(('frame', 'clip')), may hold values from -1.5 to 1.5
- value_bias: bfloat16 [768], P(('frame', 'clip')), may hold values from -1.5 to 1.5
- w_out: bfloat16 [768, 768], P(('frame', 'clip')), may hold values from -0.625 to 0.625
- out_bias: bfloat16 [768], P(('frame', 'clip')), may hold values from -1.5 to 1.5
- mlp_norm_gain: bfloat16 [768], P(('frame', 'clip')), may hold values from 0.5 to 1.5
- mlp_norm_bias: bfloat16 [768], P(('frame', 'clip')), may hold values from -1.5 to 1.5
- w_up: bfloat16 [768, 3072], P(('frame', 'clip')), may hold values from -0.21875 to 0.21875
- up_bias: bfloat16 [3072], P(('frame', 'clip')), may hold values from -1.5 to 1.5
- w_down: bfloat16 [3072, 768], P(('frame', 'clip')), may hold values from -0.109375 to 0.109375
- down_bias: bfloat16 [768], P(('frame', 'clip')), may hold values from -1.5 to 1.5
Outputs:
- output: bfloat16 [96, 320, 768], P('clip', 'frame')
- input_grad: float32 [96, 320, 768], P('clip', 'frame')
- grad_attn_norm_gain: float32 [768], P(('frame', 'clip'))
- grad_attn_norm_bias: float32 [768], P(('frame', 'clip'))
- grad_w_qkv: float32 [768, 2304], P(('frame', 'clip'))
- grad_query_bias: float32 [768], P(('frame', 'clip'))
- grad_value_bias: float32 [768], P(('frame', 'clip'))
- grad_w_out: float32 [768, 768], P(('frame', 'clip'))
- grad_out_bias: float32 [768], P(('frame', 'clip'))
- grad_mlp_norm_gain: float32 [768], P(('frame', 'clip'))
- grad_mlp_norm_bias: float32 [768], P(('frame', 'clip'))
- grad_w_up: float32 [768, 3072], P(('frame', 'clip'))
- grad_up_bias: float32 [3072], P(('frame', 'clip'))
- grad_w_down: float32 [3072, 768], P(('frame', 'clip'))
- grad_down_bias: float32 [768], P(('frame', 'clip'))
The draws below stay inside these ranges and needn't reach their ends.
Inputs may be any that keep to these rules, and one draw needn't show every extreme that they name: The first frame_count frames of a slot are one clip, the others single images; in each aligned run of 12 slots one slot holds a clip of all 8 frames. `image_group`: entries of frames that belong to the clip are unused. `keep_mask`: every frame of every slot keeps at least one of its 40 positions.
All inputs are finite; a program needn't handle non-finite values.
Results may differ from the reference program's by a relative error of at most 0.012.
Values may be sent and summed in bfloat16 or wider, within the bound.
No kernel may reach another device: no remote copies, remote signals or barrier semaphores. Data moves between devices by JAX's collectives and lax.ppermute only.
A program may use at most 256 MiB of HBM per device.

```python
import jax
import jax.numpy as jnp
from jax import lax

D = 768
HEADS = 12
HEAD_DIM = 64
FF = 3072
FRAMES = 8
BLOCK = 40
SLOTS = 12
CLIPS = 96
LENGTH = 320


def draw_frame_count(key, part):
    key = jax.random.fold_in(key, 11)
    first_key, second_key = jax.random.split(key)
    row_count = CLIPS // SLOTS
    counts = jax.random.randint(first_key, (row_count, SLOTS), 1, FRAMES + 1)
    chosen = jax.random.randint(second_key, (row_count, 1), 0, SLOTS)
    slot_index = jnp.arange(SLOTS, dtype=jnp.int32)[None, :]
    filled = jnp.where(slot_index == chosen, FRAMES, counts)
    return filled.reshape(CLIPS).astype(jnp.int32)


def draw_keep_mask(key, part):
    key = jax.random.fold_in(key, 23)
    count_key, order_key = jax.random.split(key)
    kept_count = jax.random.randint(count_key, (CLIPS, FRAMES, 1), 1, BLOCK + 1)
    scores = jax.random.randint(order_key, (CLIPS, FRAMES, BLOCK), 0, 1 << 20) * BLOCK + jnp.arange(BLOCK, dtype=jnp.int32)
    ranking = jnp.argsort(jnp.argsort(scores, axis=-1, stable=True), axis=-1, stable=True)
    return (ranking < kept_count).astype(jnp.int32).reshape(CLIPS, FRAMES * BLOCK)


def plant(values, key, smallest, high):
    spot = [jax.random.randint(jax.random.fold_in(key, axis), (), 0, length) for axis, length in enumerate(values.shape)]
    main_axis = values.shape.index(max(values.shape))
    neighbour = spot[:main_axis] + [(spot[main_axis] + 1) % values.shape[main_axis]] + spot[main_axis + 1:]
    return values.at[tuple(spot)].set(smallest).at[tuple(neighbour)].set(high)


def levels(rng, extent, cuts, least, top_value):
    def one(axis_at, shards_of):
        heights = jax.random.uniform(jax.random.fold_in(jax.random.fold_in(rng, 6), axis_at), (shards_of,), jnp.float32, least / len(cuts), top_value / len(cuts))
        return jnp.repeat(jnp.exp(heights), extent[axis_at] // shards_of).reshape((-1,) + (1,) * (len(extent) - axis_at - 1))

    factor_of = one(*cuts[0])
    for cut in cuts[1:]:
        factor_of = factor_of * one(*cut)
    return factor_of


def gaussian(stream_key, dims, width, bound, cuts=(), kind=jnp.bfloat16):
    values = width * jax.random.normal(stream_key, dims, jnp.float32)
    if cuts:
        values = values * levels(stream_key, dims, cuts, -0.22, 0.18)
    return jnp.clip(values, -bound, bound).astype(kind)


def setup_inputs(seed: int = 0) -> dict:
    splits = jax.random.split(jax.random.key(seed), 19)
    tokens = gaussian(splits[0], (CLIPS, LENGTH, D), 1.0, 6.0, ((0, 8), (1, 4)))
    cotangent = gaussian(splits[1], (CLIPS, LENGTH, D), 1.0, 6.0, ((0, 8), (1, 4)))
    frame_count = draw_frame_count(jax.random.fold_in(splits[18], 71), 0)
    image_group = plant(jax.random.randint(splits[3], (CLIPS, FRAMES), 0, 4), jax.random.fold_in(splits[3], 1), 0, 3).astype(jnp.int32)
    keep_mask = draw_keep_mask(jax.random.fold_in(splits[18], 71), 0)
    attn_norm_gain = jnp.clip(1.0 + 0.1 * jax.random.normal(splits[5], (D,), jnp.float32), 0.5, 1.5).astype(jnp.bfloat16)
    attn_norm_bias = gaussian(splits[6], (D,), 0.3, 1.5, ((0, 32),))
    w_qkv = gaussian(splits[7], (D, 3 * D), D ** -0.5, 0.21875, ((0, 32),))
    query_bias = gaussian(splits[8], (D,), 0.3, 1.5, ((0, 32),))
    value_bias = gaussian(splits[9], (D,), 0.3, 1.5, ((0, 32),))
    w_out = gaussian(splits[10], (D, D), (D // 8) ** -0.5, 0.625, ((0, 32),))
    out_bias = gaussian(splits[11], (D,), 0.3, 1.5, ((0, 32),))
    mlp_norm_gain = jnp.clip(1.0 + 0.1 * jax.random.normal(splits[12], (D,), jnp.float32), 0.5, 1.5).astype(jnp.bfloat16)
    mlp_norm_bias = gaussian(splits[13], (D,), 0.3, 1.5, ((0, 32),))
    w_up = gaussian(splits[14], (D, FF), D ** -0.5, 0.21875, ((0, 32),))
    up_bias = gaussian(splits[15], (FF,), 0.3, 1.5, ((0, 32),))
    w_down = gaussian(splits[16], (FF, D), FF ** -0.5, 0.109375, ((0, 32),))
    down_bias = gaussian(splits[17], (D,), 0.3, 1.5, ((0, 32),))
    return dict(tokens=tokens, cotangent=cotangent, frame_count=frame_count, image_group=image_group, keep_mask=keep_mask, attn_norm_gain=attn_norm_gain, attn_norm_bias=attn_norm_bias, w_qkv=w_qkv, query_bias=query_bias, value_bias=value_bias, w_out=w_out, out_bias=out_bias, mlp_norm_gain=mlp_norm_gain, mlp_norm_bias=mlp_norm_bias, w_up=w_up, up_bias=up_bias, w_down=w_down, down_bias=down_bias)


@jax.custom_vjp
def low(v):
    return lax.optimization_barrier(v.astype(jnp.bfloat16)).astype(jnp.float32)

@jax.custom_vjp
def low_back(v):
    return v

def low_keep(v):
    return (low(v), None)

def low_pass(kept, grad):
    return (grad,)

def back_keep(v):
    return (v, None)

def back_low(kept, grad):
    return (low(grad),)
low.defvjp(low_keep, low_pass)
low_back.defvjp(back_keep, back_low)
EPSILON = 1e-06
HIGHEST = lax.Precision.HIGHEST

def layer_norm(values, gain, shift):
    center = values - lax.optimization_barrier(jnp.mean(values, axis=-1, keepdims=True))
    spread = lax.optimization_barrier(jnp.mean(center * center, axis=-1, keepdims=True))
    return center * lax.rsqrt(spread + EPSILON) * gain + shift

def project(values, weight):
    return jnp.einsum('gld,de->gle', values, weight, precision=HIGHEST)

def forward(inputs, params, token_segment, key_code, kept_rows):
    attn_gain, attn_shift, w_qkv, query_bias, value_bias, w_out, out_bias, mlp_gain, mlp_shift, w_up, up_bias, w_down, down_bias = params
    model_width = w_out.shape[0]
    group_size, length = (inputs.shape[0], inputs.shape[1])
    head_shape = (group_size, length, HEADS, HEAD_DIM)
    first_norm = low(layer_norm(inputs, attn_gain, attn_shift))
    projected = project(first_norm, w_qkv)
    queries = low_back(low(projected[..., :model_width] + query_bias))
    key_rows = low_back(low(projected[..., model_width:2 * model_width]))
    value_rows = low_back(low(projected[..., 2 * model_width:] + value_bias))
    scores = jnp.einsum('gqhd,gkhd->ghqk', queries.reshape(head_shape), key_rows.reshape(head_shape), precision=HIGHEST)
    scores = low_back(scores * HEAD_DIM ** (-0.5))
    allowed = token_segment[:, None, :, None] == key_code[:, None, None, :]
    masked = jnp.where(allowed, scores, -1e+30)
    row_max = lax.optimization_barrier(jnp.max(masked, axis=-1, keepdims=True))
    weights = jnp.where(allowed, jnp.exp(masked - row_max), 0.0)
    probability = weights / lax.optimization_barrier(jnp.sum(weights, axis=-1, keepdims=True))
    attended = jnp.einsum('ghqk,gkhd->gqhd', low(probability), value_rows.reshape(head_shape), precision=HIGHEST)
    attended = low_back(low(attended.reshape(group_size, length, model_width)))
    branch = low_back(project(attended, w_out) + out_bias)
    middle = inputs + branch
    second_norm = low(layer_norm(middle, mlp_gain, mlp_shift))
    hidden = low_back(project(second_norm, w_up) + up_bias)
    active = low(jax.nn.gelu(hidden, approximate=False))
    result = low_back(project(active, w_down) + down_bias)
    return kept_rows[..., None] * (middle + result)

def reference(tokens, cotangent, frame_count, image_group, keep_mask, attn_norm_gain, attn_norm_bias, w_qkv, query_bias, value_bias, w_out, out_bias, mlp_norm_gain, mlp_norm_bias, w_up, up_bias, w_down, down_bias):
    params = jax.tree.map(lambda array: array.astype(jnp.float32), (attn_norm_gain, attn_norm_bias, w_qkv, query_bias, value_bias, w_out, out_bias, mlp_norm_gain, mlp_norm_bias, w_up, up_bias, w_down, down_bias))
    frame_index = jnp.arange(FRAMES, dtype=jnp.int32)[None, :]
    segment = jnp.where(frame_index < frame_count[:, None], 0, 1 + image_group).astype(jnp.int32)
    token_segment = jnp.repeat(segment, BLOCK, axis=1).astype(jnp.int32)
    key_code = jnp.where(keep_mask == 1, token_segment, -1).astype(jnp.int32)
    kept_rows = keep_mask.astype(jnp.float32)
    group_count = CLIPS // SLOTS

    def regroup(array):
        return array.reshape((group_count, SLOTS) + array.shape[1:])
    zeros = jax.tree.map(jnp.zeros_like, params)

    def one_group(totals, pieces):
        inputs, grads_out, segments, codes, keeps = pieces

        def run_layer(values, weights):
            return forward(values, weights, segments, codes, keeps)
        result, pullback = jax.vjp(run_layer, inputs, params)
        input_part, weight_grads = pullback(grads_out)
        totals = jax.tree.map(jnp.add, totals, weight_grads)
        return (totals, (result.astype(jnp.bfloat16), input_part))
    totals, (outputs, input_grads) = lax.scan(one_group, zeros, (regroup(tokens.astype(jnp.float32)), regroup(cotangent.astype(jnp.float32)), regroup(token_segment), regroup(key_code), regroup(kept_rows)))
    return (outputs.reshape(CLIPS, LENGTH, D), input_grads.reshape(CLIPS, LENGTH, D), totals[0], totals[1], totals[2], totals[3], totals[4], totals[5], totals[6], totals[7], totals[8], totals[9], totals[10], totals[11], totals[12])
```

```python
import jax
import jax.numpy as jnp
from jax import lax
from jax.sharding import PartitionSpec as P

HEADS = 12
EPSILON = 1e-06
AXES = ("frame", "clip")


class Grid:
    def __init__(self, frames, clips):
        self.frames = frames
        self.clips = clips
        self.sizes = {"x": frames // 2, "core": 2, "z": clips // 2, "y": 2}

    def here(self):
        frame = lax.axis_index("frame")
        clip = lax.axis_index("clip")
        return {"x": frame // 2, "core": frame % 2, "z": clip // 2, "y": clip % 2}

    def swap(self, value, **flips):
        pairs = []
        for index in range(self.frames * self.clips):
            frame, clip = divmod(index, self.clips)
            at = {"x": frame // 2, "core": frame % 2, "z": clip // 2, "y": clip % 2}
            for name, bits in flips.items():
                at[name] ^= bits
            other = (at["x"] * 2 + at["core"]) * self.clips + at["z"] * 2 + at["y"]
            pairs.append((index, other))
        return lax.ppermute(value, AXES, pairs)


def put(buffer, piece, axis, index):
    return lax.dynamic_update_index_in_dim(buffer, piece, index, axis)


def pick(value, axis, index):
    return lax.dynamic_index_in_dim(value, index, axis, keepdims=False)


def gather_axis(grid, here, value, name, axis):
    count = grid.sizes[name]
    parts = [value] + [grid.swap(value, **{name: bits}) for bits in range(1, count)]
    shape = value.shape[:axis] + (count,) + value.shape[axis:]
    buffer = jnp.zeros(shape, value.dtype)
    for bits, part in enumerate(parts):
        buffer = put(buffer, part, axis, here[name] ^ bits)
    return buffer


def gather_weight(grid, here, shard, order):
    have = []
    value = shard
    for name in order:
        axis = sum(1 for done in have if "x core z y".split().index(done) < "x core z y".split().index(name))
        value = gather_axis(grid, here, value, name, axis)
        have.append(name)
    return value.reshape((-1,) + shard.shape[1:])


def scatter_weight(grid, here, grad, order, keep=jnp.bfloat16):
    sizes = grid.sizes
    rows = grad.shape[0] // (grid.frames * grid.clips)
    value = grad.reshape((sizes["x"], sizes["core"], sizes["z"], sizes["y"], rows) + grad.shape[1:])
    left = ["x", "core", "z", "y"]
    for step, name in enumerate(order):
        axis = left.index(name)
        total = pick(value, axis, here[name]).astype(jnp.float32)
        for bits in range(1, sizes[name]):
            sent = pick(value, axis, here[name] ^ bits)
            total = total + grid.swap(sent, **{name: bits}).astype(jnp.float32)
        left.remove(name)
        value = total if step == len(order) - 1 else total.astype(keep)
    return value


def to_slots(grid, here, value):
    own = value.shape[0] // grid.frames
    frame = here["x"] * 2 + here["core"]
    pieces = []
    for bits in range(grid.frames):
        piece = lax.dynamic_slice_in_dim(value, (frame ^ bits) * own, own, 0)
        if bits:
            piece = grid.swap(piece, x=bits // 2, core=bits % 2)
        pieces.append(piece)
    return jnp.concatenate(pieces, axis=1)


def from_slots(grid, here, value):
    frames = grid.frames
    own, length = value.shape[:2]
    width = length // frames
    frame = here["x"] * 2 + here["core"]
    buffer = jnp.zeros((own * frames, width) + value.shape[2:], value.dtype)
    for bits in range(frames):
        piece = value[:, bits * width : (bits + 1) * width]
        if bits:
            piece = grid.swap(piece, x=bits // 2, core=bits % 2)
        buffer = lax.dynamic_update_slice_in_dim(buffer, piece, (frame ^ bits) * own, 0)
    return buffer


def layer_norm(values, gain, shift):
    center = values - jnp.mean(values, axis=-1, keepdims=True)
    spread = jnp.mean(center * center, axis=-1, keepdims=True)
    return center * lax.rsqrt(spread + EPSILON) * gain + shift


def gelu_exact(values):
    return jax.nn.gelu(values, approximate=False)


def raw_scores(query_rows, key_rows, segment_rows, code_rows):
    slot_count, length, model_width = query_rows.shape
    key_length = key_rows.shape[1]
    head_dim = model_width // HEADS
    query_heads = query_rows.reshape(slot_count, length, HEADS, head_dim)
    key_heads = key_rows.reshape(slot_count, key_length, HEADS, head_dim)
    scores = jnp.einsum(
        "sqhd,skhd->shqk", query_heads, key_heads, preferred_element_type=jnp.float32
    ) * head_dim ** (-0.5)
    allowed = segment_rows[:, None, :, None] == code_rows[:, None, None, :]
    return (scores, allowed)


def layer_step(full, token_rows, cotangent_rows, segment_rows, code_rows, kept_mask):
    (
        attn_gain,
        attn_shift,
        w_qkv,
        query_bias,
        value_bias,
        w_out,
        out_bias,
        mlp_gain,
        mlp_shift,
        w_up,
        up_bias,
        w_down,
        down_bias,
    ) = full
    attn_gain = attn_gain.astype(jnp.float32)
    attn_shift = attn_shift.astype(jnp.float32)
    mlp_gain = mlp_gain.astype(jnp.float32)
    mlp_shift = mlp_shift.astype(jnp.float32)
    slot_count, length, model_width = token_rows.shape
    row_count = slot_count * length
    head_dim = model_width // HEADS
    block_shape = (slot_count, length, model_width)
    inputs = token_rows.reshape(row_count, model_width).astype(jnp.float32)
    first_low = layer_norm(inputs, attn_gain, attn_shift).astype(jnp.bfloat16)
    projected = jnp.dot(first_low, w_qkv, preferred_element_type=jnp.float32)
    query_rows = (
        (projected[:, :model_width] + query_bias.astype(jnp.float32))
        .astype(jnp.bfloat16)
        .reshape(block_shape)
    )
    key_rows = projected[:, model_width : 2 * model_width].astype(jnp.bfloat16).reshape(block_shape)
    value_rows = (
        (projected[:, 2 * model_width :] + value_bias.astype(jnp.float32))
        .astype(jnp.bfloat16)
        .reshape(block_shape)
    )
    key_all, value_all, code_all = (key_rows, value_rows, code_rows)
    key_length = key_all.shape[1]
    scores, allowed = raw_scores(query_rows, key_all, segment_rows, code_all)
    masked = jnp.where(allowed, scores, -1e30)
    row_max = jnp.max(masked, axis=-1, keepdims=True)
    weights = jnp.where(allowed, jnp.exp(masked - row_max), 0.0)
    total = jnp.sum(weights, axis=-1, keepdims=True)
    log_total = row_max + jnp.log(total)
    probability = (weights / total).astype(jnp.bfloat16)
    value_heads = value_all.reshape(slot_count, key_length, HEADS, head_dim)
    attended = jnp.einsum(
        "shqk,skhd->sqhd", probability, value_heads, preferred_element_type=jnp.float32
    )
    attended_low = attended.reshape(row_count, model_width).astype(jnp.bfloat16)
    branch = jnp.dot(attended_low, w_out, preferred_element_type=jnp.float32) + out_bias.astype(
        jnp.float32
    )
    middle = inputs + branch
    second_low = layer_norm(middle, mlp_gain, mlp_shift).astype(jnp.bfloat16)
    hidden = jnp.dot(second_low, w_up, preferred_element_type=jnp.float32) + up_bias.astype(
        jnp.float32
    )
    active_low = gelu_exact(hidden).astype(jnp.bfloat16)
    result = jnp.dot(active_low, w_down, preferred_element_type=jnp.float32) + down_bias.astype(
        jnp.float32
    )
    kept_column = kept_mask.reshape(row_count, 1)
    output_rows = (kept_column * (middle + result)).astype(jnp.bfloat16).reshape(block_shape)
    grad_result = kept_column * cotangent_rows.reshape(row_count, model_width).astype(jnp.float32)
    grad_low = grad_result.astype(jnp.bfloat16)
    grad_w_down = jnp.einsum("nf,nd->fd", active_low, grad_low, preferred_element_type=jnp.float32)
    grad_down_bias = jnp.sum(grad_low.astype(jnp.float32), axis=0)
    grad_active = jnp.einsum("nd,fd->nf", grad_low, w_down, preferred_element_type=jnp.float32)
    _, gelu_pull = jax.vjp(gelu_exact, hidden)
    grad_hidden = gelu_pull(grad_active)[0].astype(jnp.bfloat16)
    grad_w_up = jnp.einsum("nd,nf->df", second_low, grad_hidden, preferred_element_type=jnp.float32)
    grad_up_bias = jnp.sum(grad_hidden.astype(jnp.float32), axis=0)
    grad_second = jnp.einsum("nf,df->nd", grad_hidden, w_up, preferred_element_type=jnp.float32)
    _, second_pull = jax.vjp(layer_norm, middle, mlp_gain, mlp_shift)
    grad_mid_norm, grad_mlp_gain, grad_mlp_shift = second_pull(grad_second)
    grad_middle = grad_result + grad_mid_norm
    branch_low = grad_middle.astype(jnp.bfloat16)
    grad_w_out = jnp.einsum(
        "nd,ne->de", attended_low, branch_low, preferred_element_type=jnp.float32
    )
    grad_out_bias = jnp.sum(branch_low.astype(jnp.float32), axis=0)
    grad_attended = jnp.einsum(
        "ne,de->nd", branch_low, w_out, preferred_element_type=jnp.float32
    ).astype(jnp.bfloat16)
    key_back, value_back, code_back = (key_rows, value_rows, code_rows)
    scores, allowed = raw_scores(query_rows, key_back, segment_rows, code_back)
    value_heads = value_back.reshape(slot_count, key_length, HEADS, head_dim)
    key_heads = key_back.reshape(slot_count, key_length, HEADS, head_dim)
    scale = head_dim ** (-0.5)
    prob_back = jnp.where(allowed, jnp.exp(scores - log_total), 0.0)
    grad_heads = grad_attended.reshape(slot_count, length, HEADS, head_dim)
    query_heads = query_rows.reshape(slot_count, length, HEADS, head_dim)
    grad_prob = jnp.einsum(
        "sqhd,skhd->shqk", grad_heads, value_heads, preferred_element_type=jnp.float32
    )
    row_delta = jnp.sum(prob_back * grad_prob, axis=-1, keepdims=True)
    grad_scores = (prob_back * (grad_prob - row_delta)).astype(jnp.bfloat16)
    grad_query = (
        (
            jnp.einsum(
                "shqk,skhd->sqhd", grad_scores, key_heads, preferred_element_type=jnp.float32
            )
            * scale
        )
        .reshape(row_count, model_width)
        .astype(jnp.bfloat16)
    )
    grad_key_all = (
        jnp.einsum("shqk,sqhd->skhd", grad_scores, query_heads, preferred_element_type=jnp.float32)
        * scale
    ).reshape(slot_count, key_length, model_width)
    grad_value_all = jnp.einsum(
        "shqk,sqhd->skhd",
        prob_back.astype(jnp.bfloat16),
        grad_heads,
        preferred_element_type=jnp.float32,
    ).reshape(slot_count, key_length, model_width)
    grad_key, grad_value = (grad_key_all, grad_value_all)
    grad_key_low = grad_key.reshape(row_count, model_width).astype(jnp.bfloat16)
    grad_value_low = grad_value.reshape(row_count, model_width).astype(jnp.bfloat16)
    grad_mixed = jnp.concatenate([grad_query, grad_key_low, grad_value_low], axis=1)
    grad_w_qkv = jnp.einsum("nd,ne->de", first_low, grad_mixed, preferred_element_type=jnp.float32)
    grad_query_bias = jnp.sum(grad_query.astype(jnp.float32), axis=0)
    grad_value_bias = jnp.sum(grad_value_low.astype(jnp.float32), axis=0)
    grad_first = jnp.einsum("ne,de->nd", grad_mixed, w_qkv, preferred_element_type=jnp.float32)
    _, first_pull = jax.vjp(layer_norm, inputs, attn_gain, attn_shift)
    grad_in_norm, grad_attn_gain, grad_attn_shift = first_pull(grad_first)
    input_rows = (grad_middle + grad_in_norm).reshape(block_shape)
    grads = (
        grad_attn_gain,
        grad_attn_shift,
        grad_w_qkv,
        grad_query_bias,
        grad_value_bias,
        grad_w_out,
        grad_out_bias,
        grad_mlp_gain,
        grad_mlp_shift,
        grad_w_up,
        grad_up_bias,
        grad_w_down,
        grad_down_bias,
    )
    return (output_rows, input_rows, grads)


def body(
    grid,
    tokens,
    cotangent,
    frame_count,
    image_group,
    keep_mask,
    attn_norm_gain,
    attn_norm_bias,
    w_qkv,
    query_bias,
    value_bias,
    w_out,
    out_bias,
    mlp_norm_gain,
    mlp_norm_bias,
    w_up,
    up_bias,
    w_down,
    down_bias,
):
    here = grid.here()
    frames_here = image_group.shape[1]
    block_width = keep_mask.shape[1] // frames_here
    frame_index = lax.axis_index("frame") * frames_here + jnp.arange(frames_here, dtype=jnp.int32)
    segment = jnp.where(frame_index[None, :] < frame_count[:, None], 0, 1 + image_group)
    token_segment = jnp.repeat(segment, block_width, axis=1)
    tags = to_slots(grid, here, token_segment * 2 + keep_mask)
    token_segment = tags // 2
    keep_slots = tags % 2
    key_code = jnp.where(keep_slots == 1, token_segment, -1)
    kept_rows = keep_slots.astype(jnp.float32)

    rows = w_out.shape[0]
    ratio = up_bias.shape[0] // rows
    small = jnp.stack(
        [attn_norm_gain, attn_norm_bias, query_bias, value_bias, out_bias, mlp_norm_gain, mlp_norm_bias, down_bias],
        axis=1,
    )
    small = jnp.concatenate([small, up_bias.reshape(rows, ratio)], axis=1)
    small = jnp.pad(small, ((0, 0), (0, 128 - small.shape[1])))
    token_rows = to_slots(grid, here, tokens)

    def gathered(shard):
        width = shard.shape[1]
        half = (width // 256) * 128
        left = gather_weight(grid, here, shard[:, :half], ("z", "x", "y", "core"))
        right = gather_weight(grid, here, shard[:, half:], ("z", "y", "x", "core"))
        return jnp.concatenate([left, right], axis=1)

    mixed = gathered(jnp.concatenate([w_qkv, small], axis=1))
    qkv_full = mixed[:, : w_qkv.shape[1]]
    small_full = mixed[:, w_qkv.shape[1] :]
    vectors = [small_full[:, i] for i in range(8)]
    up_bias_full = small_full[:, 8 : 8 + ratio].reshape(-1)
    out_full = gathered(w_out)
    up_full = gathered(w_up)
    cotangent_rows = to_slots(grid, here, cotangent)
    down_full = gathered(w_down)
    full = (
        vectors[0], vectors[1], qkv_full, vectors[2], vectors[3], out_full, vectors[4],
        vectors[5], vectors[6], up_full, up_bias_full, down_full, vectors[7],
    )
    output_rows, input_rows, grads = layer_step(
        full, token_rows, cotangent_rows, token_segment, key_code, kept_rows
    )
    output = from_slots(grid, here, output_rows)
    input_grad = from_slots(grid, here, input_rows.astype(jnp.bfloat16)).astype(jnp.float32)

    def scattered(grad):
        low = grad.astype(jnp.bfloat16)
        half = (grad.shape[1] // 256) * 128
        left = scatter_weight(grid, here, low[:, :half], ("core", "x", "y", "z"))
        right = scatter_weight(grid, here, low[:, half:], ("core", "y", "x", "z"))
        return jnp.concatenate([left, right], axis=1)

    g_down = scattered(grads[11])
    g_up = scattered(grads[9])
    g_out = scattered(grads[5])
    g_qkv = scattered(grads[2])
    devices = grid.frames * grid.clips
    order = (0, 1, 3, 4, 6, 7, 8, 12)
    pack = jnp.concatenate(
        [grads[i].reshape(devices, rows) for i in order] + [grads[10].reshape(devices, rows * ratio)], axis=1
    )
    pack = scatter_weight(grid, here, pack, ("core", "x", "y", "z"), jnp.float32)[0]
    v = {g: pack[i * rows : (i + 1) * rows] for i, g in enumerate(order)}
    return (
        output, input_grad, v[0], v[1], g_qkv, v[3], v[4], g_out, v[6], v[7], v[8],
        g_up, pack[8 * rows :], g_down, v[12],
    )


def solution(mesh):
    grid = Grid(mesh.shape["frame"], mesh.shape["clip"])

    def run(*arguments):
        return body(grid, *arguments)

    placed = (
        P("clip", "frame", None),
        P("clip", "frame", None),
        P("clip"),
        P("clip", "frame"),
        P("clip", "frame"),
        P(("frame", "clip")),
        P(("frame", "clip")),
        P(("frame", "clip"), None),
        P(("frame", "clip")),
        P(("frame", "clip")),
        P(("frame", "clip"), None),
        P(("frame", "clip")),
        P(("frame", "clip")),
        P(("frame", "clip")),
        P(("frame", "clip"), None),
        P(("frame", "clip")),
        P(("frame", "clip"), None),
        P(("frame", "clip")),
    )
    return jax.shard_map(
        run,
        mesh=mesh,
        in_specs=placed,
        out_specs=(
            P("clip", "frame", None),
            P("clip", "frame", None),
            P(("frame", "clip")),
            P(("frame", "clip")),
            P(("frame", "clip"), None),
            P(("frame", "clip")),
            P(("frame", "clip")),
            P(("frame", "clip"), None),
            P(("frame", "clip")),
            P(("frame", "clip")),
            P(("frame", "clip")),
            P(("frame", "clip"), None),
            P(("frame", "clip")),
            P(("frame", "clip"), None),
            P(("frame", "clip")),
        ),
        check_vma=False,
    )
```

```python
import jax
import jax.numpy as jnp
from jax import lax
from jax.sharding import PartitionSpec as P

HEADS = 12
EPSILON = 1e-06
AXES = ("frame", "clip")


class Grid:
    def __init__(self, frames, clips):
        self.frames = frames
        self.clips = clips
        self.sizes = {"x": frames // 2, "core": 2, "z": clips // 2, "y": 2}

    def here(self):
        frame = lax.axis_index("frame")
        clip = lax.axis_index("clip")
        return {"x": frame // 2, "core": frame % 2, "z": clip // 2, "y": clip % 2}

    def swap(self, value, **flips):
        pairs = []
        for index in range(self.frames * self.clips):
            frame, clip = divmod(index, self.clips)
            at = {"x": frame // 2, "core": frame % 2, "z": clip // 2, "y": clip % 2}
            for name, bits in flips.items():
                at[name] ^= bits
            other = (at["x"] * 2 + at["core"]) * self.clips + at["z"] * 2 + at["y"]
            pairs.append((index, other))
        return lax.ppermute(value, AXES, pairs)


def put(buffer, piece, axis, index):
    return lax.dynamic_update_index_in_dim(buffer, piece, index, axis)


def pick(value, axis, index):
    return lax.dynamic_index_in_dim(value, index, axis, keepdims=False)


def mixed_swap(grid, value, first):
    pairs = []
    for index in range(grid.frames * grid.clips):
        frame, clip = divmod(index, grid.clips)
        if frame % 2 == first:
            frame ^= 2
        else:
            clip ^= 1
        pairs.append((index, frame * grid.clips + clip))
    return lax.ppermute(value, AXES, pairs)


def cell(here, core, near, far):
    x = jnp.where(core == 0, here["x"] ^ near, here["x"] ^ far)
    y = jnp.where(core == 0, here["y"] ^ far, here["y"] ^ near)
    return x, y


def gather_group(grid, here, shard):
    count = grid.sizes["z"]
    rows, width = shard.shape
    column = jnp.zeros((count, rows, width), shard.dtype)
    for bits in range(count):
        part = grid.swap(shard, z=bits) if bits else shard
        column = put(column, part, 0, here["z"] ^ bits)
    pair = jnp.stack([column, mixed_swap(grid, column, 0)])
    other = mixed_swap(grid, pair, 1)
    halves = ((pair, other), (grid.swap(pair, core=1), grid.swap(other, core=1)))
    full = jnp.zeros((grid.sizes["x"], 2, count, 2, rows, width), shard.dtype)
    for side in range(2):
        core = here["core"] ^ side
        for far in range(2):
            for near in range(2):
                x, y = cell(here, core, near, far)
                piece = halves[side][far][near][None, None, :, None]
                full = lax.dynamic_update_slice(full, piece, (x, core, 0, y, 0, 0))
    return full.reshape(-1, width)


def scatter_group(grid, here, grad):
    sizes = grid.sizes
    count = sizes["z"]
    width = grad.shape[1]
    rows = grad.shape[0] // (grid.frames * grid.clips)
    core = here["core"]
    value = grad.reshape((sizes["x"], 2, count, 2, rows, width))
    value = pick(value, 1, core).astype(jnp.float32) + grid.swap(pick(value, 1, 1 - core), core=1).astype(jnp.float32)
    value = value.astype(jnp.bfloat16)

    def piece(near, far):
        x = jnp.where(core == 0, here["x"] ^ near, far)
        y = jnp.where(core == 0, far, here["y"] ^ near)
        return lax.dynamic_slice(value, (x, 0, y, 0, 0), (1, count, 1, rows, width))[0, :, 0]

    sent = jnp.stack([piece(1, 0), piece(1, 1)])
    kept = jnp.stack([piece(0, 0), piece(0, 1)])
    value = (kept.astype(jnp.float32) + mixed_swap(grid, sent, 0).astype(jnp.float32)).astype(jnp.bfloat16)
    own = jnp.where(core == 0, here["y"], here["x"])
    value = pick(value, 0, own).astype(jnp.float32) + mixed_swap(grid, pick(value, 0, 1 - own), 1).astype(jnp.float32)
    value = value.astype(jnp.bfloat16)
    total = pick(value, 0, here["z"]).astype(jnp.float32)
    for bits in range(1, count):
        total = total + grid.swap(pick(value, 0, here["z"] ^ bits), z=bits).astype(jnp.float32)
    return total


def to_slots(grid, here, value):
    own = value.shape[0] // grid.frames
    frame = here["x"] * 2 + here["core"]
    pieces = []
    for bits in range(grid.frames):
        piece = lax.dynamic_slice_in_dim(value, (frame ^ bits) * own, own, 0)
        if bits:
            piece = grid.swap(piece, x=bits // 2, core=bits % 2)
        pieces.append(piece)
    return jnp.concatenate(pieces, axis=1)


def from_slots(grid, here, value):
    frames = grid.frames
    own, length = value.shape[:2]
    width = length // frames
    frame = here["x"] * 2 + here["core"]
    buffer = jnp.zeros((own * frames, width) + value.shape[2:], value.dtype)
    for bits in range(frames):
        piece = value[:, bits * width : (bits + 1) * width]
        if bits:
            piece = grid.swap(piece, x=bits // 2, core=bits % 2)
        buffer = lax.dynamic_update_slice_in_dim(buffer, piece, (frame ^ bits) * own, 0)
    return buffer


def layer_norm(values, gain, shift):
    center = values - jnp.mean(values, axis=-1, keepdims=True)
    spread = jnp.mean(center * center, axis=-1, keepdims=True)
    return center * lax.rsqrt(spread + EPSILON) * gain + shift


def gelu_exact(values):
    return jax.nn.gelu(values, approximate=False)


def raw_scores(query_rows, key_rows, segment_rows, code_rows):
    slot_count, length, model_width = query_rows.shape
    key_length = key_rows.shape[1]
    head_dim = model_width // HEADS
    query_heads = query_rows.reshape(slot_count, length, HEADS, head_dim)
    key_heads = key_rows.reshape(slot_count, key_length, HEADS, head_dim)
    scores = jnp.einsum(
        "sqhd,skhd->shqk", query_heads, key_heads, preferred_element_type=jnp.float32
    ) * head_dim ** (-0.5)
    allowed = segment_rows[:, None, :, None] == code_rows[:, None, None, :]
    return (scores, allowed)


def layer_step(full, token_rows, cotangent_rows, segment_rows, code_rows, kept_mask):
    (
        attn_gain,
        attn_shift,
        w_qkv,
        query_bias,
        value_bias,
        w_out,
        out_bias,
        mlp_gain,
        mlp_shift,
        w_up,
        up_bias,
        w_down,
        down_bias,
    ) = full
    attn_gain = attn_gain.astype(jnp.float32)
    attn_shift = attn_shift.astype(jnp.float32)
    mlp_gain = mlp_gain.astype(jnp.float32)
    mlp_shift = mlp_shift.astype(jnp.float32)
    slot_count, length, model_width = token_rows.shape
    row_count = slot_count * length
    head_dim = model_width // HEADS
    block_shape = (slot_count, length, model_width)
    inputs = token_rows.reshape(row_count, model_width).astype(jnp.float32)
    first_low = layer_norm(inputs, attn_gain, attn_shift).astype(jnp.bfloat16)
    projected = jnp.dot(first_low, w_qkv, preferred_element_type=jnp.float32)
    query_rows = (
        (projected[:, :model_width] + query_bias.astype(jnp.float32))
        .astype(jnp.bfloat16)
        .reshape(block_shape)
    )
    key_rows = projected[:, model_width : 2 * model_width].astype(jnp.bfloat16).reshape(block_shape)
    value_rows = (
        (projected[:, 2 * model_width :] + value_bias.astype(jnp.float32))
        .astype(jnp.bfloat16)
        .reshape(block_shape)
    )
    key_all, value_all, code_all = (key_rows, value_rows, code_rows)
    key_length = key_all.shape[1]
    scores, allowed = raw_scores(query_rows, key_all, segment_rows, code_all)
    masked = jnp.where(allowed, scores, -1e30)
    row_max = jnp.max(masked, axis=-1, keepdims=True)
    weights = jnp.where(allowed, jnp.exp(masked - row_max), 0.0)
    total = jnp.sum(weights, axis=-1, keepdims=True)
    log_total = row_max + jnp.log(total)
    probability = (weights / total).astype(jnp.bfloat16)
    value_heads = value_all.reshape(slot_count, key_length, HEADS, head_dim)
    attended = jnp.einsum(
        "shqk,skhd->sqhd", probability, value_heads, preferred_element_type=jnp.float32
    )
    attended_low = attended.reshape(row_count, model_width).astype(jnp.bfloat16)
    branch = jnp.dot(attended_low, w_out, preferred_element_type=jnp.float32) + out_bias.astype(
        jnp.float32
    )
    middle = inputs + branch
    second_low = layer_norm(middle, mlp_gain, mlp_shift).astype(jnp.bfloat16)
    hidden = jnp.dot(second_low, w_up, preferred_element_type=jnp.float32) + up_bias.astype(
        jnp.float32
    )
    active_low = gelu_exact(hidden).astype(jnp.bfloat16)
    result = jnp.dot(active_low, w_down, preferred_element_type=jnp.float32) + down_bias.astype(
        jnp.float32
    )
    kept_column = kept_mask.reshape(row_count, 1)
    output_rows = (kept_column * (middle + result)).astype(jnp.bfloat16).reshape(block_shape)
    grad_result = kept_column * cotangent_rows.reshape(row_count, model_width).astype(jnp.float32)
    grad_low = grad_result.astype(jnp.bfloat16)
    grad_w_down = jnp.einsum("nf,nd->fd", active_low, grad_low, preferred_element_type=jnp.float32)
    grad_down_bias = jnp.sum(grad_low.astype(jnp.float32), axis=0)
    grad_active = jnp.einsum("nd,fd->nf", grad_low, w_down, preferred_element_type=jnp.float32)
    _, gelu_pull = jax.vjp(gelu_exact, hidden)
    grad_hidden = gelu_pull(grad_active)[0].astype(jnp.bfloat16)
    grad_w_up = jnp.einsum("nd,nf->df", second_low, grad_hidden, preferred_element_type=jnp.float32)
    grad_up_bias = jnp.sum(grad_hidden.astype(jnp.float32), axis=0)
    grad_second = jnp.einsum("nf,df->nd", grad_hidden, w_up, preferred_element_type=jnp.float32)
    _, second_pull = jax.vjp(layer_norm, middle, mlp_gain, mlp_shift)
    grad_mid_norm, grad_mlp_gain, grad_mlp_shift = second_pull(grad_second)
    grad_middle = grad_result + grad_mid_norm
    branch_low = grad_middle.astype(jnp.bfloat16)
    grad_w_out = jnp.einsum(
        "nd,ne->de", attended_low, branch_low, preferred_element_type=jnp.float32
    )
    grad_out_bias = jnp.sum(branch_low.astype(jnp.float32), axis=0)
    grad_attended = jnp.einsum(
        "ne,de->nd", branch_low, w_out, preferred_element_type=jnp.float32
    ).astype(jnp.bfloat16)
    key_back, value_back, code_back = (key_rows, value_rows, code_rows)
    scores, allowed = raw_scores(query_rows, key_back, segment_rows, code_back)
    value_heads = value_back.reshape(slot_count, key_length, HEADS, head_dim)
    key_heads = key_back.reshape(slot_count, key_length, HEADS, head_dim)
    scale = head_dim ** (-0.5)
    prob_back = jnp.where(allowed, jnp.exp(scores - log_total), 0.0)
    grad_heads = grad_attended.reshape(slot_count, length, HEADS, head_dim)
    query_heads = query_rows.reshape(slot_count, length, HEADS, head_dim)
    grad_prob = jnp.einsum(
        "sqhd,skhd->shqk", grad_heads, value_heads, preferred_element_type=jnp.float32
    )
    row_delta = jnp.sum(prob_back * grad_prob, axis=-1, keepdims=True)
    grad_scores = (prob_back * (grad_prob - row_delta)).astype(jnp.bfloat16)
    grad_query = (
        (
            jnp.einsum(
                "shqk,skhd->sqhd", grad_scores, key_heads, preferred_element_type=jnp.float32
            )
            * scale
        )
        .reshape(row_count, model_width)
        .astype(jnp.bfloat16)
    )
    grad_key_all = (
        jnp.einsum("shqk,sqhd->skhd", grad_scores, query_heads, preferred_element_type=jnp.float32)
        * scale
    ).reshape(slot_count, key_length, model_width)
    grad_value_all = jnp.einsum(
        "shqk,sqhd->skhd",
        prob_back.astype(jnp.bfloat16),
        grad_heads,
        preferred_element_type=jnp.float32,
    ).reshape(slot_count, key_length, model_width)
    grad_key, grad_value = (grad_key_all, grad_value_all)
    grad_key_low = grad_key.reshape(row_count, model_width).astype(jnp.bfloat16)
    grad_value_low = grad_value.reshape(row_count, model_width).astype(jnp.bfloat16)
    grad_mixed = jnp.concatenate([grad_query, grad_key_low, grad_value_low], axis=1)
    grad_w_qkv = jnp.einsum("nd,ne->de", first_low, grad_mixed, preferred_element_type=jnp.float32)
    grad_query_bias = jnp.sum(grad_query.astype(jnp.float32), axis=0)
    grad_value_bias = jnp.sum(grad_value_low.astype(jnp.float32), axis=0)
    grad_first = jnp.einsum("ne,de->nd", grad_mixed, w_qkv, preferred_element_type=jnp.float32)
    _, first_pull = jax.vjp(layer_norm, inputs, attn_gain, attn_shift)
    grad_in_norm, grad_attn_gain, grad_attn_shift = first_pull(grad_first)
    input_rows = (grad_middle + grad_in_norm).reshape(block_shape)
    grads = (
        grad_attn_gain,
        grad_attn_shift,
        grad_w_qkv,
        grad_query_bias,
        grad_value_bias,
        grad_w_out,
        grad_out_bias,
        grad_mlp_gain,
        grad_mlp_shift,
        grad_w_up,
        grad_up_bias,
        grad_w_down,
        grad_down_bias,
    )
    return (output_rows, input_rows, grads)


def body(
    grid,
    tokens,
    cotangent,
    frame_count,
    image_group,
    keep_mask,
    attn_norm_gain,
    attn_norm_bias,
    w_qkv,
    query_bias,
    value_bias,
    w_out,
    out_bias,
    mlp_norm_gain,
    mlp_norm_bias,
    w_up,
    up_bias,
    w_down,
    down_bias,
):
    here = grid.here()
    frames_here = image_group.shape[1]
    block_width = keep_mask.shape[1] // frames_here
    frame_index = lax.axis_index("frame") * frames_here + jnp.arange(frames_here, dtype=jnp.int32)
    segment = jnp.where(frame_index[None, :] < frame_count[:, None], 0, 1 + image_group)
    token_segment = jnp.repeat(segment, block_width, axis=1)
    tags = to_slots(grid, here, token_segment * 2 + keep_mask)
    token_segment = tags // 2
    keep_slots = tags % 2
    key_code = jnp.where(keep_slots == 1, token_segment, -1)
    kept_rows = keep_slots.astype(jnp.float32)

    rows = w_out.shape[0]
    ratio = up_bias.shape[0] // rows
    small = jnp.stack(
        [attn_norm_gain, attn_norm_bias, query_bias, value_bias, out_bias, mlp_norm_gain, mlp_norm_bias, down_bias],
        axis=1,
    )
    small = jnp.concatenate([small, up_bias.reshape(rows, ratio)], axis=1)
    small = jnp.pad(small, ((0, 0), (0, 128 - small.shape[1])))
    token_rows = to_slots(grid, here, tokens)

    mixed = gather_group(grid, here, jnp.concatenate([w_qkv, small], axis=1))
    down_rows = w_down.reshape(ratio, rows, w_down.shape[1])
    rest = gather_group(
        grid, here, jnp.concatenate([w_out, w_up] + [down_rows[i] for i in range(ratio)], axis=1)
    )
    qkv_full = mixed[:, : w_qkv.shape[1]]
    small_full = mixed[:, w_qkv.shape[1] :]
    vectors = [small_full[:, i] for i in range(8)]
    up_bias_full = small_full[:, 8 : 8 + ratio].reshape(-1)
    model, hidden = w_out.shape[1], w_up.shape[1]
    devices = grid.frames * grid.clips
    out_full = rest[:, :model]
    up_full = rest[:, model : model + hidden]
    down_full = (
        rest[:, model + hidden :].reshape(devices, rows, ratio, model).transpose(0, 2, 1, 3).reshape(-1, model)
    )
    cotangent_rows = to_slots(grid, here, cotangent)
    full = (
        vectors[0], vectors[1], qkv_full, vectors[2], vectors[3], out_full, vectors[4],
        vectors[5], vectors[6], up_full, up_bias_full, down_full, vectors[7],
    )
    output_rows, input_rows, grads = layer_step(
        full, token_rows, cotangent_rows, token_segment, key_code, kept_rows
    )
    output = from_slots(grid, here, output_rows)
    input_grad = from_slots(grid, here, input_rows.astype(jnp.bfloat16)).astype(jnp.float32)

    def low(grad):
        return grad.astype(jnp.bfloat16)

    g_down = scatter_group(
        grid,
        here,
        low(grads[11]).reshape(devices, ratio, rows, model).transpose(0, 2, 1, 3).reshape(devices * rows, ratio * model),
    )
    g_down = g_down.reshape(rows, ratio, model).transpose(1, 0, 2).reshape(ratio * rows, model)
    g_up = scatter_group(grid, here, low(grads[9]))
    g_qkv = scatter_group(grid, here, low(grads[2]))
    order = (0, 1, 3, 4, 6, 7, 8, 12)
    pack = jnp.concatenate([jnp.stack([grads[i] for i in order], axis=1), grads[10].reshape(-1, ratio)], axis=1)
    pack = jnp.pad(low(pack), ((0, 0), (0, 128 - pack.shape[1])))
    last = scatter_group(grid, here, jnp.concatenate([low(grads[5]), pack], axis=1))
    g_out = last[:, :model]
    v = {g: last[:, model + i] for i, g in enumerate(order)}
    g_up_bias = last[:, model + 8 : model + 8 + ratio].reshape(-1)
    return (
        output, input_grad, v[0], v[1], g_qkv, v[3], v[4], g_out, v[6], v[7], v[8],
        g_up, g_up_bias, g_down, v[12],
    )


def solution(mesh):
    grid = Grid(mesh.shape["frame"], mesh.shape["clip"])

    def run(*arguments):
        return body(grid, *arguments)

    placed = (
        P("clip", "frame", None),
        P("clip", "frame", None),
        P("clip"),
        P("clip", "frame"),
        P("clip", "frame"),
        P(("frame", "clip")),
        P(("frame", "clip")),
        P(("frame", "clip"), None),
        P(("frame", "clip")),
        P(("frame", "clip")),
        P(("frame", "clip"), None),
        P(("frame", "clip")),
        P(("frame", "clip")),
        P(("frame", "clip")),
        P(("frame", "clip"), None),
        P(("frame", "clip")),
        P(("frame", "clip"), None),
        P(("frame", "clip")),
    )
    return jax.shard_map(
        run,
        mesh=mesh,
        in_specs=placed,
        out_specs=(
            P("clip", "frame", None),
            P("clip", "frame", None),
            P(("frame", "clip")),
            P(("frame", "clip")),
            P(("frame", "clip"), None),
            P(("frame", "clip")),
            P(("frame", "clip")),
            P(("frame", "clip"), None),
            P(("frame", "clip")),
            P(("frame", "clip")),
            P(("frame", "clip")),
            P(("frame", "clip"), None),
            P(("frame", "clip")),
            P(("frame", "clip"), None),
            P(("frame", "clip")),
        ),
        check_vma=False,
    )
```

```python
import jax
import jax.numpy as jnp
from jax import lax
from jax.experimental import pallas as pl
from jax.experimental.pallas import tpu as pltpu
from jax.sharding import PartitionSpec as P

HEADS = 12
EPSILON = 1e-06
AXES = ("frame", "clip")


class Grid:
    def __init__(self, frames, clips):
        self.frames = frames
        self.clips = clips
        self.sizes = {"x": frames // 2, "core": 2, "z": clips // 2, "y": 2}

    def here(self):
        frame = lax.axis_index("frame")
        clip = lax.axis_index("clip")
        return {"x": frame // 2, "core": frame % 2, "z": clip // 2, "y": clip % 2}

    def swap(self, value, **flips):
        pairs = []
        for index in range(self.frames * self.clips):
            frame, clip = divmod(index, self.clips)
            at = {"x": frame // 2, "core": frame % 2, "z": clip // 2, "y": clip % 2}
            for name, bits in flips.items():
                at[name] ^= bits
            other = (at["x"] * 2 + at["core"]) * self.clips + at["z"] * 2 + at["y"]
            pairs.append((index, other))
        return lax.ppermute(value, AXES, pairs)


def put(buffer, piece, axis, index):
    return lax.dynamic_update_index_in_dim(buffer, piece, index, axis)


def pick(value, axis, index):
    return lax.dynamic_index_in_dim(value, index, axis, keepdims=False)


def mixed_swap(grid, value, first):
    pairs = []
    for index in range(grid.frames * grid.clips):
        frame, clip = divmod(index, grid.clips)
        if frame % 2 == first:
            frame ^= 2
        else:
            clip ^= 1
        pairs.append((index, frame * grid.clips + clip))
    return lax.ppermute(value, AXES, pairs)


def cell(here, core, near, far):
    x = jnp.where(core == 0, here["x"] ^ near, here["x"] ^ far)
    y = jnp.where(core == 0, here["y"] ^ far, here["y"] ^ near)
    return x, y


def gather_group(grid, here, shard):
    count = grid.sizes["z"]
    rows, width = shard.shape
    column = jnp.zeros((count, rows, width), shard.dtype)
    for bits in range(count):
        part = grid.swap(shard, z=bits) if bits else shard
        column = put(column, part, 0, here["z"] ^ bits)
    pair = jnp.stack([column, mixed_swap(grid, column, 0)])
    other = mixed_swap(grid, pair, 1)
    halves = ((pair, other), (grid.swap(pair, core=1), grid.swap(other, core=1)))
    full = jnp.zeros((grid.sizes["x"], 2, count, 2, rows, width), shard.dtype)
    for side in range(2):
        core = here["core"] ^ side
        for far in range(2):
            for near in range(2):
                x, y = cell(here, core, near, far)
                piece = halves[side][far][near][None, None, :, None]
                full = lax.dynamic_update_slice(full, piece, (x, core, 0, y, 0, 0))
    return full.reshape(-1, width)


def scatter_group(grid, here, grad):
    sizes = grid.sizes
    count = sizes["z"]
    width = grad.shape[1]
    rows = grad.shape[0] // (grid.frames * grid.clips)
    core = here["core"]
    value = grad.reshape((sizes["x"], 2, count, 2, rows, width))
    value = pick(value, 1, core).astype(jnp.float32) + grid.swap(pick(value, 1, 1 - core), core=1).astype(jnp.float32)
    value = value.astype(jnp.bfloat16)

    def piece(near, far):
        x = jnp.where(core == 0, here["x"] ^ near, far)
        y = jnp.where(core == 0, far, here["y"] ^ near)
        return lax.dynamic_slice(value, (x, 0, y, 0, 0), (1, count, 1, rows, width))[0, :, 0]

    sent = jnp.stack([piece(1, 0), piece(1, 1)])
    kept = jnp.stack([piece(0, 0), piece(0, 1)])
    value = (kept.astype(jnp.float32) + mixed_swap(grid, sent, 0).astype(jnp.float32)).astype(jnp.bfloat16)
    own = jnp.where(core == 0, here["y"], here["x"])
    value = pick(value, 0, own).astype(jnp.float32) + mixed_swap(grid, pick(value, 0, 1 - own), 1).astype(jnp.float32)
    value = value.astype(jnp.bfloat16)
    total = pick(value, 0, here["z"]).astype(jnp.float32)
    for bits in range(1, count):
        total = total + grid.swap(pick(value, 0, here["z"] ^ bits), z=bits).astype(jnp.float32)
    return total


def to_slots(grid, here, value):
    own = value.shape[0] // grid.frames
    frame = here["x"] * 2 + here["core"]
    pieces = []
    for bits in range(grid.frames):
        piece = lax.dynamic_slice_in_dim(value, (frame ^ bits) * own, own, 0)
        if bits:
            piece = grid.swap(piece, x=bits // 2, core=bits % 2)
        pieces.append(piece)
    return jnp.concatenate(pieces, axis=1)


def from_slots(grid, here, value):
    frames = grid.frames
    own, length = value.shape[:2]
    width = length // frames
    frame = here["x"] * 2 + here["core"]
    buffer = jnp.zeros((own * frames, width) + value.shape[2:], value.dtype)
    for bits in range(frames):
        piece = value[:, bits * width : (bits + 1) * width]
        if bits:
            piece = grid.swap(piece, x=bits // 2, core=bits % 2)
        buffer = lax.dynamic_update_slice_in_dim(buffer, piece, (frame ^ bits) * own, 0)
    return buffer


ROOT_HALF = 0.7071067811865476
DENSITY = 0.3989422804014327
NT = (((1,), (1,)), ((), ()))
NN = (((1,), (0,)), ((), ()))
TN = (((0,), (0,)), ((), ()))


def dot(left, right, dims=NN):
    return lax.dot_general(left, right, dims, preferred_element_type=jnp.float32)


def normalize(values):
    center = values - jnp.mean(values, axis=-1, keepdims=True)
    spread = jnp.mean(center * center, axis=-1, keepdims=True)
    scale = lax.rsqrt(spread + EPSILON)
    return center * scale, scale


def gelu_parts(u):
    size = jnp.abs(u)
    bell = jnp.exp(-0.5 * (u * u))
    t = 1.0 / (1.0 + (0.3275911 * ROOT_HALF) * size)
    poly = t * (
        0.5 * 0.254829592
        + t * (0.5 * -0.284496736 + t * (0.5 * 1.421413741 + t * (0.5 * -1.453152027 + t * (0.5 * 1.061405429))))
    )
    tail = poly * bell
    value = jnp.maximum(u, 0.0) - size * tail
    slope = jnp.where(u > 0, 1.0 - tail, tail) + DENSITY * (u * bell)
    return value, slope


def add_rows(ref, values):
    total = jnp.sum(values, axis=0, keepdims=True)

    @pl.when(pl.program_id(0) == 0)
    def _():
        ref[...] = total

    @pl.when(pl.program_id(0) != 0)
    def _():
        ref[...] += total


def attend_kernel(x_ref, w_ref, vec_ref, seg_ref, code_ref, h_ref, qkv_ref, o_ref, p_ref):
    model = x_ref.shape[-1]
    head = model // HEADS
    n, _ = normalize(x_ref[0].astype(jnp.float32))
    low = (n * vec_ref[0:1] + vec_ref[1:2]).astype(jnp.bfloat16)
    h_ref[0] = low
    q = dot(low, w_ref[:, :model]) + vec_ref[2:3]
    qkv_ref[0, :, :model] = q.astype(jnp.bfloat16) * jnp.bfloat16(head**-0.5)
    qkv_ref[0, :, model : 2 * model] = dot(low, w_ref[:, model : 2 * model]).astype(jnp.bfloat16)
    v = dot(low, w_ref[:, 2 * model : 3 * model]) + vec_ref[3:4]
    qkv_ref[0, :, 2 * model :] = v.astype(jnp.bfloat16)
    bias = jnp.where(seg_ref[0] == code_ref[0], 0.0, -1e30)
    for i in range(HEADS):
        at = slice(i * head, (i + 1) * head)
        k_at = slice(model + i * head, model + (i + 1) * head)
        v_at = slice(2 * model + i * head, 2 * model + (i + 1) * head)
        s = dot(qkv_ref[0, :, at], qkv_ref[0, :, k_at], NT) + bias
        e = jnp.exp(s - jnp.max(s, axis=-1, keepdims=True))
        p = (e * (1.0 / jnp.sum(e, axis=-1, keepdims=True))).astype(jnp.bfloat16)
        p_ref[0, i] = p
        o_ref[0, :, at] = dot(p, qkv_ref[0, :, v_at]).astype(jnp.bfloat16)


def up_kernel(x_ref, o_ref, wo_ref, u0, u1, u2, u3, vec_ref, ub_ref, x2_ref, h2_ref, a_ref, gp_ref):
    x2 = x_ref[0].astype(jnp.float32) + (dot(o_ref[0], wo_ref[...]) + vec_ref[4:5])
    x2_ref[0] = x2
    n, _ = normalize(x2)
    low = (n * vec_ref[5:6] + vec_ref[6:7]).astype(jnp.bfloat16)
    h2_ref[0] = low
    width = wo_ref.shape[1]
    for j, w in enumerate((u0, u1, u2, u3)):
        at = slice(j * width, (j + 1) * width)
        u = dot(low, w[...]) + ub_ref[:, at]
        value, slope = gelu_parts(u)
        a_ref[0, :, at] = value.astype(jnp.bfloat16)
        gp_ref[0, :, at] = slope.astype(jnp.bfloat16)


def down_kernel(x2_ref, a_ref, gp_ref, wd_ref, cot_ref, keep_ref, vec_ref, out_ref, gm_ref, gu_ref, gdb_ref, gub_ref):
    keep = keep_ref[0]
    y = x2_ref[0] + (dot(a_ref[0], wd_ref[...]) + vec_ref[7:8])
    out_ref[0] = (keep * y).astype(jnp.bfloat16)
    gy = keep * cot_ref[0].astype(jnp.float32)
    gm = gy.astype(jnp.bfloat16)
    gm_ref[0] = gm
    add_rows(gdb_ref, gy)
    model = gm.shape[1]
    for j in range(a_ref.shape[2] // model):
        at = slice(j * model, (j + 1) * model)
        ga = dot(gm, wd_ref[at, :], NT)
        gu = (ga * gp_ref[0, :, at].astype(jnp.float32)).astype(jnp.bfloat16)
        gu_ref[0, :, at] = gu
        add_rows(gub_ref.at[:, at], gu.astype(jnp.float32))


def norm_back(grad, n, scale, gain):
    gn = grad * gain
    mean = jnp.mean(gn, axis=-1, keepdims=True)
    cross = jnp.mean(gn * n, axis=-1, keepdims=True)
    return (gn - mean - n * cross) * scale


def middle_kernel(gu_ref, u0, u1, u2, u3, wo_ref, x2_ref, gm_ref, vec_ref, gx_ref, ga_ref, go_ref, gg_ref, gb_ref, gob_ref):
    width = wo_ref.shape[1]
    gh = None
    for j, w in enumerate((u0, u1, u2, u3)):
        part = dot(gu_ref[0, :, j * width : (j + 1) * width], w[...], NT)
        gh = part if gh is None else gh + part
    n, scale = normalize(x2_ref[0])
    add_rows(gg_ref, gh * n)
    add_rows(gb_ref, gh)
    gx = gm_ref[0].astype(jnp.float32) + norm_back(gh, n, scale, vec_ref[5:6])
    gx_ref[0] = gx
    low = gx.astype(jnp.bfloat16)
    ga_ref[0] = low
    add_rows(gob_ref, low.astype(jnp.float32))
    go_ref[0] = dot(low, wo_ref[...], NT).astype(jnp.bfloat16)


def attend_back_kernel(qkv_ref, go_ref, p_ref, g_ref, gqb_ref, gvb_ref):
    model = go_ref.shape[-1]
    head = model // HEADS
    for i in range(HEADS):
        at = slice(i * head, (i + 1) * head)
        k_at = slice(model + i * head, model + (i + 1) * head)
        v_at = slice(2 * model + i * head, 2 * model + (i + 1) * head)
        go = go_ref[0, :, at]
        p = p_ref[0, i]
        dp = dot(go, qkv_ref[0, :, v_at], NT)
        pf = p.astype(jnp.float32)
        delta = jnp.sum(pf * dp, axis=-1, keepdims=True)
        ds = (pf * (dp - delta)).astype(jnp.bfloat16)
        g_ref[0, :, at] = (dot(ds, qkv_ref[0, :, k_at]) * head**-0.5).astype(jnp.bfloat16)
        g_ref[0, :, k_at] = dot(ds, qkv_ref[0, :, at], TN).astype(jnp.bfloat16)
        g_ref[0, :, v_at] = dot(p, go, TN).astype(jnp.bfloat16)
    add_rows(gqb_ref, g_ref[0, :, :model].astype(jnp.float32))
    add_rows(gvb_ref, g_ref[0, :, 2 * model :].astype(jnp.float32))


def input_kernel(g_ref, w_ref, x_ref, gx_ref, vec_ref, out_ref, gg_ref, gb_ref):
    model = x_ref.shape[-1]
    gh = dot(g_ref[0], w_ref[:, : 3 * model], NT)
    n, scale = normalize(x_ref[0].astype(jnp.float32))
    add_rows(gg_ref, gh * n)
    add_rows(gb_ref, gh)
    out_ref[0] = (gx_ref[0] + norm_back(gh, n, scale, vec_ref[0:1])).astype(jnp.bfloat16)


def call(kernel, inputs, outputs, slots, flops, limit=56):
    specs = []
    for array, kind in inputs:
        if kind == "slot":
            rest = array.shape[1:]
            specs.append(pl.BlockSpec((1,) + rest, lambda i, n=len(rest): (i,) + (0,) * n))
        elif kind == "whole":
            specs.append(pl.BlockSpec(array.shape, lambda i, n=array.ndim: (0,) * n))
        else:
            rows = array.shape[0]
            specs.append(pl.BlockSpec((rows, rows), lambda i, j=kind: (0, j)))
    shapes = []
    places = []
    for shape, dtype in outputs:
        shapes.append(jax.ShapeDtypeStruct(shape, dtype))
        if len(shape) > 2:
            places.append(pl.BlockSpec((1,) + shape[1:], lambda i, n=len(shape) - 1: (i,) + (0,) * n))
        else:
            places.append(pl.BlockSpec(shape, lambda i: (0, 0)))
    moved = sum(a.size * a.dtype.itemsize for a, k in inputs if isinstance(k, str))
    moved += sum(s.size * s.dtype.itemsize for s in shapes)
    return pl.pallas_call(
        kernel,
        grid=(slots,),
        in_specs=specs,
        out_specs=places,
        out_shape=shapes,
        compiler_params=pltpu.CompilerParams(vmem_limit_bytes=limit * 1024 * 1024),
        cost_estimate=pl.CostEstimate(flops=flops, bytes_accessed=moved, transcendentals=0),
    )(*[a for a, _ in inputs])


def tn_grad(left, right):
    return jnp.einsum(
        "snd,sne->de", left, right, preferred_element_type=jnp.float32
    ).astype(jnp.bfloat16)


def layer(x, cot, segment, code, keep, mixed, upper, down, vec, up_bias):
    slots, length, model = x.shape
    rows = slots * length
    hidden = down.shape[0]
    bf, f32 = jnp.bfloat16, jnp.float32
    seg = segment[:, :, None]
    codes = code[:, None, :]
    kept = keep[:, :, None]
    full = (slots, length, model)
    scores = 2 * rows * length * model
    h1, qkv, o, p = call(
        attend_kernel,
        [(x, "slot"), (mixed, "whole"), (vec, "whole"), (seg, "slot"), (codes, "slot")],
        [(full, bf), ((slots, length, 3 * model), bf), (full, bf), ((slots, HEADS, length, length), bf)],
        slots,
        6 * rows * model * model + 8 * scores,
    )
    up_cols = [(upper, j) for j in range(1, 1 + hidden // model)]
    x2, h2, a, gp = call(
        up_kernel,
        [(x, "slot"), (o, "slot"), (upper, 0)] + up_cols + [(vec, "whole"), (up_bias, "whole")],
        [(full, f32), (full, bf), ((slots, length, hidden), bf), ((slots, length, hidden), bf)],
        slots,
        2 * rows * model * (model + 2 * hidden),
    )
    out, gm, gu, gdb, gub = call(
        down_kernel,
        [(x2, "slot"), (a, "slot"), (gp, "slot"), (down, "whole"), (cot, "slot"), (kept, "slot"), (vec, "whole")],
        [(full, bf), (full, bf), ((slots, length, hidden), bf), ((1, model), f32), ((1, hidden), f32)],
        slots,
        4 * rows * model * hidden,
    )
    g_down = tn_grad(a, gm)
    gx, ga, go, gmg, gmb, gob = call(
        middle_kernel,
        [(gu, "slot")] + up_cols + [(upper, 0), (x2, "slot"), (gm, "slot"), (vec, "whole")],
        [(full, f32), (full, bf), (full, bf)] + [((1, model), f32)] * 3,
        slots,
        2 * rows * model * (model + hidden),
    )
    g_up = tn_grad(h2, gu)
    g_mix, gqb, gvb = call(
        attend_back_kernel,
        [(qkv, "slot"), (go, "slot"), (p, "slot")],
        [((slots, length, 3 * model), bf)] + [((1, model), f32)] * 2,
        slots,
        16 * scores,
    )
    g_qkv = tn_grad(h1, g_mix)
    in_grad, gag, gab = call(
        input_kernel,
        [(g_mix, "slot"), (mixed, "whole"), (x, "slot"), (gx, "slot"), (vec, "whole")],
        [(full, bf)] + [((1, model), f32)] * 2,
        slots,
        6 * rows * model * model,
    )
    g_out = tn_grad(o, ga)
    return out, in_grad, g_down, g_up, g_qkv, g_out, (gag, gab, gqb, gvb, gob, gmg, gmb, gdb), gub


def body(
    grid,
    tokens,
    cotangent,
    frame_count,
    image_group,
    keep_mask,
    attn_norm_gain,
    attn_norm_bias,
    w_qkv,
    query_bias,
    value_bias,
    w_out,
    out_bias,
    mlp_norm_gain,
    mlp_norm_bias,
    w_up,
    up_bias,
    w_down,
    down_bias,
):
    here = grid.here()
    frames_here = image_group.shape[1]
    block_width = keep_mask.shape[1] // frames_here
    frame_index = lax.axis_index("frame") * frames_here + jnp.arange(frames_here, dtype=jnp.int32)
    segment = jnp.where(frame_index[None, :] < frame_count[:, None], 0, 1 + image_group)
    token_segment = jnp.repeat(segment, block_width, axis=1)
    tags = to_slots(grid, here, token_segment * 2 + keep_mask)
    token_segment = tags // 2
    keep_slots = tags % 2
    key_code = jnp.where(keep_slots == 1, token_segment, -1)
    kept_rows = keep_slots.astype(jnp.float32)

    rows = w_out.shape[0]
    ratio = up_bias.shape[0] // rows
    small = jnp.stack(
        [attn_norm_gain, attn_norm_bias, query_bias, value_bias, out_bias, mlp_norm_gain, mlp_norm_bias, down_bias],
        axis=1,
    )
    small = jnp.concatenate([small, up_bias.reshape(rows, ratio)], axis=1)
    small = jnp.pad(small, ((0, 0), (0, 128 - small.shape[1])))
    token_rows = to_slots(grid, here, tokens)

    mixed = gather_group(grid, here, jnp.concatenate([w_qkv, small], axis=1))
    upper = gather_group(grid, here, jnp.concatenate([w_out, w_up], axis=1))
    down = gather_group(grid, here, w_down)
    cotangent_rows = to_slots(grid, here, cotangent)
    vec = mixed[:, w_qkv.shape[1] :].astype(jnp.float32).T
    up_bias_row = vec[8 : 8 + ratio].T.reshape(1, -1)
    output_rows, input_rows, g_down, g_up, g_qkv, g_out, sums, g_up_bias = layer(
        token_rows, cotangent_rows, token_segment, key_code, kept_rows, mixed, upper, down, vec[:8], up_bias_row
    )
    output = from_slots(grid, here, output_rows)
    g_down = scatter_group(grid, here, g_down)
    g_up = scatter_group(grid, here, g_up)
    g_qkv = scatter_group(grid, here, g_qkv)
    input_grad = from_slots(grid, here, input_rows).astype(jnp.float32)
    model = w_out.shape[1]
    pack = jnp.concatenate(list(sums) + [g_up_bias.reshape(-1, ratio).T], axis=0)
    pack = jnp.pad(pack, ((0, 128 - pack.shape[0]), (0, 0))).T.astype(jnp.bfloat16)
    last = scatter_group(grid, here, jnp.concatenate([g_out, pack], axis=1))
    v = [last[:, model + i] for i in range(8)]
    return (
        output, input_grad, v[0], v[1], g_qkv, v[2], v[3], last[:, :model], v[4], v[5], v[6],
        g_up, last[:, model + 8 : model + 8 + ratio].reshape(-1), g_down, v[7],
    )


def solution(mesh):
    grid = Grid(mesh.shape["frame"], mesh.shape["clip"])

    def run(*arguments):
        return body(grid, *arguments)

    placed = (
        P("clip", "frame", None),
        P("clip", "frame", None),
        P("clip"),
        P("clip", "frame"),
        P("clip", "frame"),
        P(("frame", "clip")),
        P(("frame", "clip")),
        P(("frame", "clip"), None),
        P(("frame", "clip")),
        P(("frame", "clip")),
        P(("frame", "clip"), None),
        P(("frame", "clip")),
        P(("frame", "clip")),
        P(("frame", "clip")),
        P(("frame", "clip"), None),
        P(("frame", "clip")),
        P(("frame", "clip"), None),
        P(("frame", "clip")),
    )
    return jax.shard_map(
        run,
        mesh=mesh,
        in_specs=placed,
        out_specs=(
            P("clip", "frame", None),
            P("clip", "frame", None),
            P(("frame", "clip")),
            P(("frame", "clip")),
            P(("frame", "clip"), None),
            P(("frame", "clip")),
            P(("frame", "clip")),
            P(("frame", "clip"), None),
            P(("frame", "clip")),
            P(("frame", "clip")),
            P(("frame", "clip")),
            P(("frame", "clip"), None),
            P(("frame", "clip")),
            P(("frame", "clip"), None),
            P(("frame", "clip")),
        ),
        check_vma=False,
    )
```

```python
import jax
import jax.numpy as jnp
from jax import lax
from jax.experimental import pallas as pl
from jax.experimental.pallas import tpu as pltpu
from jax.sharding import Mesh
from jax.sharding import PartitionSpec as P

HEADS = 12
EPSILON = 1e-06
AXES = ("x", "core", "z", "y")
FRAME = ("x", "core")
ANY = pl.BlockSpec(memory_space=pl.ANY)


def index_of(sizes, at):
    value = 0
    for name, size in zip(AXES, sizes):
        value = value * size + at[name]
    return value


def swap(sizes, value, choose):
    pairs = []
    for x in range(sizes[0]):
        for core in range(sizes[1]):
            for z in range(sizes[2]):
                for y in range(sizes[3]):
                    at = {"x": x, "core": core, "z": z, "y": y}
                    pairs.append((index_of(sizes, at), index_of(sizes, choose(dict(at)))))
    return lax.ppermute(value, AXES, pairs)


def near_peer(at):
    at["y" if at["core"] else "x"] ^= 1
    return at


def far_peer(at):
    at["x" if at["core"] else "y"] ^= 1
    return at


def line_peer(bits):
    def choose(at):
        at["z"] ^= bits
        return at

    return choose


def core_peer(at):
    at["core"] ^= 1
    return at


def cell(core, x, y, near, far):
    return jnp.where(core == 0, x ^ near, x ^ far), jnp.where(core == 0, y ^ far, y ^ near)


def hold(value, after):
    def body(*refs):
        pass

    return pl.pallas_call(
        body,
        in_specs=[ANY] * (1 + len(after)),
        out_specs=ANY,
        out_shape=jax.ShapeDtypeStruct(value.shape, value.dtype),
        input_output_aliases={0: 0},
    )(value, *after)


def columns_of(vectors, tail):
    rows = tail.shape[0]

    def body(*refs):
        out = refs[-1]
        lines = jnp.concatenate([ref[...].astype(jnp.float32) for ref in refs[:-2]], axis=0)
        lines = jnp.pad(lines, ((0, 0), (0, 128 - rows)))
        turned = jnp.pad(lines, ((0, 128 - lines.shape[0]), (0, 0))).T[:rows]
        out[...] = turned.astype(jnp.bfloat16)
        out[:, len(vectors) : len(vectors) + tail.shape[1]] = refs[-2][...]

    return pl.pallas_call(
        body, out_shape=jax.ShapeDtypeStruct((rows, 128), jnp.bfloat16)
    )(*[v.reshape(1, rows) for v in vectors], tail)


class Gather:
    def __init__(self, sizes, here, shard):
        self.sizes, self.here = sizes, here
        self.column = jnp.stack([shard] + [swap(sizes, shard, line_peer(bits)) for bits in range(1, sizes[2])])

    def second(self, after=()):
        column = hold(self.column, after) if after else self.column
        self.pieces = {
            (0, 0): column,
            (1, 0): swap(self.sizes, column, near_peer),
            (0, 1): swap(self.sizes, column, far_peer),
        }
        return [self.pieces[1, 0], self.pieces[0, 1]]

    def third(self, after=()):
        piece = self.pieces[1, 0]
        if after:
            piece = hold(piece, after)
            self.pieces[1, 0] = piece
        self.pieces[1, 1] = swap(self.sizes, piece, far_peer)
        return [self.pieces[1, 1]]

    def whole(self):
        keys = sorted(self.pieces)
        mine = [self.pieces[key] for key in keys]
        theirs = [swap(self.sizes, piece, core_peer) for piece in mine]
        count, rows, width = mine[0].shape
        total = 2 * len(keys)

        def body(here_ref, *refs):
            out, sems = refs[total], refs[total + 1]
            copies = []
            for side in range(2):
                core = here_ref[1] ^ side
                for index, (near, far) in enumerate(keys):
                    x, y = cell(core, here_ref[0], here_ref[3], near, far)
                    slot = side * len(keys) + index
                    for bits in range(count):
                        to = out.at[x, core, here_ref[2] ^ bits, y]
                        copies.append(pltpu.make_async_copy(refs[slot].at[bits], to, sems.at[slot * count + bits]))
            for copy in copies:
                copy.start()
            for copy in copies:
                copy.wait()

        full = pl.pallas_call(
            body,
            in_specs=[pl.BlockSpec(memory_space=pltpu.SMEM)] + [ANY] * total,
            out_specs=pl.BlockSpec(memory_space=pltpu.VMEM),
            out_shape=jax.ShapeDtypeStruct((self.sizes[0], 2, count, 2, rows, width), mine[0].dtype),
            scratch_shapes=[pltpu.SemaphoreType.DMA((total * count,))],
        )(self.here, *mine, *theirs)
        return full.reshape(-1, width)


class Scatter:
    def __init__(self, sizes, here, sent, kept):
        self.sizes, self.here = sizes, here
        rows = kept.shape[1] // (sizes[2] * 2)
        shape = (sizes[0], sizes[2], 2, rows, kept.shape[2])
        self.kept = kept.reshape(shape)
        self.came = swap(sizes, sent.reshape(shape), core_peer)

    def second(self):
        x_count, count, _, rows, width = self.kept.shape
        block = (1, count, 1, rows, width)

        def body(here_ref, kept_ref, came_ref, sent_ref, own_ref):
            def fill(to_ref):
                for bits in range(count):
                    z = here_ref[2] ^ bits
                    value = kept_ref[0, z, 0].astype(jnp.float32) + came_ref[0, z, 0].astype(jnp.float32)
                    to_ref[0, bits] = value.astype(jnp.bfloat16)

            @pl.when(pl.program_id(0) == 0)
            def _():
                fill(sent_ref)

            @pl.when(pl.program_id(0) == 1)
            def _():
                fill(own_ref)

        def place(phase, far, here_ref):
            x, y = cell(here_ref[1], here_ref[0], here_ref[3], 1 - phase, far)
            return x, 0, y, 0, 0

        spec = pl.BlockSpec(block, place)
        shape = jax.ShapeDtypeStruct((2, count, rows, width), jnp.bfloat16)
        sent, own = pl.pallas_call(
            body,
            grid_spec=pltpu.PrefetchScalarGridSpec(
                num_scalar_prefetch=1,
                grid=(2, 2),
                in_specs=[spec, spec],
                out_specs=[
                    pl.BlockSpec((1, count, rows, width), lambda p, f, h: (jnp.where(p == 0, f, 1), 0, 0, 0)),
                    pl.BlockSpec((1, count, rows, width), lambda p, f, h: (jnp.where(p == 0, 0, f), 0, 0, 0)),
                ],
            ),
            out_shape=[shape, shape],
            cost_estimate=pl.CostEstimate(flops=0, bytes_accessed=6 * self.kept.size, transcendentals=0),
        )(self.here, self.kept, self.came)
        self.kept = own
        self.came = swap(self.sizes, sent, near_peer)
        return [self.came]

    def third(self):
        _, count, rows, width = self.kept.shape
        block = (1, count, rows, width)

        def body(kept_ref, came_ref, sent_ref, own_ref):
            value = kept_ref[0].astype(jnp.float32) + came_ref[0].astype(jnp.float32)
            value = value.astype(jnp.bfloat16)

            @pl.when(pl.program_id(0) == 0)
            def _():
                sent_ref[...] = value

            @pl.when(pl.program_id(0) == 1)
            def _():
                own_ref[...] = value

        spec = pl.BlockSpec(block, lambda i: (1 - i, 0, 0, 0))
        whole = pl.BlockSpec(block[1:], lambda i: (0, 0, 0))
        shape = jax.ShapeDtypeStruct(block[1:], jnp.bfloat16)
        sent, own = pl.pallas_call(
            body,
            grid=(2,),
            in_specs=[spec, spec],
            out_specs=[whole, whole],
            out_shape=[shape, shape],
            cost_estimate=pl.CostEstimate(flops=0, bytes_accessed=6 * self.kept.size, transcendentals=0),
        )(self.kept, self.came)
        self.kept = own
        self.came = swap(self.sizes, sent, far_peer)
        return [self.came]

    def fourth(self):
        value = (self.kept.astype(jnp.float32) + self.came.astype(jnp.float32)).astype(jnp.bfloat16)
        self.parts = [value[0]]
        for bits in range(1, self.sizes[2]):
            self.parts.append(swap(self.sizes, value[bits], line_peer(bits)))
        return self.parts[1:]

    def last(self):
        return sum(part.astype(jnp.float32) for part in self.parts)


ROOT_HALF = 0.7071067811865476
DENSITY = 0.3989422804014327
NT = (((1,), (1,)), ((), ()))
NN = (((1,), (0,)), ((), ()))
TN = (((0,), (0,)), ((), ()))


def dot(left, right, dims=NN):
    return lax.dot_general(left, right, dims, preferred_element_type=jnp.float32)


def normalize(values):
    center = values - jnp.mean(values, axis=-1, keepdims=True)
    spread = jnp.mean(center * center, axis=-1, keepdims=True)
    scale = lax.rsqrt(spread + EPSILON)
    return center * scale, scale


def gelu_parts(u):
    size = jnp.abs(u)
    bell = jnp.exp(-0.5 * (u * u))
    t = 1.0 / (1.0 + (0.3275911 * ROOT_HALF) * size)
    poly = t * (
        0.5 * 0.254829592
        + t * (0.5 * -0.284496736 + t * (0.5 * 1.421413741 + t * (0.5 * -1.453152027 + t * (0.5 * 1.061405429))))
    )
    tail = poly * bell
    value = jnp.maximum(u, 0.0) - size * tail
    slope = jnp.where(u > 0, 1.0 - tail, tail) + DENSITY * (u * bell)
    return value, slope


def add_rows(ref, values):
    total = jnp.sum(values, axis=0, keepdims=True)

    @pl.when(pl.program_id(0) == 0)
    def _():
        ref[...] = total

    @pl.when(pl.program_id(0) != 0)
    def _():
        ref[...] += total


def rows_of(ref):
    return ref[...].reshape(-1, ref.shape[-1])


def attend_kernel(x_ref, w_ref, vec_ref, column_ref, row_ref, h_ref, qkv_ref, o_ref, p_ref):
    model = x_ref.shape[-1]
    head = model // HEADS
    n, _ = normalize(rows_of(x_ref).astype(jnp.float32))
    low = (n * vec_ref[0:1] + vec_ref[1:2]).astype(jnp.bfloat16)
    h_ref[0] = low
    q = dot(low, w_ref[:, :model]) + vec_ref[2:3]
    qkv_ref[0, :, :model] = q.astype(jnp.bfloat16) * jnp.bfloat16(head**-0.5)
    qkv_ref[0, :, model : 2 * model] = dot(low, w_ref[:, model : 2 * model]).astype(jnp.bfloat16)
    v = dot(low, w_ref[:, 2 * model : 3 * model]) + vec_ref[3:4]
    qkv_ref[0, :, 2 * model :] = v.astype(jnp.bfloat16)
    code = row_ref[0]
    code = jnp.where(code & 1 == 1, code >> 1, -1)
    bias = jnp.where(column_ref[0] >> 1 == code, 0.0, -1e30)
    for i in range(HEADS):
        at = slice(i * head, (i + 1) * head)
        k_at = slice(model + i * head, model + (i + 1) * head)
        v_at = slice(2 * model + i * head, 2 * model + (i + 1) * head)
        s = dot(qkv_ref[0, :, at], qkv_ref[0, :, k_at], NT) + bias
        e = jnp.exp(s - jnp.max(s, axis=-1, keepdims=True))
        p = (e * (1.0 / jnp.sum(e, axis=-1, keepdims=True))).astype(jnp.bfloat16)
        p_ref[0, i] = p
        o_ref[0, :, at] = dot(p, qkv_ref[0, :, v_at]).astype(jnp.bfloat16)


def project_kernel(x_ref, o_ref, wo_ref, vec_ref, x2_ref, h2_ref):
    x2 = rows_of(x_ref).astype(jnp.float32) + (dot(o_ref[0], wo_ref[...]) + vec_ref[4:5])
    x2_ref[0] = x2
    n, _ = normalize(x2)
    h2_ref[0] = (n * vec_ref[5:6] + vec_ref[6:7]).astype(jnp.bfloat16)


def mlp(here, h2, cot, tags, upper, down, up_bias, after):
    slots, length, model = h2.shape
    rows = slots * length
    hidden = down.shape[0]
    steps = hidden // model
    peers, _, width, _ = cot.shape
    chunk = model // peers
    bf, f32 = jnp.bfloat16, jnp.float32

    def body(here_ref, h2_ref, cot_ref, tag_ref, u_ref, d_ref, b_ref, *refs):
        y_ref, gh_ref, gm_ref, ds_ref, dk_ref, us_ref, uk_ref, gub_ref, gdb_ref, y_acc, gh_acc, block = refs[len(after):]
        step = pl.program_id(0)
        core = here_ref[1]

        @pl.when(step == 0)
        def _():
            total = jnp.zeros((1, model), f32)
            for slot in range(slots):
                keep = (tag_ref[slot] & 1).astype(f32)
                gy = keep * cot_ref[:, slot].reshape(length, model).astype(f32)
                gm_ref[slot] = gy.astype(bf)
                total += jnp.sum(gy, axis=0, keepdims=True)
            gdb_ref[...] = total

        h2 = h2_ref[...].reshape(rows, model)
        gm = gm_ref[...].reshape(rows, model)
        up, down = u_ref[...], d_ref[...]
        value, slope = gelu_parts(dot(h2, up) + b_ref[...])
        a = value.astype(bf)
        y = dot(a, down)
        gu32 = dot(gm, down, NT) * slope
        gu = gu32.astype(bf)
        gub_ref[...] = jnp.sum(gu.astype(f32), axis=0, keepdims=True)
        gh = dot(gu, up, NT)

        @pl.when(step == 0)
        def _():
            y_acc[...] = y
            gh_acc[...] = gh

        @pl.when(step != 0)
        def _():
            y_acc[...] += y
            gh_acc[...] += gh

        g_down = dot(a, gm, TN).astype(bf)

        @pl.when(step < steps // 2)
        def _():
            ds_ref[0] = g_down

        @pl.when(step >= steps // 2)
        def _():
            dk_ref[0] = g_down

        block[...] = dot(h2, gu, TN).astype(bf).reshape(block.shape)
        for x in range(2):
            us_ref[x] = block[2 * x + (1 - core)]
            uk_ref[x] = block[2 * x + core]

        @pl.when(step == steps - 1)
        def _():
            y_ref[...] = y_acc[...].reshape(y_ref.shape)
            gh_ref[...] = gh_acc[...].reshape(gh_ref.shape)

    def at(step, here_ref):
        return 2 * (step % 2) + (here_ref[1] ^ (1 - step // 2))

    full = pl.BlockSpec((slots, length, model), lambda i, h: (0, 0, 0))
    shape = (slots, length, model)
    part = jax.ShapeDtypeStruct((2, model, model), bf)
    side = jax.ShapeDtypeStruct((2, chunk, hidden), bf)
    line = jax.ShapeDtypeStruct((1, model), f32)
    return pl.pallas_call(
        body,
        grid_spec=pltpu.PrefetchScalarGridSpec(
            num_scalar_prefetch=1,
            grid=(steps,),
            in_specs=[
                full,
                pl.BlockSpec(cot.shape, lambda i, h: (0, 0, 0, 0)),
                pl.BlockSpec(tags.shape, lambda i, h: (0, 0, 0)),
                pl.BlockSpec((model, model), lambda i, h: (0, 1 + at(i, h))),
                pl.BlockSpec((model, model), lambda i, h: (at(i, h), 0)),
                pl.BlockSpec((1, model), lambda i, h: (0, at(i, h))),
            ]
            + [ANY] * len(after),
            out_specs=[
                full,
                full,
                full,
                pl.BlockSpec((1, model, model), lambda i, h: (jnp.minimum(i, 1), 0, 0)),
                pl.BlockSpec((1, model, model), lambda i, h: (jnp.maximum(i - 2, 0), 0, 0)),
                pl.BlockSpec((2, chunk, model), lambda i, h: (0, 0, at(i, h))),
                pl.BlockSpec((2, chunk, model), lambda i, h: (0, 0, at(i, h))),
                pl.BlockSpec((1, model), lambda i, h: (0, at(i, h))),
                pl.BlockSpec((1, model), lambda i, h: (0, 0)),
            ],
            scratch_shapes=[
                pltpu.VMEM((rows, model), f32),
                pltpu.VMEM((rows, model), f32),
                pltpu.VMEM((4, chunk, model), bf),
            ],
        ),
        out_shape=[
            jax.ShapeDtypeStruct(shape, f32),
            jax.ShapeDtypeStruct(shape, f32),
            jax.ShapeDtypeStruct(shape, bf),
            part, part, side, side,
            jax.ShapeDtypeStruct((1, hidden), f32),
            line,
        ],
        compiler_params=pltpu.CompilerParams(vmem_limit_bytes=58 * 1024 * 1024),
        cost_estimate=pl.CostEstimate(
            flops=12 * rows * model * hidden, bytes_accessed=30 * rows * model, transcendentals=rows * hidden
        ),
    )(here, h2, cot, tags, upper, down, up_bias, *after)


def norm_back(grad, n, scale, gain):
    gn = grad * gain
    mean = jnp.mean(gn, axis=-1, keepdims=True)
    cross = jnp.mean(gn * n, axis=-1, keepdims=True)
    return (gn - mean - n * cross) * scale


def middle_kernel(y_ref, gh_ref, wo_ref, x2_ref, gm_ref, tag_ref, vec_ref, out_ref, gx_ref, ga_ref, go_ref, gg_ref, gb_ref, gob_ref):
    x2 = x2_ref[0]
    keep = (tag_ref[0] & 1).astype(jnp.float32)
    out_ref[...] = (keep * (x2 + (y_ref[0] + vec_ref[7:8]))).astype(jnp.bfloat16).reshape(out_ref.shape)
    gh = gh_ref[0]
    n, scale = normalize(x2)
    add_rows(gg_ref, gh * n)
    add_rows(gb_ref, gh)
    gx = gm_ref[0].astype(jnp.float32) + norm_back(gh, n, scale, vec_ref[5:6])
    gx_ref[0] = gx
    low = gx.astype(jnp.bfloat16)
    ga_ref[0] = low
    add_rows(gob_ref, low.astype(jnp.float32))
    go_ref[0] = dot(low, wo_ref[...], NT).astype(jnp.bfloat16)


def attend_back_kernel(qkv_ref, go_ref, p_ref, q_sum_ref, v_sum_ref, g_ref, gqb_ref, gvb_ref):
    model = go_ref.shape[-1]
    head = model // HEADS
    for i in range(HEADS):
        at = slice(i * head, (i + 1) * head)
        k_at = slice(model + i * head, model + (i + 1) * head)
        v_at = slice(2 * model + i * head, 2 * model + (i + 1) * head)
        go = go_ref[0, :, at]
        p = p_ref[0, i]
        dp = dot(go, qkv_ref[0, :, v_at], NT)
        pf = p.astype(jnp.float32)
        delta = jnp.sum(pf * dp, axis=-1, keepdims=True)
        ds = (pf * (dp - delta)).astype(jnp.bfloat16)
        g_ref[0, :, at] = (dot(ds, qkv_ref[0, :, k_at]) * head**-0.5).astype(jnp.bfloat16)
        g_ref[0, :, k_at] = dot(ds, qkv_ref[0, :, at], TN).astype(jnp.bfloat16)
        g_ref[0, :, v_at] = dot(p, go, TN).astype(jnp.bfloat16)
    gqb_ref[...] = q_sum_ref[...] + jnp.sum(g_ref[0, :, :model].astype(jnp.float32), axis=0, keepdims=True)
    gvb_ref[...] = v_sum_ref[...] + jnp.sum(g_ref[0, :, 2 * model :].astype(jnp.float32), axis=0, keepdims=True)


def input_kernel(g_ref, w_ref, x_ref, gx_ref, vec_ref, out_ref, gg_ref, gb_ref):
    model = x_ref.shape[-1]
    gh = dot(g_ref[0], w_ref[:, : 3 * model], NT)
    n, scale = normalize(rows_of(x_ref).astype(jnp.float32))
    add_rows(gg_ref, gh * n)
    add_rows(gb_ref, gh)
    grad = gx_ref[0] + norm_back(gh, n, scale, vec_ref[0:1])
    out_ref[...] = grad.astype(jnp.bfloat16).reshape(out_ref.shape)


def call(kernel, inputs, outputs, slots, flops, first=0, carry=None, after=(), limit=56):
    specs = []
    for array, kind in inputs:
        if kind == "slot":
            rest = array.shape[1:]
            specs.append(pl.BlockSpec((1,) + rest, lambda i, n=len(rest): (i + first,) + (0,) * n))
        elif kind == "frames":
            rest = array.shape[2:]
            specs.append(pl.BlockSpec((array.shape[0], 1) + rest, lambda i: (0, i + first, 0, 0)))
        elif kind == "whole":
            specs.append(pl.BlockSpec(array.shape, lambda i, n=array.ndim: (0,) * n))
        else:
            rows = array.shape[0]
            specs.append(pl.BlockSpec((rows, rows), lambda i, j=kind: (0, j)))
    shapes = []
    places = []
    aliases = {}
    extra = list(after)
    for index, (shape, dtype) in enumerate(outputs):
        shapes.append(jax.ShapeDtypeStruct(shape, dtype))
        if len(shape) == 4 and shape[1] != HEADS:
            places.append(pl.BlockSpec((shape[0], 1) + shape[2:], lambda i: (0, i + first, 0, 0)))
        elif len(shape) > 2:
            places.append(pl.BlockSpec((1,) + shape[1:], lambda i, n=len(shape) - 1: (i + first,) + (0,) * n))
            if carry is not None:
                aliases[len(inputs) + len(extra)] = index
                extra.append(carry[index])
        else:
            places.append(pl.BlockSpec(shape, lambda i: (0, 0)))
    specs += [pl.BlockSpec(memory_space=pl.ANY)] * len(extra)
    moved = sum(a.size * a.dtype.itemsize for a, k in inputs if isinstance(k, str))
    moved += sum(s.size * s.dtype.itemsize for s in shapes)
    used = len(inputs)
    skip = used + len(extra)

    def run(*refs):
        kernel(*refs[:used], *refs[skip:])

    return pl.pallas_call(
        run,
        grid=(slots,),
        in_specs=specs,
        out_specs=places,
        out_shape=shapes,
        input_output_aliases=aliases,
        compiler_params=pltpu.CompilerParams(vmem_limit_bytes=limit * 1024 * 1024),
        cost_estimate=pl.CostEstimate(flops=flops, bytes_accessed=moved, transcendentals=0),
    )(*[a for a, _ in inputs], *extra)


def row_grad(here, products, after):
    slots, length, model = products[0][0].shape
    steps = []
    for index, (_, right) in enumerate(products):
        steps += [index] * (right.shape[2] // model)
    starts = [steps.index(index) for index in range(len(products))]
    chunk = model // 4
    used = 2 * len(products)

    def body(here_ref, *refs):
        sent_ref, kept_ref, value_ref = refs[-3:]
        core = here_ref[1]
        step = pl.program_id(0)
        for index in range(len(products)):
            end = starts[index] + steps.count(index)

            @pl.when((step >= starts[index]) & (step < end))
            def _():
                left, right = refs[2 * index], refs[2 * index + 1]
                value = dot(left[...].reshape(-1, model), right[...].reshape(-1, model), TN)
                value_ref[...] = value.astype(jnp.bfloat16).reshape(value_ref.shape)

        for x in range(2):
            sent_ref[x] = value_ref[2 * x + (1 - core)]
            kept_ref[x] = value_ref[2 * x + core]

    specs = []
    for index, (left, right) in enumerate(products):
        most = right.shape[2] // model - 1
        specs.append(pl.BlockSpec((slots, length, model), lambda i, h: (0, 0, 0)))
        specs.append(
            pl.BlockSpec(
                (slots, length, model),
                lambda i, h, s=starts[index], m=most: (0, 0, jnp.clip(i - s, 0, m)),
            )
        )
    shape = jax.ShapeDtypeStruct((2, chunk, len(steps) * model), jnp.bfloat16)
    out = pl.BlockSpec((2, chunk, model), lambda i, h: (0, 0, i))
    return pl.pallas_call(
        body,
        grid_spec=pltpu.PrefetchScalarGridSpec(
            num_scalar_prefetch=1,
            grid=(len(steps),),
            in_specs=specs + [ANY] * len(after),
            out_specs=[out, out],
            scratch_shapes=[pltpu.VMEM((4, chunk, model), jnp.bfloat16)],
        ),
        out_shape=[shape, shape],
        compiler_params=pltpu.CompilerParams(vmem_limit_bytes=56 * 1024 * 1024),
        cost_estimate=pl.CostEstimate(
            flops=2 * slots * length * model * model * len(steps),
            bytes_accessed=2 * sum(r.size for _, r in products),
            transcendentals=0,
        ),
    )(here, *[array for pair in products for array in pair], *after)


def turned(lines, tail):
    width = lines[0].shape[1]

    def body(*refs):
        out = refs[-1]
        value = jnp.concatenate([ref[...] for ref in refs[:-2]], axis=0)
        value = jnp.pad(value, ((0, 128 - value.shape[0]), (0, 0))).T
        out[...] = value.astype(jnp.bfloat16)
        out[:, len(lines) : len(lines) + tail.shape[1]] = refs[-2][...].astype(jnp.bfloat16)

    return pl.pallas_call(
        body, out_shape=jax.ShapeDtypeStruct((width, 128), jnp.bfloat16)
    )(*lines, tail)


def body(
    sizes,
    tokens,
    cotangent,
    frame_count,
    image_group,
    keep_mask,
    attn_norm_gain,
    attn_norm_bias,
    w_qkv,
    query_bias,
    value_bias,
    w_out,
    out_bias,
    mlp_norm_gain,
    mlp_norm_bias,
    w_up,
    up_bias,
    w_down,
    down_bias,
):
    bf, f32 = jnp.bfloat16, jnp.float32
    here = jnp.stack([lax.axis_index(name) for name in AXES]).astype(jnp.int32)
    peers = sizes[0] * sizes[1]
    frames_here = image_group.shape[1]
    block_width = keep_mask.shape[1] // frames_here
    frame_index = lax.axis_index(FRAME) * frames_here + jnp.arange(frames_here, dtype=jnp.int32)
    segment = jnp.where(frame_index[None, :] < frame_count[:, None], 0, 1 + image_group)
    tags = jnp.repeat(segment, block_width, axis=1) * 2 + keep_mask

    def exchange(value):
        return lax.all_to_all(value, FRAME, 0, 0, tiled=True)

    rows, model = w_out.shape
    hidden = w_up.shape[1]
    ratio = hidden // model
    vectors = [
        attn_norm_gain, attn_norm_bias, query_bias, value_bias, out_bias, mlp_norm_gain, mlp_norm_bias, down_bias
    ]
    small = columns_of(vectors, up_bias.reshape(rows, ratio))
    slots = tokens.shape[0] // peers
    length = peers * tokens.shape[1]
    here_rows = slots * length
    framed = (peers, slots, tokens.shape[1], model)
    full = (slots, length, model)
    wide = (slots, length, hidden)
    scores = 2 * here_rows * length * model
    each = (1,) * slots

    get_mixed = Gather(sizes, here, jnp.concatenate([w_qkv, small], axis=1))
    x = exchange(tokens).reshape(framed)
    tags = exchange(tags).reshape(peers, slots, -1).transpose(1, 0, 2).reshape(slots, length)
    tag_rows, tag_columns = tags[:, None, :], tags[:, :, None]
    get_mixed.second()
    get_upper = Gather(sizes, here, hold(jnp.concatenate([w_out, w_up], axis=1), [get_mixed.column]))
    get_mixed.third()
    mixed = get_mixed.whole()
    get_upper.second([mixed])
    vec = mixed[:, w_qkv.shape[1] :].astype(f32).T
    up_bias_row = vec[8 : 8 + ratio].T.reshape(1, -1)
    vec = vec[:8]

    attend = (
        attend_kernel,
        [(x, "frames"), (mixed, "whole"), (vec, "whole"), (tag_columns, "slot"), (tag_rows, "slot")],
        [(full, bf), ((slots, length, 3 * model), bf), (full, bf), ((slots, HEADS, length, length), bf)],
    )
    cost = (6 * here_rows * model * model + 8 * scores) // slots
    state = call(*attend, 1, cost, 0, None, [get_upper.pieces[0, 0]])
    get_down = Gather(sizes, here, hold(w_down, [state[2]]))
    get_upper.third([state[2]])
    state = call(*attend, 1, cost, 1, state, [get_upper.pieces[1, 0], get_upper.pieces[0, 1]])
    get_down.second([state[2]])
    for slot in range(2, slots):
        state = call(*attend, 1, cost, slot, state, [get_upper.pieces[1, 1], get_down.column] if slot == 2 else [])
    h1, qkv, o, p = state
    upper = get_upper.whole()
    get_down.third([o])
    cot = exchange(hold(cotangent, [get_down.pieces[1, 1]])).reshape(framed)
    x2, h2 = call(
        project_kernel,
        [(x, "frames"), (o, "slot"), (upper, 0), (vec, "whole")],
        [(full, f32), (full, bf)],
        slots,
        2 * here_rows * model * model,
        after=[get_down.pieces[1, 0], get_down.pieces[0, 1]],
    )
    down = get_down.whole()
    y, gh, gm, down_sent, down_kept, up_sent, up_kept, gub, gdb = mlp(
        here, h2, cot, tag_columns, upper, down, up_bias_row, []
    )
    put_down = Scatter(sizes, here, down_sent, down_kept)
    out, gx, ga, go, gmg, gmb, gob = call(
        middle_kernel,
        [(y, "slot"), (gh, "slot"), (upper, 0), (x2, "slot"), (gm, "slot"), (tag_columns, "slot"), (vec, "whole")],
        [(framed, bf), (full, f32), (full, bf), (full, bf)] + [((1, model), f32)] * 3,
        slots,
        2 * here_rows * model * model,
    )
    put_down.second()
    put_up = Scatter(sizes, here, hold(up_sent, [put_down.kept]), up_kept)
    output = exchange(out.reshape(tokens.shape))
    zero = jnp.zeros((1, model), f32)
    state = [None, zero, zero]
    order = [[put_up.came]]
    for slot in range(slots):
        state = call(
            attend_back_kernel,
            [(qkv, "slot"), (go, "slot"), (p, "slot"), (state[1], "whole"), (state[2], "whole")],
            [((slots, length, 3 * model), bf)] + [((1, model), f32)] * 2,
            1,
            16 * scores // slots,
            slot,
            state if slot else None,
            order[slot] if slot < len(order) else [],
        )
        if slot == 0:
            put_down.kept = hold(put_down.kept, [state[0]])
            order.append(put_down.third() + put_up.second())
        elif slot == 1:
            put_down.kept = hold(put_down.kept, [state[0]])
            order.append(put_down.fourth()[:0])
    g_mix, gqb, gvb = state
    put_up.kept = hold(put_up.kept, [g_mix])
    put_up.third()
    put_mixed = Scatter(sizes, here, *row_grad(here, [(h1, g_mix), (o, ga)], [put_down.came]))
    in_grad, gag, gab = call(
        input_kernel,
        [(g_mix, "slot"), (mixed, "whole"), (x, "frames"), (gx, "slot"), (vec, "whole")],
        [(framed, bf)] + [((1, model), f32)] * 2,
        slots,
        6 * here_rows * model * model,
        after=[put_mixed.kept, put_up.came],
    )
    put_up.fourth()
    put_mixed.second()
    input_grad = exchange(hold(in_grad.reshape(tokens.shape), [put_mixed.kept])).astype(f32)
    sums = [gag, gab, gqb, gvb, gob, gmg, gmb, gdb]
    pack = turned(sums, gub.reshape(-1, ratio))
    pack = lax.all_to_all(pack.reshape(-1, rows, 128), AXES, 0, 0, tiled=True)
    last = jnp.sum(pack.astype(f32), axis=0)
    put_mixed.third()
    put_mixed.fourth()
    mixed_rows = put_mixed.last()
    g_qkv, g_out = mixed_rows[:, : 3 * model], mixed_rows[:, 3 * model :]
    v = [last[:, i] for i in range(8)]
    return (
        output, input_grad, v[0], v[1], g_qkv, v[2], v[3], g_out, v[4], v[5], v[6],
        put_up.last(), last[:, 8 : 8 + ratio].reshape(-1), put_down.last(), v[7],
    )


def solution(mesh):
    frames, clips = mesh.shape["frame"], mesh.shape["clip"]
    sizes = (frames // 2, 2, clips // 2, 2)
    mesh = Mesh(mesh.devices.reshape(sizes), AXES)

    def run(*arguments):
        return body(sizes, *arguments)

    placed = (
        P(("z", "y"), FRAME, None),
        P(("z", "y"), FRAME, None),
        P(("z", "y")),
        P(("z", "y"), FRAME),
        P(("z", "y"), FRAME),
        P(AXES),
        P(AXES),
        P(AXES, None),
        P(AXES),
        P(AXES),
        P(AXES, None),
        P(AXES),
        P(AXES),
        P(AXES),
        P(AXES, None),
        P(AXES),
        P(AXES, None),
        P(AXES),
    )
    return jax.shard_map(
        run,
        mesh=mesh,
        in_specs=placed,
        out_specs=(
            P(("z", "y"), FRAME, None),
            P(("z", "y"), FRAME, None),
            P(AXES),
            P(AXES),
            P(AXES, None),
            P(AXES),
            P(AXES),
            P(AXES, None),
            P(AXES),
            P(AXES),
            P(AXES),
            P(AXES, None),
            P(AXES),
            P(AXES, None),
            P(AXES),
        ),
        check_vma=False,
    )
```

```python
import jax
import jax.numpy as jnp
from jax import lax
from jax.experimental import pallas as pl
from jax.experimental.pallas import tpu as pltpu
from jax.sharding import Mesh
from jax.sharding import PartitionSpec as P

HEADS = 12
EPSILON = 1e-06
AXES = ("x", "core", "z", "y")
FRAME = ("x", "core")
ANY = pl.BlockSpec(memory_space=pl.ANY)


def index_of(sizes, at):
    value = 0
    for name, size in zip(AXES, sizes):
        value = value * size + at[name]
    return value


def swap(sizes, value, choose):
    pairs = []
    for x in range(sizes[0]):
        for core in range(sizes[1]):
            for z in range(sizes[2]):
                for y in range(sizes[3]):
                    at = {"x": x, "core": core, "z": z, "y": y}
                    pairs.append((index_of(sizes, at), index_of(sizes, choose(dict(at)))))
    return lax.ppermute(value, AXES, pairs)


def near_peer(at):
    at["y" if at["core"] else "x"] ^= 1
    return at


def far_peer(at):
    at["x" if at["core"] else "y"] ^= 1
    return at


def line_peer(bits):
    def choose(at):
        at["z"] ^= bits
        return at

    return choose


def core_peer(at):
    at["core"] ^= 1
    return at


def cell(core, x, y, near, far):
    return jnp.where(core == 0, x ^ near, x ^ far), jnp.where(core == 0, y ^ far, y ^ near)


def hold(values, after):
    def body(*refs):
        pass

    return pl.pallas_call(
        body,
        in_specs=[ANY] * (len(values) + len(after)),
        out_specs=[ANY] * len(values),
        out_shape=[jax.ShapeDtypeStruct(value.shape, value.dtype) for value in values],
        input_output_aliases={index: index for index in range(len(values))},
    )(*values, *after)


def copy_after(value, after):
    def body(in_ref, *refs):
        refs[-1][...] = in_ref[...]

    return pl.pallas_call(
        body,
        in_specs=[pl.BlockSpec(memory_space=pltpu.VMEM)] + [ANY] * len(after),
        out_specs=pl.BlockSpec(memory_space=pltpu.VMEM),
        out_shape=jax.ShapeDtypeStruct(value.shape, value.dtype),
    )(value, *after)


def columns_of(vectors, tail):
    rows = tail.shape[0]

    def body(*refs):
        out = refs[-1]
        lines = jnp.concatenate([ref[...].astype(jnp.float32) for ref in refs[:-2]], axis=0)
        lines = jnp.pad(lines, ((0, 0), (0, 128 - rows)))
        turned = jnp.pad(lines, ((0, 128 - lines.shape[0]), (0, 0))).T[:rows]
        out[...] = turned.astype(jnp.bfloat16)
        out[:, len(vectors) : len(vectors) + tail.shape[1]] = refs[-2][...]

    return pl.pallas_call(
        body, out_shape=jax.ShapeDtypeStruct((rows, 128), jnp.bfloat16)
    )(*[v.reshape(1, rows) for v in vectors], tail)


class Gather:
    def __init__(self, sizes, here, shard):
        self.sizes, self.here = sizes, here
        self.parts = [shard] + [swap(sizes, shard, line_peer(bits)) for bits in range(1, sizes[2])]

    def stack(self, after=()):
        parts = self.parts[:1] + list(hold(self.parts[1:], after)) if after else self.parts
        self.pieces = {(0, 0): jnp.stack(parts)}
        return [self.pieces[0, 0]]

    def second(self):
        column = self.pieces[0, 0]
        self.pieces[1, 0] = swap(self.sizes, column, near_peer)
        self.pieces[0, 1] = swap(self.sizes, column, far_peer)
        return [self.pieces[1, 0], self.pieces[0, 1]]

    def third(self, after=()):
        (self.pieces[1, 0],) = hold([self.pieces[1, 0]], [self.pieces[0, 1]] + list(after))
        self.pieces[1, 1] = swap(self.sizes, self.pieces[1, 0], far_peer)
        return [self.pieces[1, 1]]

    def whole(self, lines=0, after=()):
        if after:
            (self.pieces[1, 1],) = hold([self.pieces[1, 1]], after)
        keys = sorted(self.pieces)
        mine = [self.pieces[key] for key in keys]
        theirs = [swap(self.sizes, piece, core_peer) for piece in mine]
        count, rows, width = mine[0].shape
        total = 2 * len(keys)
        devices = self.sizes[0] * self.sizes[1] * self.sizes[2] * self.sizes[3]

        def body(here_ref, *refs):
            out, sems = refs[total], refs[-1]
            copies = []
            for side in range(2):
                core = here_ref[1] ^ side
                for index, (near, far) in enumerate(keys):
                    x, y = cell(core, here_ref[0], here_ref[3], near, far)
                    slot = side * len(keys) + index
                    for bits in range(count):
                        to = out.at[x, core, here_ref[2] ^ bits, y]
                        copies.append(pltpu.make_async_copy(refs[slot].at[bits], to, sems.at[slot * count + bits]))
            for copy in copies:
                copy.start()
            for copy in copies:
                copy.wait()
            if lines:
                tail = out[..., width - 128 :].astype(jnp.float32).reshape(devices * rows, 128)
                refs[total + 1][...] = tail.T[:lines]

        vmem = pl.BlockSpec(memory_space=pltpu.VMEM)
        shapes = [jax.ShapeDtypeStruct((self.sizes[0], 2, count, 2, rows, width), mine[0].dtype)]
        if lines:
            shapes.append(jax.ShapeDtypeStruct((lines, devices * rows), jnp.float32))
        results = pl.pallas_call(
            body,
            in_specs=[pl.BlockSpec(memory_space=pltpu.SMEM)] + [ANY] * total,
            out_specs=[vmem] * len(shapes),
            out_shape=shapes,
            scratch_shapes=[pltpu.SemaphoreType.DMA((total * count,))],
        )(self.here, *mine, *theirs)
        full = results[0].reshape(-1, width)
        return (full, results[1]) if lines else full


class Scatter:
    def __init__(self, sizes, here, sent, kept):
        self.sizes, self.here = sizes, here
        rows = kept.shape[1] // (sizes[2] * 2)
        shape = (sizes[0], sizes[2], 2, rows, kept.shape[2])
        self.kept = kept.reshape(shape)
        self.came = swap(sizes, sent.reshape(shape), core_peer)

    def second(self):
        x_count, count, _, rows, width = self.kept.shape
        block = (1, count, 1, rows, width)

        def body(here_ref, kept_ref, came_ref, sent_ref, own_ref):
            def fill(to_ref):
                for bits in range(count):
                    z = here_ref[2] ^ bits
                    value = kept_ref[0, z, 0].astype(jnp.float32) + came_ref[0, z, 0].astype(jnp.float32)
                    to_ref[0, bits] = value.astype(jnp.bfloat16)

            @pl.when(pl.program_id(0) == 0)
            def _():
                fill(sent_ref)

            @pl.when(pl.program_id(0) == 1)
            def _():
                fill(own_ref)

        def place(phase, far, here_ref):
            x, y = cell(here_ref[1], here_ref[0], here_ref[3], 1 - phase, far)
            return x, 0, y, 0, 0

        spec = pl.BlockSpec(block, place)
        shape = jax.ShapeDtypeStruct((2, count, rows, width), jnp.bfloat16)
        sent, own = pl.pallas_call(
            body,
            grid_spec=pltpu.PrefetchScalarGridSpec(
                num_scalar_prefetch=1,
                grid=(2, 2),
                in_specs=[spec, spec],
                out_specs=[
                    pl.BlockSpec((1, count, rows, width), lambda p, f, h: (jnp.where(p == 0, f, 1), 0, 0, 0)),
                    pl.BlockSpec((1, count, rows, width), lambda p, f, h: (jnp.where(p == 0, 0, f), 0, 0, 0)),
                ],
            ),
            out_shape=[shape, shape],
            cost_estimate=pl.CostEstimate(flops=0, bytes_accessed=6 * self.kept.size, transcendentals=0),
        )(self.here, self.kept, self.came)
        self.kept = own
        self.came = swap(self.sizes, sent, near_peer)
        return [self.came]

    def third(self):
        _, count, rows, width = self.kept.shape
        block = (1, count, rows, width)

        def body(kept_ref, came_ref, sent_ref, own_ref):
            value = kept_ref[0].astype(jnp.float32) + came_ref[0].astype(jnp.float32)
            value = value.astype(jnp.bfloat16)

            @pl.when(pl.program_id(0) == 0)
            def _():
                sent_ref[...] = value

            @pl.when(pl.program_id(0) == 1)
            def _():
                own_ref[...] = value

        spec = pl.BlockSpec(block, lambda i: (1 - i, 0, 0, 0))
        whole = pl.BlockSpec(block[1:], lambda i: (0, 0, 0))
        shape = jax.ShapeDtypeStruct(block[1:], jnp.bfloat16)
        sent, own = pl.pallas_call(
            body,
            grid=(2,),
            in_specs=[spec, spec],
            out_specs=[whole, whole],
            out_shape=[shape, shape],
            cost_estimate=pl.CostEstimate(flops=0, bytes_accessed=6 * self.kept.size, transcendentals=0),
        )(self.kept, self.came)
        self.kept = own
        self.came = swap(self.sizes, sent, far_peer)
        return [self.came]

    def fourth(self):
        value = (self.kept.astype(jnp.float32) + self.came.astype(jnp.float32)).astype(jnp.bfloat16)
        self.parts = [value[0]]
        for bits in range(1, self.sizes[2]):
            self.parts.append(swap(self.sizes, value[bits], line_peer(bits)))
        return self.parts[1:]

    def last(self):
        return sum(part.astype(jnp.float32) for part in self.parts)


ROOT_HALF = 0.7071067811865476
DENSITY = 0.3989422804014327
NT = (((1,), (1,)), ((), ()))
NN = (((1,), (0,)), ((), ()))
TN = (((0,), (0,)), ((), ()))


def dot(left, right, dims=NN):
    return lax.dot_general(left, right, dims, preferred_element_type=jnp.float32)


def normalize(values):
    center = values - jnp.mean(values, axis=-1, keepdims=True)
    spread = jnp.mean(center * center, axis=-1, keepdims=True)
    scale = lax.rsqrt(spread + EPSILON)
    return center * scale, scale


def gelu_parts(u):
    size = jnp.abs(u)
    bell = jnp.exp(-0.5 * (u * u))
    t = 1.0 / (1.0 + (0.3275911 * ROOT_HALF) * size)
    poly = t * (
        0.5 * 0.254829592
        + t * (0.5 * -0.284496736 + t * (0.5 * 1.421413741 + t * (0.5 * -1.453152027 + t * (0.5 * 1.061405429))))
    )
    tail = poly * bell
    value = jnp.maximum(u, 0.0) - size * tail
    slope = jnp.where(u > 0, 1.0 - tail, tail) + DENSITY * (u * bell)
    return value, slope


def add_rows(ref, values):
    total = jnp.sum(values, axis=0, keepdims=True)

    @pl.when(pl.program_id(0) == 0)
    def _():
        ref[...] = total

    @pl.when(pl.program_id(0) != 0)
    def _():
        ref[...] += total


def rows_of(refs):
    return jnp.concatenate([ref[0, : ref.shape[1] - 8] for ref in refs], axis=0)


def tags_of(refs):
    width = refs[0].shape[1] - 8
    rows = width * len(refs)
    column, line = None, None
    for index, ref in enumerate(refs):
        tags = ref[0, width:, :128]
        row = lax.broadcasted_iota(jnp.int32, (rows, 128), 0)
        place = lax.broadcasted_iota(jnp.int32, (rows, 128), 1) + index * width
        chosen = jnp.where(row == place, 1.0, 0.0).astype(jnp.bfloat16)
        one, other = dot(chosen, tags, NT), dot(tags, chosen, NT)
        column = one if column is None else column + one
        line = other if line is None else line + other
    return column[:, :1].astype(jnp.int32), line[:1].astype(jnp.int32)


def spread(refs, rows):
    width = refs[0].shape[1]
    for index, ref in enumerate(refs):
        ref[0] = rows[index * width : (index + 1) * width]


def attend_kernel(x_ref, w_ref, vec_ref, h_ref, qkv_ref, o_ref, p_ref, tag_ref):
    model = x_ref[0].shape[-1]
    head = model // HEADS
    n, _ = normalize(rows_of(x_ref).astype(jnp.float32))
    low = (n * vec_ref[0:1] + vec_ref[1:2]).astype(jnp.bfloat16)
    h_ref[0] = low
    q = dot(low, w_ref[:, :model]) + vec_ref[2:3]
    qkv_ref[0, :, :model] = q.astype(jnp.bfloat16) * jnp.bfloat16(head**-0.5)
    qkv_ref[0, :, model : 2 * model] = dot(low, w_ref[:, model : 2 * model]).astype(jnp.bfloat16)
    v = dot(low, w_ref[:, 2 * model : 3 * model]) + vec_ref[3:4]
    qkv_ref[0, :, 2 * model :] = v.astype(jnp.bfloat16)
    column, line = tags_of(x_ref)
    tag_ref[0] = column
    code = jnp.where(line & 1 == 1, line >> 1, -1)
    bias = jnp.where(column >> 1 == code, 0.0, -1e30)
    for i in range(HEADS):
        at = slice(i * head, (i + 1) * head)
        k_at = slice(model + i * head, model + (i + 1) * head)
        v_at = slice(2 * model + i * head, 2 * model + (i + 1) * head)
        s = dot(qkv_ref[0, :, at], qkv_ref[0, :, k_at], NT) + bias
        e = jnp.exp(s - jnp.max(s, axis=-1, keepdims=True))
        p = (e * (1.0 / jnp.sum(e, axis=-1, keepdims=True))).astype(jnp.bfloat16)
        p_ref[0, i] = p
        o_ref[0, :, at] = dot(p, qkv_ref[0, :, v_at]).astype(jnp.bfloat16)


def project_kernel(x_ref, o_ref, wo_ref, vec_ref, x2_ref, h2_ref):
    x2 = rows_of(x_ref).astype(jnp.float32) + (dot(o_ref[0], wo_ref[...]) + vec_ref[4:5])
    x2_ref[0] = x2
    n, _ = normalize(x2)
    h2_ref[0] = (n * vec_ref[5:6] + vec_ref[6:7]).astype(jnp.bfloat16)


def mlp(here, h2, cot, tags, upper, rest, down_rows, up_bias, after):
    slots, length, model = h2.shape
    rows = slots * length
    steps = upper.shape[0]
    hidden = steps * model
    peers = len(cot)
    share = rest.shape[0] // steps
    chunk = model // peers
    bf, f32 = jnp.bfloat16, jnp.float32

    def body(here_ref, h2_ref, tag_ref, u_ref, d_ref, b_ref, *refs):
        cot_refs = refs[:peers]
        y_ref, gh_ref, gm_ref, ds_ref, dk_ref, us_ref, uk_ref, gub_ref, gdb_ref, y_acc, gh_acc, block = refs[
            peers + len(after) :
        ]
        step = pl.program_id(0)
        core = here_ref[1]

        @pl.when(step == 0)
        def _():
            total = jnp.zeros((1, model), f32)
            for slot in range(slots):
                keep = (tag_ref[slot] & 1).astype(f32)
                gy = keep * jnp.concatenate([ref[slot] for ref in cot_refs], axis=0).astype(f32)
                gm_ref[slot] = gy.astype(bf)
                total += jnp.sum(gy, axis=0, keepdims=True)
            gdb_ref[...] = total

        h2 = h2_ref[...].reshape(rows, model)
        gm = gm_ref[...].reshape(rows, model)
        up, down = u_ref[0], d_ref[...].reshape(model, model)
        value, slope = gelu_parts(dot(h2, up) + b_ref[...])
        a = value.astype(bf)
        y = dot(a, down)
        gu32 = dot(gm, down, NT) * slope
        gu = gu32.astype(bf)
        gub_ref[...] = jnp.sum(gu.astype(f32), axis=0, keepdims=True)
        gh = dot(gu, up, NT)

        @pl.when(step == 0)
        def _():
            y_acc[...] = y
            gh_acc[...] = gh

        @pl.when(step != 0)
        def _():
            y_acc[...] += y
            gh_acc[...] += gh

        g_down = dot(a, gm, TN).astype(bf)

        @pl.when(step < steps // 2)
        def _():
            ds_ref[0] = g_down

        @pl.when(step >= steps // 2)
        def _():
            dk_ref[0] = g_down

        block[...] = dot(h2, gu, TN).astype(bf).reshape(block.shape)
        for x in range(2):
            us_ref[x] = block[2 * x + (1 - core)]
            uk_ref[x] = block[2 * x + core]

        @pl.when(step == steps - 1)
        def _():
            y_ref[...] = y_acc[...].reshape(y_ref.shape)
            gh_ref[...] = gh_acc[...].reshape(gh_ref.shape)

    def at(step, here_ref):
        return 2 * (step % 2) + (here_ref[1] ^ (1 - step // 2))

    full = pl.BlockSpec((slots, length, model), lambda i, h: (0, 0, 0))
    shape = (slots, length, model)
    part = jax.ShapeDtypeStruct((2, model, model), bf)
    side = jax.ShapeDtypeStruct((2, chunk, hidden), bf)
    line = jax.ShapeDtypeStruct((1, model), f32)
    return pl.pallas_call(
        body,
        grid_spec=pltpu.PrefetchScalarGridSpec(
            num_scalar_prefetch=1,
            grid=(steps,),
            in_specs=[
                full,
                pl.BlockSpec(tags.shape, lambda i, h: (0, 0, 0)),
                pl.BlockSpec((1, model, model), lambda i, h: (at(i, h), 0, 0)),
                pl.BlockSpec((share, down_rows, model), lambda i, h: (at(i, h), 0, 0)),
                pl.BlockSpec((1, model), lambda i, h: (0, at(i, h))),
            ]
            + [pl.BlockSpec(cot[0].shape, lambda i, h: (0, 0, 0))] * peers
            + [ANY] * len(after),
            out_specs=[
                full,
                full,
                full,
                pl.BlockSpec((1, model, model), lambda i, h: (jnp.minimum(i, 1), 0, 0)),
                pl.BlockSpec((1, model, model), lambda i, h: (jnp.maximum(i - 2, 0), 0, 0)),
                pl.BlockSpec((2, chunk, model), lambda i, h: (0, 0, at(i, h))),
                pl.BlockSpec((2, chunk, model), lambda i, h: (0, 0, at(i, h))),
                pl.BlockSpec((1, model), lambda i, h: (0, at(i, h))),
                pl.BlockSpec((1, model), lambda i, h: (0, 0)),
            ],
            scratch_shapes=[
                pltpu.VMEM((rows, model), f32),
                pltpu.VMEM((rows, model), f32),
                pltpu.VMEM((4, chunk, model), bf),
            ],
        ),
        out_shape=[
            jax.ShapeDtypeStruct(shape, f32),
            jax.ShapeDtypeStruct(shape, f32),
            jax.ShapeDtypeStruct(shape, bf),
            part, part, side, side,
            jax.ShapeDtypeStruct((1, hidden), f32),
            line,
        ],
        compiler_params=pltpu.CompilerParams(vmem_limit_bytes=58 * 1024 * 1024),
        cost_estimate=pl.CostEstimate(
            flops=12 * rows * model * hidden, bytes_accessed=30 * rows * model, transcendentals=rows * hidden
        ),
    )(here, h2, tags, upper, rest, up_bias, *cot, *after)


def norm_back(grad, n, scale, gain):
    gn = grad * gain
    mean = jnp.mean(gn, axis=-1, keepdims=True)
    cross = jnp.mean(gn * n, axis=-1, keepdims=True)
    return (gn - mean - n * cross) * scale


def middle_kernel(y_ref, gh_ref, wo_ref, x2_ref, gm_ref, tag_ref, vec_ref, out_ref, gx_ref, ga_ref, go_ref, gg_ref, gb_ref, gob_ref):
    x2 = x2_ref[0]
    keep = (tag_ref[0] & 1).astype(jnp.float32)
    spread(out_ref, (keep * (x2 + (y_ref[0] + vec_ref[7:8]))).astype(jnp.bfloat16))
    gh = gh_ref[0]
    n, scale = normalize(x2)
    add_rows(gg_ref, gh * n)
    add_rows(gb_ref, gh)
    gx = gm_ref[0].astype(jnp.float32) + norm_back(gh, n, scale, vec_ref[5:6])
    gx_ref[0] = gx
    low = gx.astype(jnp.bfloat16)
    ga_ref[0] = low
    add_rows(gob_ref, low.astype(jnp.float32))
    go_ref[0] = dot(low, wo_ref[...], NT).astype(jnp.bfloat16)


def attend_back_kernel(qkv_ref, go_ref, p_ref, q_sum_ref, v_sum_ref, g_ref, gqb_ref, gvb_ref):
    model = go_ref.shape[-1]
    head = model // HEADS
    for i in range(HEADS):
        at = slice(i * head, (i + 1) * head)
        k_at = slice(model + i * head, model + (i + 1) * head)
        v_at = slice(2 * model + i * head, 2 * model + (i + 1) * head)
        go = go_ref[0, :, at]
        p = p_ref[0, i]
        dp = dot(go, qkv_ref[0, :, v_at], NT)
        pf = p.astype(jnp.float32)
        delta = jnp.sum(pf * dp, axis=-1, keepdims=True)
        ds = (pf * (dp - delta)).astype(jnp.bfloat16)
        g_ref[0, :, at] = (dot(ds, qkv_ref[0, :, k_at]) * head**-0.5).astype(jnp.bfloat16)
        g_ref[0, :, k_at] = dot(ds, qkv_ref[0, :, at], TN).astype(jnp.bfloat16)
        g_ref[0, :, v_at] = dot(p, go, TN).astype(jnp.bfloat16)
    gqb_ref[...] = q_sum_ref[...] + jnp.sum(g_ref[0, :, :model].astype(jnp.float32), axis=0, keepdims=True)
    gvb_ref[...] = v_sum_ref[...] + jnp.sum(g_ref[0, :, 2 * model :].astype(jnp.float32), axis=0, keepdims=True)


def input_kernel(g_ref, w_ref, x_ref, gx_ref, vec_ref, out_ref, gg_ref, gb_ref):
    model = x_ref[0].shape[-1]
    gh = dot(g_ref[0], w_ref[:, : 3 * model], NT)
    n, scale = normalize(rows_of(x_ref).astype(jnp.float32))
    add_rows(gg_ref, gh * n)
    add_rows(gb_ref, gh)
    grad = gx_ref[0] + norm_back(gh, n, scale, vec_ref[0:1])
    spread(out_ref, grad.astype(jnp.bfloat16))


def call(kernel, inputs, outputs, slots, flops, first=0, carry=None, after=(), limit=56):
    specs = []
    arrays = []
    groups = []

    def slot_spec(shape):
        return pl.BlockSpec((1,) + shape[1:], lambda i, n=len(shape) - 1: (i + first,) + (0,) * n)

    for array, kind in inputs:
        if kind == "frames":
            groups.append(len(array))
            arrays += array
            specs += [slot_spec(piece.shape) for piece in array]
            continue
        groups.append(0)
        arrays.append(array)
        if kind == "slot":
            specs.append(slot_spec(array.shape))
        elif kind == "whole":
            specs.append(pl.BlockSpec(array.shape, lambda i, n=array.ndim: (0,) * n))
        else:
            rows = array.shape[0]
            specs.append(pl.BlockSpec((rows, rows), lambda i, j=kind: (0, j)))
    used = len(arrays)
    extra = list(after)
    shapes = []
    places = []
    aliases = {}
    for output in outputs:
        parts = output if isinstance(output, list) else [output]
        groups.append(len(parts) if isinstance(output, list) else 0)
        for shape, dtype in parts:
            shapes.append(jax.ShapeDtypeStruct(shape, dtype))
            if len(shape) > 2:
                places.append(slot_spec(shape))
                if carry is not None:
                    aliases[used + len(extra)] = len(shapes) - 1
                    extra.append(carry[len(shapes) - 1])
            else:
                places.append(pl.BlockSpec(shape, lambda i: (0, 0)))
    moved = sum(s.size * s.dtype.itemsize for s in arrays + shapes)
    skip = used + len(extra)

    def run(*refs):
        refs = list(refs[:used]) + list(refs[skip:])
        arguments = []
        for size in groups:
            arguments.append(refs[:size] if size else refs[0])
            refs = refs[size or 1 :]
        kernel(*arguments)

    results = pl.pallas_call(
        run,
        grid=(slots,),
        in_specs=specs + [ANY] * len(extra),
        out_specs=places,
        out_shape=shapes,
        input_output_aliases=aliases,
        compiler_params=pltpu.CompilerParams(vmem_limit_bytes=limit * 1024 * 1024),
        cost_estimate=pl.CostEstimate(flops=flops, bytes_accessed=moved, transcendentals=0),
    )(*arrays, *extra)
    final = []
    for output in outputs:
        size = len(output) if isinstance(output, list) else 0
        final.append(list(results[:size]) if size else results[0])
        results = results[size or 1 :]
    return final


def row_grad(here, products, after):
    slots, length, model = products[0][0].shape
    steps = []
    for index, (_, right) in enumerate(products):
        steps += [index] * (right.shape[2] // model)
    starts = [steps.index(index) for index in range(len(products))]
    chunk = model // 4
    used = 2 * len(products)

    def body(here_ref, *refs):
        sent_ref, kept_ref, value_ref = refs[-3:]
        core = here_ref[1]
        step = pl.program_id(0)
        for index in range(len(products)):
            end = starts[index] + steps.count(index)

            @pl.when((step >= starts[index]) & (step < end))
            def _():
                left, right = refs[2 * index], refs[2 * index + 1]
                value = dot(left[...].reshape(-1, model), right[...].reshape(-1, model), TN)
                value_ref[...] = value.astype(jnp.bfloat16).reshape(value_ref.shape)

        for x in range(2):
            sent_ref[x] = value_ref[2 * x + (1 - core)]
            kept_ref[x] = value_ref[2 * x + core]

    specs = []
    for index, (left, right) in enumerate(products):
        most = right.shape[2] // model - 1
        specs.append(pl.BlockSpec((slots, length, model), lambda i, h: (0, 0, 0)))
        specs.append(
            pl.BlockSpec(
                (slots, length, model),
                lambda i, h, s=starts[index], m=most: (0, 0, jnp.clip(i - s, 0, m)),
            )
        )
    shape = jax.ShapeDtypeStruct((2, chunk, len(steps) * model), jnp.bfloat16)
    out = pl.BlockSpec((2, chunk, model), lambda i, h: (0, 0, i))
    return pl.pallas_call(
        body,
        grid_spec=pltpu.PrefetchScalarGridSpec(
            num_scalar_prefetch=1,
            grid=(len(steps),),
            in_specs=specs + [ANY] * len(after),
            out_specs=[out, out],
            scratch_shapes=[pltpu.VMEM((4, chunk, model), jnp.bfloat16)],
        ),
        out_shape=[shape, shape],
        compiler_params=pltpu.CompilerParams(vmem_limit_bytes=56 * 1024 * 1024),
        cost_estimate=pl.CostEstimate(
            flops=2 * slots * length * model * model * len(steps),
            bytes_accessed=2 * sum(r.size for _, r in products),
            transcendentals=0,
        ),
    )(here, *[array for pair in products for array in pair], *after)


def turned(lines, tail, after):
    width = lines[0].shape[1]
    used = len(lines)

    def body(*refs):
        out = refs[-1]
        value = jnp.concatenate([ref[...] for ref in refs[:used]], axis=0)
        value = jnp.pad(value, ((0, 128 - value.shape[0]), (0, 0))).T
        out[...] = value.astype(jnp.bfloat16)
        out[:, used : used + tail.shape[1]] = refs[used][...].astype(jnp.bfloat16)

    vmem = pl.BlockSpec(memory_space=pltpu.VMEM)
    return pl.pallas_call(
        body,
        in_specs=[vmem] * (used + 1) + [ANY] * len(after),
        out_specs=vmem,
        out_shape=jax.ShapeDtypeStruct((width, 128), jnp.bfloat16),
    )(*lines, tail, *after)


def join(here, pieces, dtype):
    slots, width, model = pieces[0].shape
    count = len(pieces)

    def body(here_ref, *refs):
        for step in range(count):

            @pl.when(pl.program_id(0) == step)
            def _():
                refs[-1][...] = refs[step][...].astype(dtype)

    whole = pl.BlockSpec((slots, width, model), lambda i, h: (0, 0, 0))
    return pl.pallas_call(
        body,
        grid_spec=pltpu.PrefetchScalarGridSpec(
            num_scalar_prefetch=1,
            grid=(count,),
            in_specs=[whole] * count,
            out_specs=pl.BlockSpec((slots, width, model), lambda i, h: ((2 * h[0] + h[1]) ^ i, 0, 0)),
        ),
        out_shape=jax.ShapeDtypeStruct((slots * count, width, model), dtype),
    )(here, *pieces)


def row_blocks(down, out, up):
    width = out.shape[1]

    def body(down_ref, out_ref, up_ref, to_ref):
        at = down.shape[0]
        to_ref[:at] = down_ref[...]
        to_ref[at : at + out.shape[0]] = out_ref[...]
        at += out.shape[0]
        for step in range(up.shape[1] // width):
            to_ref[at : at + up.shape[0]] = up_ref[:, step * width : (step + 1) * width]
            at += up.shape[0]

    total = down.shape[0] + out.shape[0] + up.shape[0] * up.shape[1] // width
    return pl.pallas_call(body, out_shape=jax.ShapeDtypeStruct((total, width), down.dtype))(down, out, up)


def body(
    sizes,
    tokens,
    cotangent,
    frame_count,
    image_group,
    keep_mask,
    attn_norm_gain,
    attn_norm_bias,
    w_qkv,
    query_bias,
    value_bias,
    w_out,
    out_bias,
    mlp_norm_gain,
    mlp_norm_bias,
    w_up,
    up_bias,
    w_down,
    down_bias,
):
    bf, f32 = jnp.bfloat16, jnp.float32
    here = jnp.stack([lax.axis_index(name) for name in AXES]).astype(jnp.int32)
    peers = sizes[0] * sizes[1]
    frames_here = image_group.shape[1]
    block_width = keep_mask.shape[1] // frames_here
    frame_index = lax.axis_index(FRAME) * frames_here + jnp.arange(frames_here, dtype=jnp.int32)
    segment = jnp.where(frame_index[None, :] < frame_count[:, None], 0, 1 + image_group)
    tags = jnp.repeat(segment, block_width, axis=1) * 2 + keep_mask

    def frame_peer(bits):
        def choose(at):
            at["x"] ^= bits // 2
            at["core"] ^= bits % 2
            return at

        return choose

    def exchange(pieces):
        return list(pieces[:1]) + [swap(sizes, pieces[bits], frame_peer(bits)) for bits in range(1, peers)]

    def slots_for(value):
        own = value.shape[0] // peers
        frame = lax.axis_index(FRAME)
        return [lax.dynamic_slice_in_dim(value, (frame ^ bits) * own, own, 0) for bits in range(peers)]

    rows, model = w_out.shape
    hidden = w_up.shape[1]
    ratio = hidden // model
    vectors = [
        attn_norm_gain, attn_norm_bias, query_bias, value_bias, out_bias, mlp_norm_gain, mlp_norm_bias, down_bias
    ]
    small = columns_of(vectors, up_bias.reshape(rows, ratio))
    slots = tokens.shape[0] // peers
    length = peers * tokens.shape[1]
    here_rows = slots * length
    framed = [((slots, tokens.shape[1], model), bf)] * peers
    full = (slots, length, model)
    wide = (slots, length, hidden)
    scores = 2 * here_rows * length * model
    each = (1,) * slots

    rest = lax.all_gather(row_blocks(w_down, w_out, w_up), AXES, axis=0, tiled=True)
    rest = rest.reshape(-1, (ratio + 1 + ratio) * rows, model)
    devices = rest.shape[0]
    tags = jnp.pad(tags.astype(bf)[:, None, :], ((0, 0), (0, 7), (0, model - tags.shape[1])))
    x = exchange(slots_for(jnp.concatenate([tokens, tags], axis=1)))
    get_mixed = Gather(sizes, here, jnp.concatenate([w_qkv, small], axis=1))
    get_mixed.stack(x[1:])
    get_mixed.second()
    get_mixed.third()
    mixed, vec = get_mixed.whole(16)
    up_bias_row = vec[8 : 8 + ratio].T.reshape(1, -1)

    attend = (
        attend_kernel,
        [(x, "frames"), (mixed, "whole"), (vec, "whole")],
        [
            (full, bf), ((slots, length, 3 * model), bf), (full, bf), ((slots, HEADS, length, length), bf),
            ((slots, length, 1), jnp.int32),
        ],
    )
    cost = (6 * here_rows * model * model + 8 * scores) // slots
    h1, qkv, o, p, tag_columns = call(*attend, slots, cost * slots)
    cot = exchange(slots_for(copy_after(cotangent, [mixed])))
    w_out_full = rest[:, ratio * rows : (ratio + 1) * rows].reshape(model, model)
    upper = rest[:, (ratio + 1) * rows :].reshape(devices, ratio, rows, model).transpose(1, 0, 2, 3)
    upper = upper.reshape(ratio, model, model)
    x2, h2 = call(
        project_kernel,
        [(x, "frames"), (o, "slot"), (w_out_full, "whole"), (vec, "whole")],
        [(full, f32), (full, bf)],
        slots,
        2 * here_rows * model * model,
    )
    y, gh, gm, down_sent, down_kept, up_sent, up_kept, gub, gdb = mlp(
        here, h2, cot, tag_columns, upper, rest, ratio * rows, up_bias_row, []
    )
    put_down = Scatter(sizes, here, down_sent, down_kept)
    put_up = Scatter(sizes, here, up_sent, up_kept)
    out, gx, ga, go, gmg, gmb, gob = call(
        middle_kernel,
        [(y, "slot"), (gh, "slot"), (w_out_full, "whole"), (x2, "slot"), (gm, "slot"), (tag_columns, "slot"), (vec, "whole")],
        [framed, (full, f32), (full, bf), (full, bf)] + [((1, model), f32)] * 3,
        slots,
        2 * here_rows * model * model,
    )
    (put_down.kept,) = hold([put_down.kept], [go])
    put_down.second()
    (put_up.kept,) = hold([put_up.kept], [put_down.kept])
    put_up.second()
    zero = jnp.zeros((1, model), f32)
    state = [None, zero, zero]
    ready = [put_down.kept, put_up.kept]
    for slot in range(slots):
        state = call(
            attend_back_kernel,
            [(qkv, "slot"), (go, "slot"), (p, "slot"), (state[1], "whole"), (state[2], "whole")],
            [((slots, length, 3 * model), bf)] + [((1, model), f32)] * 2,
            1,
            16 * scores // slots,
            slot,
            state if slot else None,
            ready,
        )
        ready = []
        if slot == 0:
            (put_down.kept,) = hold([put_down.kept], [state[0]])
            put_down.third()
            ready = [put_down.kept]
            out = exchange(hold(out, [state[0]]))
        elif slot == 1:
            put_down.kept, put_up.kept = hold([put_down.kept, put_up.kept], [state[0]])
            put_down.fourth()
            put_up.third()
            ready = [put_down.parts[0], put_up.kept] + out[1:]
    g_mix, gqb, gvb = state
    (put_up.kept,) = hold([put_up.kept], [g_mix])
    put_up.fourth()
    in_grad, gag, gab = call(
        input_kernel,
        [(g_mix, "slot"), (mixed, "whole"), (x, "frames"), (gx, "slot"), (vec, "whole")],
        [framed] + [((1, model), f32)] * 2,
        slots,
        6 * here_rows * model * model,
        after=put_down.parts[1:] + [put_up.parts[0]],
    )
    in_grad = exchange(in_grad)
    put_mixed = Scatter(sizes, here, *row_grad(here, [(h1, g_mix), (o, ga)], [gag]))
    (put_mixed.kept,) = hold([put_mixed.kept], put_up.parts[1:])
    put_mixed.second()
    sums = [gag, gab, gqb, gvb, gob, gmg, gmb, gdb]
    pack = turned(sums, gub.reshape(-1, ratio), [])
    pack = lax.all_to_all(pack.reshape(-1, rows, 128), AXES, 0, 0, tiled=True)
    last = jnp.sum(pack.astype(f32), axis=0)
    put_mixed.third()
    put_mixed.fourth()
    mixed_rows = put_mixed.last()
    g_qkv, g_out = mixed_rows[:, : 3 * model], mixed_rows[:, 3 * model :]
    v = [last[:, i] for i in range(8)]
    return (
        join(here, out, bf), join(here, in_grad, f32), v[0], v[1], g_qkv, v[2], v[3], g_out, v[4], v[5], v[6],
        put_up.last(), last[:, 8 : 8 + ratio].reshape(-1), put_down.last(), v[7],
    )


def solution(mesh):
    frames, clips = mesh.shape["frame"], mesh.shape["clip"]
    sizes = (frames // 2, 2, clips // 2, 2)
    mesh = Mesh(mesh.devices.reshape(sizes), AXES)

    def run(*arguments):
        return body(sizes, *arguments)

    placed = (
        P(("z", "y"), FRAME, None),
        P(("z", "y"), FRAME, None),
        P(("z", "y")),
        P(("z", "y"), FRAME),
        P(("z", "y"), FRAME),
        P(AXES),
        P(AXES),
        P(AXES, None),
        P(AXES),
        P(AXES),
        P(AXES, None),
        P(AXES),
        P(AXES),
        P(AXES),
        P(AXES, None),
        P(AXES),
        P(AXES, None),
        P(AXES),
    )
    return jax.shard_map(
        run,
        mesh=mesh,
        in_specs=placed,
        out_specs=(
            P(("z", "y"), FRAME, None),
            P(("z", "y"), FRAME, None),
            P(AXES),
            P(AXES),
            P(AXES, None),
            P(AXES),
            P(AXES),
            P(AXES, None),
            P(AXES),
            P(AXES),
            P(AXES),
            P(AXES, None),
            P(AXES),
            P(AXES, None),
            P(AXES),
        ),
        check_vma=False,
    )
```

```python
import jax
import jax.numpy as jnp
from jax import lax
from jax.experimental import pallas as pl
from jax.experimental.pallas import tpu as pltpu
from jax.sharding import Mesh
from jax.sharding import PartitionSpec as P

HEADS = 12
EPSILON = 1e-06
AXES = ("x", "core", "z", "y")
FRAME = ("x", "core")
ANY = pl.BlockSpec(memory_space=pl.ANY)


def index_of(sizes, at):
    value = 0
    for name, size in zip(AXES, sizes):
        value = value * size + at[name]
    return value


def swap(sizes, value, choose):
    pairs = []
    for x in range(sizes[0]):
        for core in range(sizes[1]):
            for z in range(sizes[2]):
                for y in range(sizes[3]):
                    at = {"x": x, "core": core, "z": z, "y": y}
                    pairs.append((index_of(sizes, at), index_of(sizes, choose(dict(at)))))
    return lax.ppermute(value, AXES, pairs)


def near_peer(at):
    at["y" if at["core"] else "x"] ^= 1
    return at


def far_peer(at):
    at["x" if at["core"] else "y"] ^= 1
    return at


def line_peer(bits):
    def choose(at):
        at["z"] ^= bits
        return at

    return choose


def core_peer(at):
    at["core"] ^= 1
    return at


def cell(core, x, y, near, far):
    return jnp.where(core == 0, x ^ near, x ^ far), jnp.where(core == 0, y ^ far, y ^ near)


def hold(values, after):
    def body(*refs):
        pass

    return pl.pallas_call(
        body,
        in_specs=[ANY] * (len(values) + len(after)),
        out_specs=[ANY] * len(values),
        out_shape=[jax.ShapeDtypeStruct(value.shape, value.dtype) for value in values],
        input_output_aliases={index: index for index in range(len(values))},
    )(*values, *after)


def copy_after(value, after):
    def body(in_ref, *refs):
        refs[-1][...] = in_ref[...]

    return pl.pallas_call(
        body,
        in_specs=[pl.BlockSpec(memory_space=pltpu.VMEM)] + [ANY] * len(after),
        out_specs=pl.BlockSpec(memory_space=pltpu.VMEM),
        out_shape=jax.ShapeDtypeStruct(value.shape, value.dtype),
    )(value, *after)


def columns_of(vectors, tail):
    rows = tail.shape[0]

    def body(*refs):
        out = refs[-1]
        lines = jnp.concatenate([ref[...].astype(jnp.float32) for ref in refs[:-2]], axis=0)
        lines = jnp.pad(lines, ((0, 0), (0, 128 - rows)))
        turned = jnp.pad(lines, ((0, 128 - lines.shape[0]), (0, 0))).T[:rows]
        out[...] = turned.astype(jnp.bfloat16)
        out[:, len(vectors) : len(vectors) + tail.shape[1]] = refs[-2][...]

    return pl.pallas_call(
        body, out_shape=jax.ShapeDtypeStruct((rows, 128), jnp.bfloat16)
    )(*[v.reshape(1, rows) for v in vectors], tail)


class Gather:
    def __init__(self, sizes, here, shard):
        self.sizes, self.here = sizes, here
        self.parts = [shard] + [swap(sizes, shard, line_peer(bits)) for bits in range(1, sizes[2])]

    def stack(self, after=()):
        parts = self.parts[:1] + list(hold(self.parts[1:], after)) if after else self.parts
        self.pieces = {(0, 0): jnp.stack(parts)}
        return [self.pieces[0, 0]]

    def second(self):
        column = self.pieces[0, 0]
        self.pieces[1, 0] = swap(self.sizes, column, near_peer)
        self.pieces[0, 1] = swap(self.sizes, column, far_peer)
        return [self.pieces[1, 0], self.pieces[0, 1]]

    def third(self, after=()):
        (self.pieces[1, 0],) = hold([self.pieces[1, 0]], [self.pieces[0, 1]] + list(after))
        self.pieces[1, 1] = swap(self.sizes, self.pieces[1, 0], far_peer)
        return [self.pieces[1, 1]]

    def whole(self, lines=0, after=()):
        if after:
            (self.pieces[1, 1],) = hold([self.pieces[1, 1]], after)
        keys = sorted(self.pieces)
        mine = [self.pieces[key] for key in keys]
        theirs = [swap(self.sizes, piece, core_peer) for piece in mine]
        count, rows, width = mine[0].shape
        total = 2 * len(keys)
        devices = self.sizes[0] * self.sizes[1] * self.sizes[2] * self.sizes[3]

        def body(here_ref, *refs):
            out, sems = refs[total], refs[-1]
            copies = []
            for side in range(2):
                core = here_ref[1] ^ side
                for index, (near, far) in enumerate(keys):
                    x, y = cell(core, here_ref[0], here_ref[3], near, far)
                    slot = side * len(keys) + index
                    for bits in range(count):
                        to = out.at[x, core, here_ref[2] ^ bits, y]
                        copies.append(pltpu.make_async_copy(refs[slot].at[bits], to, sems.at[slot * count + bits]))
            for copy in copies:
                copy.start()
            for copy in copies:
                copy.wait()
            if lines:
                tail = out[..., width - 128 :].astype(jnp.float32).reshape(devices * rows, 128)
                refs[total + 1][...] = tail.T[:lines]

        vmem = pl.BlockSpec(memory_space=pltpu.VMEM)
        shapes = [jax.ShapeDtypeStruct((self.sizes[0], 2, count, 2, rows, width), mine[0].dtype)]
        if lines:
            shapes.append(jax.ShapeDtypeStruct((lines, devices * rows), jnp.float32))
        results = pl.pallas_call(
            body,
            in_specs=[pl.BlockSpec(memory_space=pltpu.SMEM)] + [ANY] * total,
            out_specs=[vmem] * len(shapes),
            out_shape=shapes,
            scratch_shapes=[pltpu.SemaphoreType.DMA((total * count,))],
        )(self.here, *mine, *theirs)
        full = results[0].reshape(-1, width)
        return (full, results[1]) if lines else full


class Scatter:
    def __init__(self, sizes, here, sent, kept):
        self.sizes, self.here = sizes, here
        rows = kept.shape[1] // (sizes[2] * 2)
        shape = (sizes[0], sizes[2], 2, rows, kept.shape[2])
        self.terms = [kept.reshape(shape), swap(sizes, sent.reshape(shape), core_peer)]

    def hold(self, after):
        self.terms[0] = hold(self.terms[:1], after)[0]

    def add(self, cells):
        _, count, _, rows, width = self.terms[0].shape
        steps = len(cells)
        used = len(self.terms)
        near, first = cells[0]

        def body(here_ref, *refs):
            for bit in range(2):
                z = (here_ref[2] & 1) ^ bit
                value = refs[0][0, z, 0].astype(jnp.float32) + refs[1][0, z, 0].astype(jnp.float32)
                for ref in refs[2:used]:
                    value += ref[0, bit].astype(jnp.float32)
                refs[used][0, bit] = value.astype(jnp.bfloat16)

        def place(step, pair, here_ref):
            far = first if steps == 1 else step
            x, y = cell(here_ref[1], here_ref[0], here_ref[3], near, far)
            return x, (here_ref[2] >> 1) ^ pair, y, 0, 0

        plain = (1, 2, rows, width)
        specs = [pl.BlockSpec((1, 2, 1, rows, width), place)] * 2
        for term in self.terms[2:]:
            many = term.shape[0] > 1
            specs.append(
                pl.BlockSpec(plain, lambda i, b, h, m=many: ((first if steps == 1 else i) if m else 0, b, 0, 0))
            )
        return pl.pallas_call(
            body,
            grid_spec=pltpu.PrefetchScalarGridSpec(
                num_scalar_prefetch=1,
                grid=(steps, count // 2),
                in_specs=specs,
                out_specs=pl.BlockSpec(plain, lambda i, b, h: (i, b, 0, 0)),
            ),
            out_shape=jax.ShapeDtypeStruct((steps, count, rows, width), jnp.bfloat16),
            cost_estimate=pl.CostEstimate(
                flops=0, bytes_accessed=2 * steps * count * rows * width * (used + 1), transcendentals=0
            ),
        )(self.here, *self.terms)

    def second(self):
        self.sent = self.add([(1, 0), (1, 1)])
        self.terms.append(swap(self.sizes, self.sent, near_peer))

    def third(self):
        self.sent = self.add([(0, 1)])
        self.terms.append(swap(self.sizes, self.sent, far_peer))

    def fourth(self):
        value = self.add([(0, 0)])[0]
        self.sent = value
        self.parts = [value[0]]
        for bits in range(1, self.sizes[2]):
            self.parts.append(swap(self.sizes, value[bits], line_peer(bits)))

    def last(self):
        return sum(part.astype(jnp.float32) for part in self.parts)


ROOT_HALF = 0.7071067811865476
DENSITY = 0.3989422804014327
NT = (((1,), (1,)), ((), ()))
NN = (((1,), (0,)), ((), ()))
TN = (((0,), (0,)), ((), ()))


def dot(left, right, dims=NN):
    return lax.dot_general(left, right, dims, preferred_element_type=jnp.float32)


def normalize(values):
    center = values - jnp.mean(values, axis=-1, keepdims=True)
    spread = jnp.mean(center * center, axis=-1, keepdims=True)
    scale = lax.rsqrt(spread + EPSILON)
    return center * scale, scale


def gelu_parts(u):
    size = jnp.abs(u)
    bell = jnp.exp(-0.5 * (u * u))
    t = 1.0 / (1.0 + (0.3275911 * ROOT_HALF) * size)
    poly = t * (
        0.5 * 0.254829592
        + t * (0.5 * -0.284496736 + t * (0.5 * 1.421413741 + t * (0.5 * -1.453152027 + t * (0.5 * 1.061405429))))
    )
    tail = poly * bell
    value = jnp.maximum(u, 0.0) - size * tail
    slope = jnp.where(u > 0, 1.0 - tail, tail) + DENSITY * (u * bell)
    return value, slope


def add_rows(ref, values):
    total = jnp.sum(values, axis=0, keepdims=True)

    @pl.when(pl.program_id(0) == 0)
    def _():
        ref[...] = total

    @pl.when(pl.program_id(0) != 0)
    def _():
        ref[...] += total


def rows_of(refs):
    return jnp.concatenate([ref[0, : ref.shape[1] - 8] for ref in refs], axis=0)


def tags_of(refs):
    width = refs[0].shape[1] - 8
    rows = width * len(refs)
    column, line = None, None
    for index, ref in enumerate(refs):
        tags = ref[0, width:, :128]
        row = lax.broadcasted_iota(jnp.int32, (rows, 128), 0)
        place = lax.broadcasted_iota(jnp.int32, (rows, 128), 1) + index * width
        chosen = jnp.where(row == place, 1.0, 0.0).astype(jnp.bfloat16)
        one, other = dot(chosen, tags, NT), dot(tags, chosen, NT)
        column = one if column is None else column + one
        line = other if line is None else line + other
    return column[:, :1].astype(jnp.int32), line[:1].astype(jnp.int32)


def spread(refs, rows):
    width = refs[0].shape[1]
    for index, ref in enumerate(refs):
        ref[0] = rows[index * width : (index + 1) * width]


def attend_kernel(x_ref, w_ref, vec_ref, h_ref, qkv_ref, o_ref, p_ref, tag_ref):
    model = x_ref[0].shape[-1]
    head = model // HEADS
    n, _ = normalize(rows_of(x_ref).astype(jnp.float32))
    low = (n * vec_ref[0:1] + vec_ref[1:2]).astype(jnp.bfloat16)
    h_ref[0] = low
    q = dot(low, w_ref[:, :model]) + vec_ref[2:3]
    qkv_ref[0, :, :model] = q.astype(jnp.bfloat16) * jnp.bfloat16(head**-0.5)
    qkv_ref[0, :, model : 2 * model] = dot(low, w_ref[:, model : 2 * model]).astype(jnp.bfloat16)
    v = dot(low, w_ref[:, 2 * model : 3 * model]) + vec_ref[3:4]
    qkv_ref[0, :, 2 * model :] = v.astype(jnp.bfloat16)
    column, line = tags_of(x_ref)
    tag_ref[0] = column
    code = jnp.where(line & 1 == 1, line >> 1, -1)
    bias = jnp.where(column >> 1 == code, 0.0, -1e30)
    for i in range(HEADS):
        at = slice(i * head, (i + 1) * head)
        k_at = slice(model + i * head, model + (i + 1) * head)
        v_at = slice(2 * model + i * head, 2 * model + (i + 1) * head)
        s = dot(qkv_ref[0, :, at], qkv_ref[0, :, k_at], NT) + bias
        e = jnp.exp(s - jnp.max(s, axis=-1, keepdims=True))
        p = (e * (1.0 / jnp.sum(e, axis=-1, keepdims=True))).astype(jnp.bfloat16)
        p_ref[0, i] = p
        o_ref[0, :, at] = dot(p, qkv_ref[0, :, v_at]).astype(jnp.bfloat16)


def project_kernel(x_ref, o_ref, wo_ref, vec_ref, x2_ref, h2_ref):
    x2 = rows_of(x_ref).astype(jnp.float32) + (dot(o_ref[0], wo_ref[...]) + vec_ref[4:5])
    x2_ref[0] = x2
    n, _ = normalize(x2)
    h2_ref[0] = (n * vec_ref[5:6] + vec_ref[6:7]).astype(jnp.bfloat16)


def mlp(here, h2, cot, tags, rest, up_bias, shard):
    slots, length, model = h2.shape
    rows = slots * length
    hidden = up_bias.shape[1]
    steps = hidden // model
    peers = len(cot)
    chunk = model // peers
    bf, f32 = jnp.bfloat16, jnp.float32

    def body(here_ref, h2_ref, tag_ref, u_ref, b_ref, *refs):
        cot_refs = refs[:peers]
        down_refs = refs[peers : peers + steps]
        y_ref, gh_ref, gm_ref, sent_ref, kept_ref, gub_ref, gdb_ref, y_acc, gh_acc, ups, downs, sems = refs[
            peers + steps :
        ]
        step = pl.program_id(0)
        core = here_ref[1]

        @pl.when(step == 0)
        def _():
            total = jnp.zeros((1, model), f32)
            for slot in range(slots):
                keep = (tag_ref[slot] & 1).astype(f32)
                gy = keep * jnp.concatenate([ref[slot] for ref in cot_refs], axis=0).astype(f32)
                gm_ref[slot] = gy.astype(bf)
                total += jnp.sum(gy, axis=0, keepdims=True)
            gdb_ref[...] = total

        h2 = h2_ref[...].reshape(rows, model)
        gm = gm_ref[...].reshape(rows, model)
        up = u_ref[...]
        parts = [ref[...].astype(f32).reshape(-1, 1, shard, model) for ref in down_refs]
        down = jnp.concatenate(parts, axis=1).reshape(model, model).astype(bf)
        value, slope = gelu_parts(dot(h2, up) + b_ref[...])
        a = value.astype(bf)
        y = dot(a, down)
        gu32 = dot(gm, down, NT) * slope
        gu = gu32.astype(bf)
        gub_ref[...] = jnp.sum(gu.astype(f32), axis=0, keepdims=True)
        gh = dot(gu, up, NT)

        @pl.when(step == 0)
        def _():
            y_acc[...] = y
            gh_acc[...] = gh

        @pl.when(step != 0)
        def _():
            y_acc[...] += y
            gh_acc[...] += gh

        g_down = dot(a, gm, TN).reshape(-1, steps, shard, model)
        g_up = dot(h2, gu, TN).astype(bf).reshape(ups.shape)
        up_at = pl.ds(pl.multiple_of(at(step, here_ref) * model, 128), model)

        def up_copies():
            found = []
            for x in range(2):
                found.append(pltpu.make_async_copy(ups.at[2 * x + (1 - core)], sent_ref.at[x, :, up_at], sems.at[2 * x]))
                found.append(pltpu.make_async_copy(ups.at[2 * x + core], kept_ref.at[x, :, up_at], sems.at[2 * x + 1]))
            return found

        def down_copies(to_ref):
            return [
                pltpu.make_async_copy(
                    downs.at[part],
                    to_ref.at[step % 2, :, pl.ds(hidden + part * model, model)],
                    sems.at[4 + part],
                )
                for part in range(steps)
            ]

        @pl.when(step != 0)
        def _():
            for copy in up_copies() + down_copies(kept_ref):
                copy.wait()

        ups[...] = g_up
        for part in range(steps):
            downs[part] = g_down[:, part].reshape(chunk, model).astype(bf)
        for copy in up_copies():
            copy.start()

        @pl.when(step < steps // 2)
        def _():
            for copy in down_copies(sent_ref):
                copy.start()

        @pl.when(step >= steps // 2)
        def _():
            for copy in down_copies(kept_ref):
                copy.start()

        @pl.when(step == steps - 1)
        def _():
            y_ref[...] = y_acc[...].reshape(y_ref.shape)
            gh_ref[...] = gh_acc[...].reshape(gh_ref.shape)
            for copy in up_copies() + down_copies(kept_ref):
                copy.wait()

    def at(step, here_ref):
        return 2 * (step % 2) + (here_ref[1] ^ (1 - step // 2))

    full = pl.BlockSpec((slots, length, model), lambda i, h: (0, 0, 0))
    shape = (slots, length, model)
    side = jax.ShapeDtypeStruct((2, chunk, 2 * hidden), bf)
    line = jax.ShapeDtypeStruct((1, model), f32)
    return pl.pallas_call(
        body,
        grid_spec=pltpu.PrefetchScalarGridSpec(
            num_scalar_prefetch=1,
            grid=(steps,),
            in_specs=[
                full,
                pl.BlockSpec(tags.shape, lambda i, h: (0, 0, 0)),
                pl.BlockSpec((model, model), lambda i, h: (0, 1 + at(i, h))),
                pl.BlockSpec((1, model), lambda i, h: (0, at(i, h))),
            ]
            + [pl.BlockSpec(cot[0].shape, lambda i, h: (0, 0, 0))] * peers
            + [
                pl.BlockSpec((chunk, model), lambda i, h, c=1 + steps + step: (at(i, h), c))
                for step in range(steps)
            ],
            out_specs=[
                full,
                full,
                full,
                ANY,
                ANY,
                pl.BlockSpec((1, model), lambda i, h: (0, at(i, h))),
                pl.BlockSpec((1, model), lambda i, h: (0, 0)),
            ],
            scratch_shapes=[
                pltpu.VMEM((rows, model), f32),
                pltpu.VMEM((rows, model), f32),
                pltpu.VMEM((4, chunk, model), bf),
                pltpu.VMEM((steps, chunk, model), bf),
                pltpu.SemaphoreType.DMA((4 + steps,)),
            ],
        ),
        out_shape=[
            jax.ShapeDtypeStruct(shape, f32),
            jax.ShapeDtypeStruct(shape, f32),
            jax.ShapeDtypeStruct(shape, bf),
            side,
            side,
            jax.ShapeDtypeStruct((1, hidden), f32),
            line,
        ],
        compiler_params=pltpu.CompilerParams(vmem_limit_bytes=58 * 1024 * 1024),
        cost_estimate=pl.CostEstimate(
            flops=12 * rows * model * hidden, bytes_accessed=30 * rows * model, transcendentals=rows * hidden
        ),
    )(here, h2, tags, rest, up_bias, *cot, *([rest] * steps))


def norm_back(grad, n, scale, gain):
    gn = grad * gain
    mean = jnp.mean(gn, axis=-1, keepdims=True)
    cross = jnp.mean(gn * n, axis=-1, keepdims=True)
    return (gn - mean - n * cross) * scale


def middle_kernel(y_ref, gh_ref, wo_ref, x2_ref, gm_ref, tag_ref, vec_ref, out_ref, gx_ref, ga_ref, go_ref, gg_ref, gb_ref, gob_ref):
    x2 = x2_ref[0]
    keep = (tag_ref[0] & 1).astype(jnp.float32)
    spread(out_ref, (keep * (x2 + (y_ref[0] + vec_ref[7:8]))).astype(jnp.bfloat16))
    gh = gh_ref[0]
    n, scale = normalize(x2)
    add_rows(gg_ref, gh * n)
    add_rows(gb_ref, gh)
    gx = gm_ref[0].astype(jnp.float32) + norm_back(gh, n, scale, vec_ref[5:6])
    gx_ref[0] = gx
    low = gx.astype(jnp.bfloat16)
    ga_ref[0] = low
    add_rows(gob_ref, low.astype(jnp.float32))
    go_ref[0] = dot(low, wo_ref[...], NT).astype(jnp.bfloat16)


def attend_back_kernel(qkv_ref, go_ref, p_ref, g_ref, gqb_ref, gvb_ref):
    model = go_ref.shape[-1]
    head = model // HEADS
    for i in range(HEADS):
        at = slice(i * head, (i + 1) * head)
        k_at = slice(model + i * head, model + (i + 1) * head)
        v_at = slice(2 * model + i * head, 2 * model + (i + 1) * head)
        go = go_ref[0, :, at]
        p = p_ref[0, i]
        dp = dot(go, qkv_ref[0, :, v_at], NT)
        pf = p.astype(jnp.float32)
        delta = jnp.sum(pf * dp, axis=-1, keepdims=True)
        ds = (pf * (dp - delta)).astype(jnp.bfloat16)
        g_ref[0, :, at] = (dot(ds, qkv_ref[0, :, k_at]) * head**-0.5).astype(jnp.bfloat16)
        g_ref[0, :, k_at] = dot(ds, qkv_ref[0, :, at], TN).astype(jnp.bfloat16)
        g_ref[0, :, v_at] = dot(p, go, TN).astype(jnp.bfloat16)
    add_rows(gqb_ref, g_ref[0, :, :model].astype(jnp.float32))
    add_rows(gvb_ref, g_ref[0, :, 2 * model :].astype(jnp.float32))


def input_kernel(g_ref, w_ref, x_ref, gx_ref, vec_ref, out_ref, gg_ref, gb_ref):
    model = x_ref[0].shape[-1]
    gh = dot(g_ref[0], w_ref[:, : 3 * model], NT)
    n, scale = normalize(rows_of(x_ref).astype(jnp.float32))
    add_rows(gg_ref, gh * n)
    add_rows(gb_ref, gh)
    grad = gx_ref[0] + norm_back(gh, n, scale, vec_ref[0:1])
    spread(out_ref, grad.astype(jnp.bfloat16))


def call(kernel, inputs, outputs, slots, flops, first=0, carry=None, after=(), limit=56):
    specs = []
    arrays = []
    groups = []

    def slot_spec(shape):
        return pl.BlockSpec((1,) + shape[1:], lambda i, n=len(shape) - 1: (i + first,) + (0,) * n)

    for array, kind in inputs:
        if kind == "frames":
            groups.append(len(array))
            arrays += array
            specs += [slot_spec(piece.shape) for piece in array]
            continue
        groups.append(0)
        arrays.append(array)
        if kind == "slot":
            specs.append(slot_spec(array.shape))
        elif kind == "whole":
            specs.append(pl.BlockSpec(array.shape, lambda i, n=array.ndim: (0,) * n))
        else:
            rows = array.shape[0]
            specs.append(pl.BlockSpec((rows, rows), lambda i, j=kind: (0, j)))
    used = len(arrays)
    extra = list(after)
    shapes = []
    places = []
    aliases = {}
    for output in outputs:
        parts = output if isinstance(output, list) else [output]
        groups.append(len(parts) if isinstance(output, list) else 0)
        for shape, dtype in parts:
            shapes.append(jax.ShapeDtypeStruct(shape, dtype))
            if len(shape) > 2:
                places.append(slot_spec(shape))
                if carry is not None:
                    aliases[used + len(extra)] = len(shapes) - 1
                    extra.append(carry[len(shapes) - 1])
            else:
                places.append(pl.BlockSpec(shape, lambda i: (0, 0)))
    moved = sum(s.size * s.dtype.itemsize for s in arrays + shapes)
    skip = used + len(extra)

    def run(*refs):
        refs = list(refs[:used]) + list(refs[skip:])
        arguments = []
        for size in groups:
            arguments.append(refs[:size] if size else refs[0])
            refs = refs[size or 1 :]
        kernel(*arguments)

    results = pl.pallas_call(
        run,
        grid=(slots,),
        in_specs=specs + [ANY] * len(extra),
        out_specs=places,
        out_shape=shapes,
        input_output_aliases=aliases,
        compiler_params=pltpu.CompilerParams(vmem_limit_bytes=limit * 1024 * 1024),
        cost_estimate=pl.CostEstimate(flops=flops, bytes_accessed=moved, transcendentals=0),
    )(*arrays, *extra)
    final = []
    for output in outputs:
        size = len(output) if isinstance(output, list) else 0
        final.append(list(results[:size]) if size else results[0])
        results = results[size or 1 :]
    return final


def row_grad(here, products, after):
    slots, length, model = products[0][0].shape
    steps = []
    for index, (_, right) in enumerate(products):
        steps += [index] * (right.shape[2] // model)
    starts = [steps.index(index) for index in range(len(products))]
    chunk = model // 4
    used = 2 * len(products)

    def body(here_ref, *refs):
        sent_ref, kept_ref, value_ref = refs[-3:]
        core = here_ref[1]
        step = pl.program_id(0)
        for index in range(len(products)):
            end = starts[index] + steps.count(index)

            @pl.when((step >= starts[index]) & (step < end))
            def _():
                left, right = refs[2 * index], refs[2 * index + 1]
                value = dot(left[...].reshape(-1, model), right[...].reshape(-1, model), TN)
                value_ref[...] = value.astype(jnp.bfloat16).reshape(value_ref.shape)

        for x in range(2):
            sent_ref[x] = value_ref[2 * x + (1 - core)]
            kept_ref[x] = value_ref[2 * x + core]

    specs = []
    for index, (left, right) in enumerate(products):
        most = right.shape[2] // model - 1
        specs.append(pl.BlockSpec((slots, length, model), lambda i, h: (0, 0, 0)))
        specs.append(
            pl.BlockSpec(
                (slots, length, model),
                lambda i, h, s=starts[index], m=most: (0, 0, jnp.clip(i - s, 0, m)),
            )
        )
    shape = jax.ShapeDtypeStruct((2, chunk, len(steps) * model), jnp.bfloat16)
    out = pl.BlockSpec((2, chunk, model), lambda i, h: (0, 0, i))
    return pl.pallas_call(
        body,
        grid_spec=pltpu.PrefetchScalarGridSpec(
            num_scalar_prefetch=1,
            grid=(len(steps),),
            in_specs=specs + [ANY] * len(after),
            out_specs=[out, out],
            scratch_shapes=[pltpu.VMEM((4, chunk, model), jnp.bfloat16)],
        ),
        out_shape=[shape, shape],
        compiler_params=pltpu.CompilerParams(vmem_limit_bytes=56 * 1024 * 1024),
        cost_estimate=pl.CostEstimate(
            flops=2 * slots * length * model * model * len(steps),
            bytes_accessed=2 * sum(r.size for _, r in products),
            transcendentals=0,
        ),
    )(here, *[array for pair in products for array in pair], *after)


def turned(lines, tail, after):
    width = lines[0].shape[1]
    used = len(lines)

    def body(*refs):
        out = refs[-1]
        value = jnp.concatenate([ref[...] for ref in refs[:used]], axis=0)
        value = jnp.pad(value, ((0, 128 - value.shape[0]), (0, 0))).T
        out[...] = value.astype(jnp.bfloat16)
        out[:, used : used + tail.shape[1]] = refs[used][...].astype(jnp.bfloat16)

    vmem = pl.BlockSpec(memory_space=pltpu.VMEM)
    return pl.pallas_call(
        body,
        in_specs=[vmem] * (used + 1) + [ANY] * len(after),
        out_specs=vmem,
        out_shape=jax.ShapeDtypeStruct((width, 128), jnp.bfloat16),
    )(*lines, tail, *after)


def join(here, pieces, dtype):
    slots, width, model = pieces[0].shape
    count = len(pieces)

    def body(here_ref, *refs):
        for step in range(count):

            @pl.when(pl.program_id(0) == step)
            def _():
                refs[-1][...] = refs[step][...].astype(dtype)

    whole = pl.BlockSpec((slots, width, model), lambda i, h: (0, 0, 0))
    return pl.pallas_call(
        body,
        grid_spec=pltpu.PrefetchScalarGridSpec(
            num_scalar_prefetch=1,
            grid=(count,),
            in_specs=[whole] * count,
            out_specs=pl.BlockSpec((slots, width, model), lambda i, h: ((2 * h[0] + h[1]) ^ i, 0, 0)),
        ),
        out_shape=jax.ShapeDtypeStruct((slots * count, width, model), dtype),
    )(here, *pieces)


def side_by_side(out, up, down):
    rows, width = out.shape
    blocks = down.shape[0] // rows

    def body(out_ref, up_ref, down_ref, to_ref):
        to_ref[:, :width] = out_ref[...]
        to_ref[:, width : width + up.shape[1]] = up_ref[...]
        value = down_ref[...].astype(jnp.float32).reshape(blocks, rows, width)
        for step in range(blocks):
            at = width + up.shape[1] + step * width
            to_ref[:, at : at + width] = value[step].astype(down.dtype)

    total = width + up.shape[1] + blocks * width
    return pl.pallas_call(body, out_shape=jax.ShapeDtypeStruct((rows, total), down.dtype))(out, up, down)


def body(
    sizes,
    tokens,
    cotangent,
    frame_count,
    image_group,
    keep_mask,
    attn_norm_gain,
    attn_norm_bias,
    w_qkv,
    query_bias,
    value_bias,
    w_out,
    out_bias,
    mlp_norm_gain,
    mlp_norm_bias,
    w_up,
    up_bias,
    w_down,
    down_bias,
):
    bf, f32 = jnp.bfloat16, jnp.float32
    here = jnp.stack([lax.axis_index(name) for name in AXES]).astype(jnp.int32)
    peers = sizes[0] * sizes[1]
    frames_here = image_group.shape[1]
    block_width = keep_mask.shape[1] // frames_here
    frame_index = lax.axis_index(FRAME) * frames_here + jnp.arange(frames_here, dtype=jnp.int32)
    segment = jnp.where(frame_index[None, :] < frame_count[:, None], 0, 1 + image_group)
    tags = jnp.repeat(segment, block_width, axis=1) * 2 + keep_mask

    def frame_peer(bits):
        def choose(at):
            at["x"] ^= bits // 2
            at["core"] ^= bits % 2
            return at

        return choose

    def exchange(pieces):
        return list(pieces[:1]) + [swap(sizes, pieces[bits], frame_peer(bits)) for bits in range(1, peers)]

    def slots_for(value):
        own = value.shape[0] // peers
        frame = lax.axis_index(FRAME)
        return [lax.dynamic_slice_in_dim(value, (frame ^ bits) * own, own, 0) for bits in range(peers)]

    rows, model = w_out.shape
    hidden = w_up.shape[1]
    ratio = hidden // model
    vectors = [
        attn_norm_gain, attn_norm_bias, query_bias, value_bias, out_bias, mlp_norm_gain, mlp_norm_bias, down_bias
    ]
    small = columns_of(vectors, up_bias.reshape(rows, ratio))
    slots = tokens.shape[0] // peers
    length = peers * tokens.shape[1]
    here_rows = slots * length
    framed = [((slots, tokens.shape[1], model), bf)] * peers
    full = (slots, length, model)
    wide = (slots, length, hidden)
    scores = 2 * here_rows * length * model
    each = (1,) * slots

    rest = lax.all_gather(side_by_side(w_out, w_up, w_down), AXES, axis=0, tiled=True)
    tags = jnp.pad(tags.astype(bf)[:, None, :], ((0, 0), (0, 7), (0, model - tags.shape[1])))
    x = exchange(slots_for(jnp.concatenate([tokens, tags], axis=1)))
    get_mixed = Gather(sizes, here, jnp.concatenate([w_qkv, small], axis=1))
    get_mixed.stack(x[1:])
    get_mixed.second()
    get_mixed.third()
    mixed, vec = get_mixed.whole(16)
    up_bias_row = vec[8 : 8 + ratio].T.reshape(1, -1)

    attend = (
        attend_kernel,
        [(x, "frames"), (mixed, "whole"), (vec, "whole")],
        [
            (full, bf), ((slots, length, 3 * model), bf), (full, bf), ((slots, HEADS, length, length), bf),
            ((slots, length, 1), jnp.int32),
        ],
    )
    cost = (6 * here_rows * model * model + 8 * scores) // slots
    h1, qkv, o, p, tag_columns = call(*attend, slots, cost * slots)
    cot = exchange(slots_for(copy_after(cotangent, [mixed])))
    x2, h2 = call(
        project_kernel,
        [(x, "frames"), (o, "slot"), (rest, 0), (vec, "whole")],
        [(full, f32), (full, bf)],
        slots,
        2 * here_rows * model * model,
    )
    y, gh, gm, sent, kept, gub, gdb = mlp(here, h2, cot, tag_columns, rest, up_bias_row, rows)
    put_rest = Scatter(sizes, here, sent, kept)
    out, gx, ga, go, gmg, gmb, gob = call(
        middle_kernel,
        [(y, "slot"), (gh, "slot"), (rest, 0), (x2, "slot"), (gm, "slot"), (tag_columns, "slot"), (vec, "whole")],
        [framed, (full, f32), (full, bf), (full, bf)] + [((1, model), f32)] * 3,
        slots,
        2 * here_rows * model * model,
    )
    put_rest.hold([go])
    put_rest.second()
    g_mix, gqb, gvb = call(
        attend_back_kernel,
        [(qkv, "slot"), (go, "slot"), (p, "slot")],
        [((slots, length, 3 * model), bf)] + [((1, model), f32)] * 2,
        slots,
        16 * scores,
        after=[put_rest.sent],
    )
    put_rest.hold([g_mix])
    put_rest.third()
    in_grad, gag, gab = call(
        input_kernel,
        [(g_mix, "slot"), (mixed, "whole"), (x, "frames"), (gx, "slot"), (vec, "whole")],
        [framed] + [((1, model), f32)] * 2,
        slots,
        6 * here_rows * model * model,
        after=[put_rest.sent],
    )
    out = exchange(hold(out, [g_mix]))
    in_grad = exchange(in_grad)
    put_rest.hold([gag])
    put_rest.fourth()
    sent, kept = row_grad(here, [(h1, g_mix), (o, ga)], [gag, put_rest.sent] + out[1:])
    put_mixed = Scatter(sizes, here, hold([sent], in_grad[1:])[0], kept)
    put_mixed.second()
    sums = [gag, gab, gqb, gvb, gob, gmg, gmb, gdb]
    pack = turned(sums, gub.reshape(-1, ratio), [])
    pack = lax.all_to_all(pack.reshape(-1, rows, 128), AXES, 0, 0, tiled=True)
    last = jnp.sum(pack.astype(f32), axis=0)
    put_mixed.third()
    put_mixed.hold([pack])
    put_mixed.fourth()
    rest_rows = put_rest.last()
    g_up = rest_rows[:, :hidden]
    g_down = rest_rows[:, hidden:].reshape(rows, ratio, model).transpose(1, 0, 2).reshape(ratio * rows, model)
    mixed_rows = put_mixed.last()
    g_qkv, g_out = mixed_rows[:, : 3 * model], mixed_rows[:, 3 * model :]
    v = [last[:, i] for i in range(8)]
    return (
        join(here, out, bf), join(here, in_grad, f32), v[0], v[1], g_qkv, v[2], v[3], g_out, v[4], v[5], v[6],
        g_up, last[:, 8 : 8 + ratio].reshape(-1), g_down, v[7],
    )


def solution(mesh):
    frames, clips = mesh.shape["frame"], mesh.shape["clip"]
    sizes = (frames // 2, 2, clips // 2, 2)
    mesh = Mesh(mesh.devices.reshape(sizes), AXES)

    def run(*arguments):
        return body(sizes, *arguments)

    placed = (
        P(("z", "y"), FRAME, None),
        P(("z", "y"), FRAME, None),
        P(("z", "y")),
        P(("z", "y"), FRAME),
        P(("z", "y"), FRAME),
        P(AXES),
        P(AXES),
        P(AXES, None),
        P(AXES),
        P(AXES),
        P(AXES, None),
        P(AXES),
        P(AXES),
        P(AXES),
        P(AXES, None),
        P(AXES),
        P(AXES, None),
        P(AXES),
    )
    return jax.shard_map(
        run,
        mesh=mesh,
        in_specs=placed,
        out_specs=(
            P(("z", "y"), FRAME, None),
            P(("z", "y"), FRAME, None),
            P(AXES),
            P(AXES),
            P(AXES, None),
            P(AXES),
            P(AXES),
            P(AXES, None),
            P(AXES),
            P(AXES),
            P(AXES),
            P(AXES, None),
            P(AXES),
            P(AXES, None),
            P(AXES),
        ),
        check_vma=False,
    )
```

```python
import jax
import jax.numpy as jnp
from jax import lax
from jax.experimental import pallas as pl
from jax.experimental.pallas import tpu as pltpu
from jax.sharding import Mesh
from jax.sharding import PartitionSpec as P

HEADS = 12
EPSILON = 1e-06
AXES = ("x", "core", "z", "y")
FRAME = ("x", "core")
ANY = pl.BlockSpec(memory_space=pl.ANY)


def index_of(sizes, at):
    value = 0
    for name, size in zip(AXES, sizes):
        value = value * size + at[name]
    return value


def swap(sizes, value, choose):
    pairs = []
    for x in range(sizes[0]):
        for core in range(sizes[1]):
            for z in range(sizes[2]):
                for y in range(sizes[3]):
                    at = {"x": x, "core": core, "z": z, "y": y}
                    pairs.append((index_of(sizes, at), index_of(sizes, choose(dict(at)))))
    return lax.ppermute(value, AXES, pairs)


def near_peer(at):
    at["y" if at["core"] else "x"] ^= 1
    return at


def far_peer(at):
    at["x" if at["core"] else "y"] ^= 1
    return at


def line_peer(bits):
    def choose(at):
        at["z"] ^= bits
        return at

    return choose


def core_peer(at):
    at["core"] ^= 1
    return at


def cell(core, x, y, near, far):
    return jnp.where(core == 0, x ^ near, x ^ far), jnp.where(core == 0, y ^ far, y ^ near)


def hold(values, after):
    def body(*refs):
        pass

    return pl.pallas_call(
        body,
        in_specs=[ANY] * (len(values) + len(after)),
        out_specs=[ANY] * len(values),
        out_shape=[jax.ShapeDtypeStruct(value.shape, value.dtype) for value in values],
        input_output_aliases={index: index for index in range(len(values))},
    )(*values, *after)


def copy_after(value, after):
    def body(in_ref, *refs):
        refs[-1][...] = in_ref[...]

    return pl.pallas_call(
        body,
        in_specs=[pl.BlockSpec(memory_space=pltpu.VMEM)] + [ANY] * len(after),
        out_specs=pl.BlockSpec(memory_space=pltpu.VMEM),
        out_shape=jax.ShapeDtypeStruct(value.shape, value.dtype),
    )(value, *after)


def columns_of(vectors, tail):
    rows = tail.shape[0]

    def body(*refs):
        out = refs[-1]
        lines = jnp.concatenate([ref[...].astype(jnp.float32) for ref in refs[:-2]], axis=0)
        lines = jnp.pad(lines, ((0, 0), (0, 128 - rows)))
        turned = jnp.pad(lines, ((0, 128 - lines.shape[0]), (0, 0))).T[:rows]
        out[...] = turned.astype(jnp.bfloat16)
        out[:, len(vectors) : len(vectors) + tail.shape[1]] = refs[-2][...]

    return pl.pallas_call(
        body, out_shape=jax.ShapeDtypeStruct((rows, 128), jnp.bfloat16)
    )(*[v.reshape(1, rows) for v in vectors], tail)


class Gather:
    def __init__(self, sizes, here, shard):
        self.sizes, self.here = sizes, here
        self.parts = [shard] + [swap(sizes, shard, line_peer(bits)) for bits in range(1, sizes[2])]

    def stack(self, after=()):
        parts = self.parts[:1] + list(hold(self.parts[1:], after)) if after else self.parts
        self.pieces = {(0, 0): jnp.stack(parts)}
        return [self.pieces[0, 0]]

    def second(self):
        column = self.pieces[0, 0]
        self.pieces[1, 0] = swap(self.sizes, column, near_peer)
        self.pieces[0, 1] = swap(self.sizes, column, far_peer)
        return [self.pieces[1, 0], self.pieces[0, 1]]

    def third(self, after=()):
        (self.pieces[1, 0],) = hold([self.pieces[1, 0]], [self.pieces[0, 1]] + list(after))
        self.pieces[1, 1] = swap(self.sizes, self.pieces[1, 0], far_peer)
        return [self.pieces[1, 1]]

    def whole(self, lines=0, after=()):
        if after:
            (self.pieces[1, 1],) = hold([self.pieces[1, 1]], after)
        keys = sorted(self.pieces)
        mine = [self.pieces[key] for key in keys]
        theirs = [swap(self.sizes, piece, core_peer) for piece in mine]
        count, rows, width = mine[0].shape
        total = 2 * len(keys)
        devices = self.sizes[0] * self.sizes[1] * self.sizes[2] * self.sizes[3]

        def body(here_ref, *refs):
            out, sems = refs[total], refs[-1]
            copies = []
            for side in range(2):
                core = here_ref[1] ^ side
                for index, (near, far) in enumerate(keys):
                    x, y = cell(core, here_ref[0], here_ref[3], near, far)
                    slot = side * len(keys) + index
                    for bits in range(count):
                        to = out.at[x, core, here_ref[2] ^ bits, y]
                        copies.append(pltpu.make_async_copy(refs[slot].at[bits], to, sems.at[slot * count + bits]))
            for copy in copies:
                copy.start()
            for copy in copies:
                copy.wait()
            if lines:
                tail = out[..., width - 128 :].astype(jnp.float32).reshape(devices * rows, 128)
                refs[total + 1][...] = tail.T[:lines]

        vmem = pl.BlockSpec(memory_space=pltpu.VMEM)
        shapes = [jax.ShapeDtypeStruct((self.sizes[0], 2, count, 2, rows, width), mine[0].dtype)]
        if lines:
            shapes.append(jax.ShapeDtypeStruct((lines, devices * rows), jnp.float32))
        results = pl.pallas_call(
            body,
            in_specs=[pl.BlockSpec(memory_space=pltpu.SMEM)] + [ANY] * total,
            out_specs=[vmem] * len(shapes),
            out_shape=shapes,
            scratch_shapes=[pltpu.SemaphoreType.DMA((total * count,))],
        )(self.here, *mine, *theirs)
        full = results[0].reshape(-1, width)
        return (full, results[1]) if lines else full


class Scatter:
    def __init__(self, sizes, here, sent, kept):
        self.sizes, self.here = sizes, here
        rows = kept.shape[1] // (sizes[2] * 2)
        shape = (sizes[0], sizes[2], 2, rows, kept.shape[2])
        self.terms = [kept.reshape(shape), swap(sizes, sent.reshape(shape), core_peer)]

    def hold(self, after):
        self.terms[0] = hold(self.terms[:1], after)[0]

    def add(self, cells):
        _, count, _, rows, width = self.terms[0].shape
        steps = len(cells)
        used = len(self.terms)
        near, first = cells[0]

        def body(here_ref, *refs):
            for bit in range(2):
                z = (here_ref[2] & 1) ^ bit
                value = refs[0][0, z, 0].astype(jnp.float32) + refs[1][0, z, 0].astype(jnp.float32)
                for ref in refs[2:used]:
                    value += ref[0, bit].astype(jnp.float32)
                refs[used][0, bit] = value.astype(jnp.bfloat16)

        def place(step, pair, here_ref):
            far = first if steps == 1 else step
            x, y = cell(here_ref[1], here_ref[0], here_ref[3], near, far)
            return x, (here_ref[2] >> 1) ^ pair, y, 0, 0

        plain = (1, 2, rows, width)
        specs = [pl.BlockSpec((1, 2, 1, rows, width), place)] * 2
        for term in self.terms[2:]:
            many = term.shape[0] > 1
            specs.append(
                pl.BlockSpec(plain, lambda i, b, h, m=many: ((first if steps == 1 else i) if m else 0, b, 0, 0))
            )
        return pl.pallas_call(
            body,
            grid_spec=pltpu.PrefetchScalarGridSpec(
                num_scalar_prefetch=1,
                grid=(steps, count // 2),
                in_specs=specs,
                out_specs=pl.BlockSpec(plain, lambda i, b, h: (i, b, 0, 0)),
            ),
            out_shape=jax.ShapeDtypeStruct((steps, count, rows, width), jnp.bfloat16),
            cost_estimate=pl.CostEstimate(
                flops=0, bytes_accessed=2 * steps * count * rows * width * (used + 1), transcendentals=0
            ),
        )(self.here, *self.terms)

    def second(self):
        self.sent = self.add([(1, 0), (1, 1)])
        self.terms.append(swap(self.sizes, self.sent, near_peer))

    def third(self):
        self.sent = self.add([(0, 1)])
        self.terms.append(swap(self.sizes, self.sent, far_peer))

    def fourth(self):
        value = self.add([(0, 0)])[0]
        self.sent = value
        self.parts = [value[0]]
        for bits in range(1, self.sizes[2]):
            self.parts.append(swap(self.sizes, value[bits], line_peer(bits)))

    def last(self):
        return sum(part.astype(jnp.float32) for part in self.parts)


ROOT_HALF = 0.7071067811865476
DENSITY = 0.3989422804014327
NT = (((1,), (1,)), ((), ()))
NN = (((1,), (0,)), ((), ()))
TN = (((0,), (0,)), ((), ()))


def dot(left, right, dims=NN):
    return lax.dot_general(left, right, dims, preferred_element_type=jnp.float32)


def normalize(values):
    center = values - jnp.mean(values, axis=-1, keepdims=True)
    spread = jnp.mean(center * center, axis=-1, keepdims=True)
    scale = lax.rsqrt(spread + EPSILON)
    return center * scale, scale


def gelu_parts(u):
    size = jnp.abs(u)
    bell = jnp.exp(-0.5 * (u * u))
    t = 1.0 / (1.0 + (0.3275911 * ROOT_HALF) * size)
    poly = t * (
        0.5 * 0.254829592
        + t * (0.5 * -0.284496736 + t * (0.5 * 1.421413741 + t * (0.5 * -1.453152027 + t * (0.5 * 1.061405429))))
    )
    tail = poly * bell
    value = jnp.maximum(u, 0.0) - size * tail
    slope = jnp.where(u > 0, 1.0 - tail, tail) + DENSITY * (u * bell)
    return value, slope


def add_rows(ref, values):
    total = jnp.sum(values, axis=0, keepdims=True)

    @pl.when(pl.program_id(0) == 0)
    def _():
        ref[...] = total

    @pl.when(pl.program_id(0) != 0)
    def _():
        ref[...] += total


def rows_of(refs):
    return jnp.concatenate([ref[0, : ref.shape[1] - 8] for ref in refs], axis=0)


def tags_of(refs):
    width = refs[0].shape[1] - 8
    rows = width * len(refs)
    column, line = None, None
    for index, ref in enumerate(refs):
        tags = ref[0, width:, :128]
        row = lax.broadcasted_iota(jnp.int32, (rows, 128), 0)
        place = lax.broadcasted_iota(jnp.int32, (rows, 128), 1) + index * width
        chosen = jnp.where(row == place, 1.0, 0.0).astype(jnp.bfloat16)
        one, other = dot(chosen, tags, NT), dot(tags, chosen, NT)
        column = one if column is None else column + one
        line = other if line is None else line + other
    return column[:, :1].astype(jnp.int32), line[:1].astype(jnp.int32)


def spread(refs, rows):
    width = refs[0].shape[1]
    for index, ref in enumerate(refs):
        ref[0] = rows[index * width : (index + 1) * width]


def attend_kernel(x_ref, w_ref, vec_ref, h_ref, qkv_ref, o_ref, p_ref, tag_ref):
    model = x_ref[0].shape[-1]
    head = model // HEADS
    n, _ = normalize(rows_of(x_ref).astype(jnp.float32))
    low = (n * vec_ref[0:1] + vec_ref[1:2]).astype(jnp.bfloat16)
    h_ref[0] = low
    q = dot(low, w_ref[:, :model]) + vec_ref[2:3]
    qkv_ref[0, :, :model] = q.astype(jnp.bfloat16) * jnp.bfloat16(head**-0.5)
    qkv_ref[0, :, model : 2 * model] = dot(low, w_ref[:, model : 2 * model]).astype(jnp.bfloat16)
    v = dot(low, w_ref[:, 2 * model : 3 * model]) + vec_ref[3:4]
    qkv_ref[0, :, 2 * model :] = v.astype(jnp.bfloat16)
    column, line = tags_of(x_ref)
    tag_ref[0] = column
    code = jnp.where(line & 1 == 1, line >> 1, -1)
    bias = jnp.where(column >> 1 == code, 0.0, -1e30)
    for i in range(HEADS):
        at = slice(i * head, (i + 1) * head)
        k_at = slice(model + i * head, model + (i + 1) * head)
        v_at = slice(2 * model + i * head, 2 * model + (i + 1) * head)
        s = dot(qkv_ref[0, :, at], qkv_ref[0, :, k_at], NT) + bias
        e = jnp.exp(s - jnp.max(s, axis=-1, keepdims=True))
        p = (e * (1.0 / jnp.sum(e, axis=-1, keepdims=True))).astype(jnp.bfloat16)
        p_ref[0, i] = p
        o_ref[0, :, at] = dot(p, qkv_ref[0, :, v_at]).astype(jnp.bfloat16)


def project_kernel(x_ref, o_ref, wo_ref, vec_ref, x2_ref, h2_ref):
    x2 = rows_of(x_ref).astype(jnp.float32) + (dot(o_ref[0], wo_ref[...]) + vec_ref[4:5])
    x2_ref[0] = x2
    n, _ = normalize(x2)
    h2_ref[0] = (n * vec_ref[5:6] + vec_ref[6:7]).astype(jnp.bfloat16)


def mlp(here, h2, x2, cot, tags, rest, vec, up_bias, shard):
    slots, length, model = h2.shape
    rows = slots * length
    hidden = up_bias.shape[1]
    steps = hidden // model
    peers = len(cot)
    chunk = model // peers
    bf, f32 = jnp.bfloat16, jnp.float32

    def body(here_ref, h2_ref, x2_ref, tag_ref, vec_ref, u_ref, b_ref, *refs):
        cot_refs = refs[:peers]
        down_refs = refs[peers : peers + steps]
        out_refs = refs[peers + steps : 2 * peers + steps]
        gh_ref, gm_ref, sent_ref, kept_ref, gub_ref, gdb_ref, y_acc, gh_acc, ups, downs, sems = refs[
            2 * peers + steps :
        ]
        step = pl.program_id(0)
        core = here_ref[1]

        @pl.when(step == 0)
        def _():
            total = jnp.zeros((1, model), f32)
            for slot in range(slots):
                keep = (tag_ref[slot] & 1).astype(f32)
                gy = keep * jnp.concatenate([ref[slot] for ref in cot_refs], axis=0).astype(f32)
                gm_ref[slot] = gy.astype(bf)
                total += jnp.sum(gy, axis=0, keepdims=True)
            gdb_ref[...] = total

        h2 = h2_ref[...].reshape(rows, model)
        gm = gm_ref[...].reshape(rows, model)
        up = u_ref[...]
        parts = [ref[...].astype(f32).reshape(-1, 1, shard, model) for ref in down_refs]
        down = jnp.concatenate(parts, axis=1).reshape(model, model).astype(bf)
        value, slope = gelu_parts(dot(h2, up) + b_ref[...])
        a = value.astype(bf)
        y = dot(a, down)
        gu32 = dot(gm, down, NT) * slope
        gu = gu32.astype(bf)
        gub_ref[...] = jnp.sum(gu.astype(f32), axis=0, keepdims=True)
        gh = dot(gu, up, NT)

        @pl.when(step == 0)
        def _():
            y_acc[...] = y
            gh_acc[...] = gh

        @pl.when(step != 0)
        def _():
            y_acc[...] += y
            gh_acc[...] += gh

        g_down = dot(a, gm, TN).reshape(-1, steps, shard, model)
        g_up = dot(h2, gu, TN).astype(bf).reshape(ups.shape)
        up_at = pl.ds(pl.multiple_of(at(step, here_ref) * model, 128), model)

        def up_copies():
            found = []
            for x in range(2):
                found.append(pltpu.make_async_copy(ups.at[2 * x + (1 - core)], sent_ref.at[x, :, up_at], sems.at[2 * x]))
                found.append(pltpu.make_async_copy(ups.at[2 * x + core], kept_ref.at[x, :, up_at], sems.at[2 * x + 1]))
            return found

        def down_copies(to_ref):
            return [
                pltpu.make_async_copy(
                    downs.at[part],
                    to_ref.at[step % 2, :, pl.ds(hidden + part * model, model)],
                    sems.at[4 + part],
                )
                for part in range(steps)
            ]

        @pl.when(step != 0)
        def _():
            for copy in up_copies() + down_copies(kept_ref):
                copy.wait()

        ups[...] = g_up
        for part in range(steps):
            downs[part] = g_down[:, part].reshape(chunk, model).astype(bf)
        for copy in up_copies():
            copy.start()

        @pl.when(step < steps // 2)
        def _():
            for copy in down_copies(sent_ref):
                copy.start()

        @pl.when(step >= steps // 2)
        def _():
            for copy in down_copies(kept_ref):
                copy.start()

        @pl.when(step == steps - 1)
        def _():
            width = length // peers
            for slot in range(slots):
                y = y_acc[slot * length : (slot + 1) * length] + vec_ref[7:8]
                keep = (tag_ref[slot] & 1).astype(f32)
                result = (keep * (x2_ref[slot] + y)).astype(bf)
                for index, ref in enumerate(out_refs):
                    ref[slot] = result[index * width : (index + 1) * width]
            gh_ref[...] = gh_acc[...].reshape(gh_ref.shape)
            for copy in up_copies() + down_copies(kept_ref):
                copy.wait()

    def at(step, here_ref):
        return 2 * (step % 2) + (here_ref[1] ^ (1 - step // 2))

    full = pl.BlockSpec((slots, length, model), lambda i, h: (0, 0, 0))
    shape = (slots, length, model)
    side = jax.ShapeDtypeStruct((2, chunk, 2 * hidden), bf)
    line = jax.ShapeDtypeStruct((1, model), f32)
    results = pl.pallas_call(
        body,
        grid_spec=pltpu.PrefetchScalarGridSpec(
            num_scalar_prefetch=1,
            grid=(steps,),
            in_specs=[
                full,
                full,
                pl.BlockSpec(tags.shape, lambda i, h: (0, 0, 0)),
                pl.BlockSpec(vec.shape, lambda i, h: (0, 0)),
                pl.BlockSpec((model, model), lambda i, h: (0, 1 + at(i, h))),
                pl.BlockSpec((1, model), lambda i, h: (0, at(i, h))),
            ]
            + [pl.BlockSpec(cot[0].shape, lambda i, h: (0, 0, 0))] * peers
            + [
                pl.BlockSpec((chunk, model), lambda i, h, c=1 + steps + step: (at(i, h), c))
                for step in range(steps)
            ],
            out_specs=[pl.BlockSpec(cot[0].shape, lambda i, h: (0, 0, 0))] * peers
            + [
                full,
                full,
                ANY,
                ANY,
                pl.BlockSpec((1, model), lambda i, h: (0, at(i, h))),
                pl.BlockSpec((1, model), lambda i, h: (0, 0)),
            ],
            scratch_shapes=[
                pltpu.VMEM((rows, model), f32),
                pltpu.VMEM((rows, model), f32),
                pltpu.VMEM((4, chunk, model), bf),
                pltpu.VMEM((steps, chunk, model), bf),
                pltpu.SemaphoreType.DMA((4 + steps,)),
            ],
        ),
        out_shape=[jax.ShapeDtypeStruct(cot[0].shape, bf)] * peers
        + [
            jax.ShapeDtypeStruct(shape, f32),
            jax.ShapeDtypeStruct(shape, bf),
            side,
            side,
            jax.ShapeDtypeStruct((1, hidden), f32),
            line,
        ],
        compiler_params=pltpu.CompilerParams(vmem_limit_bytes=58 * 1024 * 1024),
        cost_estimate=pl.CostEstimate(
            flops=12 * rows * model * hidden, bytes_accessed=30 * rows * model, transcendentals=rows * hidden
        ),
    )(here, h2, x2, tags, vec, rest, up_bias, *cot, *([rest] * steps))
    return [list(results[:peers])] + list(results[peers:])


def norm_back(grad, n, scale, gain):
    gn = grad * gain
    mean = jnp.mean(gn, axis=-1, keepdims=True)
    cross = jnp.mean(gn * n, axis=-1, keepdims=True)
    return (gn - mean - n * cross) * scale


def middle_kernel(gh_ref, wo_ref, x2_ref, gm_ref, vec_ref, gx_ref, ga_ref, go_ref, gg_ref, gb_ref, gob_ref):
    gh = gh_ref[0]
    n, scale = normalize(x2_ref[0])
    add_rows(gg_ref, gh * n)
    add_rows(gb_ref, gh)
    gx = gm_ref[0].astype(jnp.float32) + norm_back(gh, n, scale, vec_ref[5:6])
    gx_ref[0] = gx
    low = gx.astype(jnp.bfloat16)
    ga_ref[0] = low
    add_rows(gob_ref, low.astype(jnp.float32))
    go_ref[0] = dot(low, wo_ref[...], NT).astype(jnp.bfloat16)


def attend_back_kernel(qkv_ref, go_ref, p_ref, g_ref, gqb_ref, gvb_ref):
    model = go_ref.shape[-1]
    head = model // HEADS
    for i in range(HEADS):
        at = slice(i * head, (i + 1) * head)
        k_at = slice(model + i * head, model + (i + 1) * head)
        v_at = slice(2 * model + i * head, 2 * model + (i + 1) * head)
        go = go_ref[0, :, at]
        p = p_ref[0, i]
        dp = dot(go, qkv_ref[0, :, v_at], NT)
        pf = p.astype(jnp.float32)
        delta = jnp.sum(pf * dp, axis=-1, keepdims=True)
        ds = (pf * (dp - delta)).astype(jnp.bfloat16)
        g_ref[0, :, at] = (dot(ds, qkv_ref[0, :, k_at]) * head**-0.5).astype(jnp.bfloat16)
        g_ref[0, :, k_at] = dot(ds, qkv_ref[0, :, at], TN).astype(jnp.bfloat16)
        g_ref[0, :, v_at] = dot(p, go, TN).astype(jnp.bfloat16)
    add_rows(gqb_ref, g_ref[0, :, :model].astype(jnp.float32))
    add_rows(gvb_ref, g_ref[0, :, 2 * model :].astype(jnp.float32))


def input_kernel(g_ref, w_ref, x_ref, gx_ref, vec_ref, out_ref, gg_ref, gb_ref):
    model = x_ref[0].shape[-1]
    gh = dot(g_ref[0], w_ref[:, : 3 * model], NT)
    n, scale = normalize(rows_of(x_ref).astype(jnp.float32))
    add_rows(gg_ref, gh * n)
    add_rows(gb_ref, gh)
    grad = gx_ref[0] + norm_back(gh, n, scale, vec_ref[0:1])
    spread(out_ref, grad.astype(jnp.bfloat16))


def call(kernel, inputs, outputs, slots, flops, first=0, carry=None, after=(), limit=56):
    specs = []
    arrays = []
    groups = []

    def slot_spec(shape):
        return pl.BlockSpec((1,) + shape[1:], lambda i, n=len(shape) - 1: (i + first,) + (0,) * n)

    for array, kind in inputs:
        if kind == "frames":
            groups.append(len(array))
            arrays += array
            specs += [slot_spec(piece.shape) for piece in array]
            continue
        groups.append(0)
        arrays.append(array)
        if kind == "slot":
            specs.append(slot_spec(array.shape))
        elif kind == "whole":
            specs.append(pl.BlockSpec(array.shape, lambda i, n=array.ndim: (0,) * n))
        else:
            rows = array.shape[0]
            specs.append(pl.BlockSpec((rows, rows), lambda i, j=kind: (0, j)))
    used = len(arrays)
    extra = list(after)
    shapes = []
    places = []
    aliases = {}
    for output in outputs:
        parts = output if isinstance(output, list) else [output]
        groups.append(len(parts) if isinstance(output, list) else 0)
        for shape, dtype in parts:
            shapes.append(jax.ShapeDtypeStruct(shape, dtype))
            if len(shape) > 2:
                places.append(slot_spec(shape))
                if carry is not None:
                    aliases[used + len(extra)] = len(shapes) - 1
                    extra.append(carry[len(shapes) - 1])
            else:
                places.append(pl.BlockSpec(shape, lambda i: (0, 0)))
    moved = sum(s.size * s.dtype.itemsize for s in arrays + shapes)
    skip = used + len(extra)

    def run(*refs):
        refs = list(refs[:used]) + list(refs[skip:])
        arguments = []
        for size in groups:
            arguments.append(refs[:size] if size else refs[0])
            refs = refs[size or 1 :]
        kernel(*arguments)

    results = pl.pallas_call(
        run,
        grid=(slots,),
        in_specs=specs + [ANY] * len(extra),
        out_specs=places,
        out_shape=shapes,
        input_output_aliases=aliases,
        compiler_params=pltpu.CompilerParams(vmem_limit_bytes=limit * 1024 * 1024),
        cost_estimate=pl.CostEstimate(flops=flops, bytes_accessed=moved, transcendentals=0),
    )(*arrays, *extra)
    final = []
    for output in outputs:
        size = len(output) if isinstance(output, list) else 0
        final.append(list(results[:size]) if size else results[0])
        results = results[size or 1 :]
    return final


def row_grad(here, products, after):
    slots, length, model = products[0][0].shape
    steps = []
    for index, (_, right) in enumerate(products):
        steps += [index] * (right.shape[2] // model)
    starts = [steps.index(index) for index in range(len(products))]
    chunk = model // 4
    used = 2 * len(products)

    def body(here_ref, *refs):
        sent_ref, kept_ref, value_ref = refs[-3:]
        core = here_ref[1]
        step = pl.program_id(0)
        for index in range(len(products)):
            end = starts[index] + steps.count(index)

            @pl.when((step >= starts[index]) & (step < end))
            def _():
                left, right = refs[2 * index], refs[2 * index + 1]
                value = dot(left[...].reshape(-1, model), right[...].reshape(-1, model), TN)
                value_ref[...] = value.astype(jnp.bfloat16).reshape(value_ref.shape)

        for x in range(2):
            sent_ref[x] = value_ref[2 * x + (1 - core)]
            kept_ref[x] = value_ref[2 * x + core]

    specs = []
    for index, (left, right) in enumerate(products):
        most = right.shape[2] // model - 1
        specs.append(pl.BlockSpec((slots, length, model), lambda i, h: (0, 0, 0)))
        specs.append(
            pl.BlockSpec(
                (slots, length, model),
                lambda i, h, s=starts[index], m=most: (0, 0, jnp.clip(i - s, 0, m)),
            )
        )
    shape = jax.ShapeDtypeStruct((2, chunk, len(steps) * model), jnp.bfloat16)
    out = pl.BlockSpec((2, chunk, model), lambda i, h: (0, 0, i))
    return pl.pallas_call(
        body,
        grid_spec=pltpu.PrefetchScalarGridSpec(
            num_scalar_prefetch=1,
            grid=(len(steps),),
            in_specs=specs + [ANY] * len(after),
            out_specs=[out, out],
            scratch_shapes=[pltpu.VMEM((4, chunk, model), jnp.bfloat16)],
        ),
        out_shape=[shape, shape],
        compiler_params=pltpu.CompilerParams(vmem_limit_bytes=56 * 1024 * 1024),
        cost_estimate=pl.CostEstimate(
            flops=2 * slots * length * model * model * len(steps),
            bytes_accessed=2 * sum(r.size for _, r in products),
            transcendentals=0,
        ),
    )(here, *[array for pair in products for array in pair], *after)


def turned(lines, tail, after):
    width = lines[0].shape[1]
    used = len(lines)

    def body(*refs):
        out = refs[-1]
        value = jnp.concatenate([ref[...] for ref in refs[:used]], axis=0)
        value = jnp.pad(value, ((0, 128 - value.shape[0]), (0, 0))).T
        out[...] = value.astype(jnp.bfloat16)
        out[:, used : used + tail.shape[1]] = refs[used][...].astype(jnp.bfloat16)

    vmem = pl.BlockSpec(memory_space=pltpu.VMEM)
    return pl.pallas_call(
        body,
        in_specs=[vmem] * (used + 1) + [ANY] * len(after),
        out_specs=vmem,
        out_shape=jax.ShapeDtypeStruct((width, 128), jnp.bfloat16),
    )(*lines, tail, *after)


def join(here, pieces, dtype):
    slots, width, model = pieces[0].shape
    count = len(pieces)

    def body(here_ref, *refs):
        for step in range(count):

            @pl.when(pl.program_id(0) == step)
            def _():
                refs[-1][...] = refs[step][...].astype(dtype)

    whole = pl.BlockSpec((slots, width, model), lambda i, h: (0, 0, 0))
    return pl.pallas_call(
        body,
        grid_spec=pltpu.PrefetchScalarGridSpec(
            num_scalar_prefetch=1,
            grid=(count,),
            in_specs=[whole] * count,
            out_specs=pl.BlockSpec((slots, width, model), lambda i, h: ((2 * h[0] + h[1]) ^ i, 0, 0)),
        ),
        out_shape=jax.ShapeDtypeStruct((slots * count, width, model), dtype),
    )(here, *pieces)


def side_by_side(out, up, down):
    rows, width = out.shape
    blocks = down.shape[0] // rows

    def body(out_ref, up_ref, down_ref, to_ref):
        to_ref[:, :width] = out_ref[...]
        to_ref[:, width : width + up.shape[1]] = up_ref[...]
        value = down_ref[...].astype(jnp.float32).reshape(blocks, rows, width)
        for step in range(blocks):
            at = width + up.shape[1] + step * width
            to_ref[:, at : at + width] = value[step].astype(down.dtype)

    total = width + up.shape[1] + blocks * width
    return pl.pallas_call(body, out_shape=jax.ShapeDtypeStruct((rows, total), down.dtype))(out, up, down)


def body(
    sizes,
    tokens,
    cotangent,
    frame_count,
    image_group,
    keep_mask,
    attn_norm_gain,
    attn_norm_bias,
    w_qkv,
    query_bias,
    value_bias,
    w_out,
    out_bias,
    mlp_norm_gain,
    mlp_norm_bias,
    w_up,
    up_bias,
    w_down,
    down_bias,
):
    bf, f32 = jnp.bfloat16, jnp.float32
    here = jnp.stack([lax.axis_index(name) for name in AXES]).astype(jnp.int32)
    peers = sizes[0] * sizes[1]
    frames_here = image_group.shape[1]
    block_width = keep_mask.shape[1] // frames_here
    frame_index = lax.axis_index(FRAME) * frames_here + jnp.arange(frames_here, dtype=jnp.int32)
    segment = jnp.where(frame_index[None, :] < frame_count[:, None], 0, 1 + image_group)
    tags = jnp.repeat(segment, block_width, axis=1) * 2 + keep_mask

    def frame_peer(bits):
        def choose(at):
            at["x"] ^= bits // 2
            at["core"] ^= bits % 2
            return at

        return choose

    def exchange(pieces):
        return list(pieces[:1]) + [swap(sizes, pieces[bits], frame_peer(bits)) for bits in range(1, len(pieces))]

    def slots_for(value):
        own = value.shape[0] // peers
        frame = lax.axis_index(FRAME)
        return [lax.dynamic_slice_in_dim(value, (frame ^ bits) * own, own, 0) for bits in range(peers)]

    rows, model = w_out.shape
    hidden = w_up.shape[1]
    ratio = hidden // model
    vectors = [
        attn_norm_gain, attn_norm_bias, query_bias, value_bias, out_bias, mlp_norm_gain, mlp_norm_bias, down_bias
    ]
    small = columns_of(vectors, up_bias.reshape(rows, ratio))
    slots = tokens.shape[0] // peers
    length = peers * tokens.shape[1]
    here_rows = slots * length
    framed = [((slots, tokens.shape[1], model), bf)] * peers
    full = (slots, length, model)
    wide = (slots, length, hidden)
    scores = 2 * here_rows * length * model
    each = (1,) * slots

    rest = lax.all_gather(side_by_side(w_out, w_up, w_down), AXES, axis=0, tiled=True)
    tags = jnp.pad(tags.astype(bf)[:, None, :], ((0, 0), (0, 7), (0, model - tags.shape[1])))
    x = exchange(slots_for(jnp.concatenate([tokens, tags], axis=1)))
    get_mixed = Gather(sizes, here, jnp.concatenate([w_qkv, small], axis=1))
    get_mixed.stack(x[1:])
    get_mixed.second()
    get_mixed.third()
    mixed, vec = get_mixed.whole(16)
    up_bias_row = vec[8 : 8 + ratio].T.reshape(1, -1)

    attend = (
        attend_kernel,
        [(x, "frames"), (mixed, "whole"), (vec, "whole")],
        [
            (full, bf), ((slots, length, 3 * model), bf), (full, bf), ((slots, HEADS, length, length), bf),
            ((slots, length, 1), jnp.int32),
        ],
    )
    cost = (6 * here_rows * model * model + 8 * scores) // slots
    h1, qkv, o, p, tag_columns = call(*attend, slots, cost * slots)
    cot = exchange(slots_for(copy_after(cotangent, [mixed])))
    x2, h2 = call(
        project_kernel,
        [(x, "frames"), (o, "slot"), (rest, 0), (vec, "whole")],
        [(full, f32), (full, bf)],
        slots,
        2 * here_rows * model * model,
    )
    out, gh, gm, sent, kept, gub, gdb = mlp(here, h2, x2, cot, tag_columns, rest, vec, up_bias_row, rows)
    put_rest = Scatter(sizes, here, sent, kept)
    gx, ga, go, gmg, gmb, gob = call(
        middle_kernel,
        [(gh, "slot"), (rest, 0), (x2, "slot"), (gm, "slot"), (vec, "whole")],
        [(full, f32), (full, bf), (full, bf)] + [((1, model), f32)] * 3,
        slots,
        2 * here_rows * model * model,
    )
    late = out[3:]
    out = exchange(out[:3])
    put_rest.hold([go] + out[1:])
    put_rest.second()
    g_mix, gqb, gvb = call(
        attend_back_kernel,
        [(qkv, "slot"), (go, "slot"), (p, "slot")],
        [((slots, length, 3 * model), bf)] + [((1, model), f32)] * 2,
        slots,
        16 * scores,
        after=[put_rest.sent],
    )
    put_rest.hold([g_mix])
    put_rest.third()
    out += [swap(sizes, piece, frame_peer(3 + index)) for index, piece in enumerate(hold(late, [g_mix]))]
    sent, kept = row_grad(here, [(h1, g_mix), (o, ga)], [put_rest.sent])
    put_mixed = Scatter(sizes, here, sent, kept)
    in_grad, gag, gab = call(
        input_kernel,
        [(g_mix, "slot"), (mixed, "whole"), (x, "frames"), (gx, "slot"), (vec, "whole")],
        [framed] + [((1, model), f32)] * 2,
        slots,
        6 * here_rows * model * model,
        after=[kept],
    )
    put_mixed.hold([gag])
    put_mixed.second()
    put_rest.hold([put_mixed.sent])
    put_rest.fourth()
    put_mixed.third()
    in_grad = exchange(list(hold(in_grad, [put_mixed.sent])))
    out = list(hold(out, [put_mixed.sent]))
    put_mixed.fourth()
    in_grad = list(hold(in_grad, [put_mixed.sent]))
    sums = [gag, gab, gqb, gvb, gob, gmg, gmb, gdb]
    pack = turned(sums, gub.reshape(-1, ratio), [put_mixed.sent])
    pack = lax.all_to_all(pack.reshape(-1, rows, 128), AXES, 0, 0, tiled=True)
    last = jnp.sum(pack.astype(f32), axis=0)
    rest_rows = put_rest.last()
    g_up = rest_rows[:, :hidden]
    g_down = rest_rows[:, hidden:].reshape(rows, ratio, model).transpose(1, 0, 2).reshape(ratio * rows, model)
    mixed_rows = put_mixed.last()
    g_qkv, g_out = mixed_rows[:, : 3 * model], mixed_rows[:, 3 * model :]
    v = [last[:, i] for i in range(8)]
    return (
        join(here, out, bf), join(here, in_grad, f32), v[0], v[1], g_qkv, v[2], v[3], g_out, v[4], v[5], v[6],
        g_up, last[:, 8 : 8 + ratio].reshape(-1), g_down, v[7],
    )


def solution(mesh):
    frames, clips = mesh.shape["frame"], mesh.shape["clip"]
    sizes = (frames // 2, 2, clips // 2, 2)
    mesh = Mesh(mesh.devices.reshape(sizes), AXES)

    def run(*arguments):
        return body(sizes, *arguments)

    placed = (
        P(("z", "y"), FRAME, None),
        P(("z", "y"), FRAME, None),
        P(("z", "y")),
        P(("z", "y"), FRAME),
        P(("z", "y"), FRAME),
        P(AXES),
        P(AXES),
        P(AXES, None),
        P(AXES),
        P(AXES),
        P(AXES, None),
        P(AXES),
        P(AXES),
        P(AXES),
        P(AXES, None),
        P(AXES),
        P(AXES, None),
        P(AXES),
    )
    return jax.shard_map(
        run,
        mesh=mesh,
        in_specs=placed,
        out_specs=(
            P(("z", "y"), FRAME, None),
            P(("z", "y"), FRAME, None),
            P(AXES),
            P(AXES),
            P(AXES, None),
            P(AXES),
            P(AXES),
            P(AXES, None),
            P(AXES),
            P(AXES),
            P(AXES),
            P(AXES, None),
            P(AXES),
            P(AXES, None),
            P(AXES),
        ),
        check_vma=False,
    )
```

```python
import jax
import jax.numpy as jnp
from jax import lax
from jax.experimental import pallas as pl
from jax.experimental.pallas import tpu as pltpu
from jax.sharding import Mesh
from jax.sharding import PartitionSpec as P

HEADS = 12
EPSILON = 1e-06
AXES = ("x", "core", "z", "y")
FRAME = ("x", "core")
ANY = pl.BlockSpec(memory_space=pl.ANY)


def index_of(sizes, at):
    value = 0
    for name, size in zip(AXES, sizes):
        value = value * size + at[name]
    return value


def swap(sizes, value, choose):
    pairs = []
    for x in range(sizes[0]):
        for core in range(sizes[1]):
            for z in range(sizes[2]):
                for y in range(sizes[3]):
                    at = {"x": x, "core": core, "z": z, "y": y}
                    pairs.append((index_of(sizes, at), index_of(sizes, choose(dict(at)))))
    return lax.ppermute(value, AXES, pairs)


def near_peer(at):
    at["y" if at["core"] else "x"] ^= 1
    return at


def far_peer(at):
    at["x" if at["core"] else "y"] ^= 1
    return at


def line_peer(bits):
    def choose(at):
        at["z"] ^= bits
        return at

    return choose


def core_peer(at):
    at["core"] ^= 1
    return at


def cell(core, x, y, near, far):
    return jnp.where(core == 0, x ^ near, x ^ far), jnp.where(core == 0, y ^ far, y ^ near)


def hold(values, after):
    def body(*refs):
        pass

    return pl.pallas_call(
        body,
        in_specs=[ANY] * (len(values) + len(after)),
        out_specs=[ANY] * len(values),
        out_shape=[jax.ShapeDtypeStruct(value.shape, value.dtype) for value in values],
        input_output_aliases={index: index for index in range(len(values))},
    )(*values, *after)


def copy_after(value, after):
    def body(in_ref, *refs):
        refs[-1][...] = in_ref[...]

    return pl.pallas_call(
        body,
        in_specs=[pl.BlockSpec(memory_space=pltpu.VMEM)] + [ANY] * len(after),
        out_specs=pl.BlockSpec(memory_space=pltpu.VMEM),
        out_shape=jax.ShapeDtypeStruct(value.shape, value.dtype),
    )(value, *after)


def columns_of(vectors, tail):
    rows = tail.shape[0]

    def body(*refs):
        out = refs[-1]
        lines = jnp.concatenate([ref[...].astype(jnp.float32) for ref in refs[:-2]], axis=0)
        lines = jnp.pad(lines, ((0, 0), (0, 128 - rows)))
        turned = jnp.pad(lines, ((0, 128 - lines.shape[0]), (0, 0))).T[:rows]
        out[...] = turned.astype(jnp.bfloat16)
        out[:, len(vectors) : len(vectors) + tail.shape[1]] = refs[-2][...]

    return pl.pallas_call(
        body, out_shape=jax.ShapeDtypeStruct((rows, 128), jnp.bfloat16)
    )(*[v.reshape(1, rows) for v in vectors], tail)


class Gather:
    def __init__(self, sizes, here, shard):
        self.sizes, self.here = sizes, here
        self.parts = [shard] + [swap(sizes, shard, line_peer(bits)) for bits in range(1, sizes[2])]

    def stack(self, after=()):
        parts = self.parts[:1] + list(hold(self.parts[1:], after)) if after else self.parts
        self.pieces = {(0, 0): jnp.stack(parts)}
        return [self.pieces[0, 0]]

    def second(self):
        column = self.pieces[0, 0]
        self.pieces[1, 0] = swap(self.sizes, column, near_peer)
        self.pieces[0, 1] = swap(self.sizes, column, far_peer)
        return [self.pieces[1, 0], self.pieces[0, 1]]

    def third(self, after=()):
        (self.pieces[1, 0],) = hold([self.pieces[1, 0]], [self.pieces[0, 1]] + list(after))
        self.pieces[1, 1] = swap(self.sizes, self.pieces[1, 0], far_peer)
        return [self.pieces[1, 1]]

    def whole(self, lines=0, after=()):
        if after:
            (self.pieces[1, 1],) = hold([self.pieces[1, 1]], after)
        keys = sorted(self.pieces)
        mine = [self.pieces[key] for key in keys]
        theirs = [swap(self.sizes, piece, core_peer) for piece in mine]
        count, rows, width = mine[0].shape
        total = 2 * len(keys)
        devices = self.sizes[0] * self.sizes[1] * self.sizes[2] * self.sizes[3]

        def body(here_ref, *refs):
            out, sems = refs[total], refs[-1]
            copies = []
            for side in range(2):
                core = here_ref[1] ^ side
                for index, (near, far) in enumerate(keys):
                    x, y = cell(core, here_ref[0], here_ref[3], near, far)
                    slot = side * len(keys) + index
                    for bits in range(count):
                        to = out.at[x, core, here_ref[2] ^ bits, y]
                        copies.append(pltpu.make_async_copy(refs[slot].at[bits], to, sems.at[slot * count + bits]))
            for copy in copies:
                copy.start()
            for copy in copies:
                copy.wait()
            if lines:
                tail = out[..., width - 128 :].astype(jnp.float32).reshape(devices * rows, 128)
                refs[total + 1][...] = tail.T[:lines]

        vmem = pl.BlockSpec(memory_space=pltpu.VMEM)
        shapes = [jax.ShapeDtypeStruct((self.sizes[0], 2, count, 2, rows, width), mine[0].dtype)]
        if lines:
            shapes.append(jax.ShapeDtypeStruct((lines, devices * rows), jnp.float32))
        results = pl.pallas_call(
            body,
            in_specs=[pl.BlockSpec(memory_space=pltpu.SMEM)] + [ANY] * total,
            out_specs=[vmem] * len(shapes),
            out_shape=shapes,
            scratch_shapes=[pltpu.SemaphoreType.DMA((total * count,))],
        )(self.here, *mine, *theirs)
        full = results[0].reshape(-1, width)
        return (full, results[1]) if lines else full


class Scatter:
    def __init__(self, sizes, here, sent, kept):
        self.sizes, self.here = sizes, here
        rows = kept.shape[1] // (sizes[2] * 2)
        shape = (sizes[0], sizes[2], 2, rows, kept.shape[2])
        self.terms = [kept.reshape(shape), swap(sizes, sent.reshape(shape), core_peer)]

    def hold(self, after):
        self.terms[0] = hold(self.terms[:1], after)[0]

    def add(self, cells):
        _, count, _, rows, width = self.terms[0].shape
        steps = len(cells)
        used = len(self.terms)
        near, first = cells[0]

        def body(here_ref, *refs):
            for bit in range(2):
                z = (here_ref[2] & 1) ^ bit
                value = refs[0][0, z, 0].astype(jnp.float32) + refs[1][0, z, 0].astype(jnp.float32)
                for ref in refs[2:used]:
                    value += ref[0, bit].astype(jnp.float32)
                refs[used][0, bit] = value.astype(jnp.bfloat16)

        def place(step, pair, here_ref):
            far = first if steps == 1 else step
            x, y = cell(here_ref[1], here_ref[0], here_ref[3], near, far)
            return x, (here_ref[2] >> 1) ^ pair, y, 0, 0

        plain = (1, 2, rows, width)
        specs = [pl.BlockSpec((1, 2, 1, rows, width), place)] * 2
        for term in self.terms[2:]:
            many = term.shape[0] > 1
            specs.append(
                pl.BlockSpec(plain, lambda i, b, h, m=many: ((first if steps == 1 else i) if m else 0, b, 0, 0))
            )
        return pl.pallas_call(
            body,
            grid_spec=pltpu.PrefetchScalarGridSpec(
                num_scalar_prefetch=1,
                grid=(steps, count // 2),
                in_specs=specs,
                out_specs=pl.BlockSpec(plain, lambda i, b, h: (i, b, 0, 0)),
            ),
            out_shape=jax.ShapeDtypeStruct((steps, count, rows, width), jnp.bfloat16),
            cost_estimate=pl.CostEstimate(
                flops=0, bytes_accessed=2 * steps * count * rows * width * (used + 1), transcendentals=0
            ),
        )(self.here, *self.terms)

    def second(self):
        self.sent = self.add([(1, 0), (1, 1)])
        self.terms.append(swap(self.sizes, self.sent, near_peer))

    def third(self):
        self.sent = self.add([(0, 1)])
        self.terms.append(swap(self.sizes, self.sent, far_peer))

    def fourth(self):
        value = self.add([(0, 0)])[0]
        self.sent = value
        self.parts = [value[0]]
        for bits in range(1, self.sizes[2]):
            self.parts.append(swap(self.sizes, value[bits], line_peer(bits)))

    def last(self):
        return sum(part.astype(jnp.float32) for part in self.parts)


ROOT_HALF = 0.7071067811865476
DENSITY = 0.3989422804014327
NT = (((1,), (1,)), ((), ()))
NN = (((1,), (0,)), ((), ()))
TN = (((0,), (0,)), ((), ()))


def dot(left, right, dims=NN):
    return lax.dot_general(left, right, dims, preferred_element_type=jnp.float32)


def normalize(values):
    center = values - jnp.mean(values, axis=-1, keepdims=True)
    spread = jnp.mean(center * center, axis=-1, keepdims=True)
    scale = lax.rsqrt(spread + EPSILON)
    return center * scale, scale


def gelu_parts(u):
    size = jnp.abs(u)
    bell = jnp.exp(-0.5 * (u * u))
    t = 1.0 / (1.0 + (0.3275911 * ROOT_HALF) * size)
    poly = t * (
        0.5 * 0.254829592
        + t * (0.5 * -0.284496736 + t * (0.5 * 1.421413741 + t * (0.5 * -1.453152027 + t * (0.5 * 1.061405429))))
    )
    tail = poly * bell
    value = jnp.maximum(u, 0.0) - size * tail
    slope = jnp.where(u > 0, 1.0 - tail, tail) + DENSITY * (u * bell)
    return value, slope


def add_rows(ref, values):
    total = jnp.sum(values, axis=0, keepdims=True)

    @pl.when(pl.program_id(0) == 0)
    def _():
        ref[...] = total

    @pl.when(pl.program_id(0) != 0)
    def _():
        ref[...] += total


def rows_of(refs):
    return jnp.concatenate([ref[0, : ref.shape[1] - 8] for ref in refs], axis=0)


def tags_of(refs):
    width = refs[0].shape[1] - 8
    rows = width * len(refs)
    column, line = None, None
    for index, ref in enumerate(refs):
        tags = ref[0, width:, :128]
        row = lax.broadcasted_iota(jnp.int32, (rows, 128), 0)
        place = lax.broadcasted_iota(jnp.int32, (rows, 128), 1) + index * width
        chosen = jnp.where(row == place, 1.0, 0.0).astype(jnp.bfloat16)
        one, other = dot(chosen, tags, NT), dot(tags, chosen, NT)
        column = one if column is None else column + one
        line = other if line is None else line + other
    return column[:, :1].astype(jnp.int32), line[:1].astype(jnp.int32)


def spread(refs, rows):
    width = refs[0].shape[1]
    for index, ref in enumerate(refs):
        ref[0] = rows[index * width : (index + 1) * width]


def attend_kernel(x_ref, w_ref, vec_ref, h_ref, qkv_ref, o_ref, p_ref, tag_ref):
    model = x_ref[0].shape[-1]
    head = model // HEADS
    n, _ = normalize(rows_of(x_ref).astype(jnp.float32))
    low = (n * vec_ref[0:1] + vec_ref[1:2]).astype(jnp.bfloat16)
    h_ref[0] = low
    q = dot(low, w_ref[:, :model]) + vec_ref[2:3]
    qkv_ref[0, :, :model] = q.astype(jnp.bfloat16) * jnp.bfloat16(head**-0.5)
    qkv_ref[0, :, model : 2 * model] = dot(low, w_ref[:, model : 2 * model]).astype(jnp.bfloat16)
    v = dot(low, w_ref[:, 2 * model : 3 * model]) + vec_ref[3:4]
    qkv_ref[0, :, 2 * model :] = v.astype(jnp.bfloat16)
    column, line = tags_of(x_ref)
    tag_ref[0] = column
    code = jnp.where(line & 1 == 1, line >> 1, -1)
    bias = jnp.where(column >> 1 == code, 0.0, -1e30)
    for i in range(HEADS):
        at = slice(i * head, (i + 1) * head)
        k_at = slice(model + i * head, model + (i + 1) * head)
        v_at = slice(2 * model + i * head, 2 * model + (i + 1) * head)
        s = dot(qkv_ref[0, :, at], qkv_ref[0, :, k_at], NT) + bias
        e = jnp.exp(s - jnp.max(s, axis=-1, keepdims=True))
        p = (e * (1.0 / jnp.sum(e, axis=-1, keepdims=True))).astype(jnp.bfloat16)
        p_ref[0, i] = p
        o_ref[0, :, at] = dot(p, qkv_ref[0, :, v_at]).astype(jnp.bfloat16)


def project_kernel(x_ref, o_ref, wo_ref, vec_ref, x2_ref, h2_ref):
    x2 = rows_of(x_ref).astype(jnp.float32) + (dot(o_ref[0], wo_ref[...]) + vec_ref[4:5])
    x2_ref[0] = x2
    n, _ = normalize(x2)
    h2_ref[0] = (n * vec_ref[5:6] + vec_ref[6:7]).astype(jnp.bfloat16)


def mlp(here, h2, x2, cot, tags, rest, vec, up_bias, shard):
    slots, length, model = h2.shape
    rows = slots * length
    hidden = up_bias.shape[1]
    steps = hidden // model
    peers = len(cot)
    chunk = model // peers
    bf, f32 = jnp.bfloat16, jnp.float32

    def body(here_ref, h2_ref, x2_ref, tag_ref, vec_ref, u_ref, b_ref, *refs):
        cot_refs = refs[:peers]
        down_refs = refs[peers : peers + steps]
        out_refs = refs[peers + steps : 2 * peers + steps]
        gh_ref, gm_ref, sent_ref, kept_ref, gub_ref, gdb_ref, y_acc, gh_acc, ups, downs, sems = refs[
            2 * peers + steps :
        ]
        step = pl.program_id(0)
        core = here_ref[1]

        @pl.when(step == 0)
        def _():
            total = jnp.zeros((1, model), f32)
            for slot in range(slots):
                keep = (tag_ref[slot] & 1).astype(f32)
                gy = keep * jnp.concatenate([ref[slot] for ref in cot_refs], axis=0).astype(f32)
                gm_ref[slot] = gy.astype(bf)
                total += jnp.sum(gy, axis=0, keepdims=True)
            gdb_ref[...] = total

        h2 = h2_ref[...].reshape(rows, model)
        gm = gm_ref[...].reshape(rows, model)
        up = u_ref[...]
        parts = [ref[...].astype(f32).reshape(-1, 1, shard, model) for ref in down_refs]
        down = jnp.concatenate(parts, axis=1).reshape(model, model).astype(bf)
        value, slope = gelu_parts(dot(h2, up) + b_ref[...])
        a = value.astype(bf)
        y = dot(a, down)
        gu32 = dot(gm, down, NT) * slope
        gu = gu32.astype(bf)
        gub_ref[...] = jnp.sum(gu.astype(f32), axis=0, keepdims=True)
        gh = dot(gu, up, NT)

        @pl.when(step == 0)
        def _():
            y_acc[...] = y
            gh_acc[...] = gh

        @pl.when(step != 0)
        def _():
            y_acc[...] += y
            gh_acc[...] += gh

        g_down = dot(a, gm, TN).reshape(-1, steps, shard, model)
        g_up = dot(h2, gu, TN).astype(bf).reshape(ups.shape)
        up_at = pl.ds(pl.multiple_of(at(step, here_ref) * model, 128), model)

        def up_copies():
            found = []
            for x in range(2):
                found.append(pltpu.make_async_copy(ups.at[2 * x + (1 - core)], sent_ref.at[x, :, up_at], sems.at[2 * x]))
                found.append(pltpu.make_async_copy(ups.at[2 * x + core], kept_ref.at[x, :, up_at], sems.at[2 * x + 1]))
            return found

        def down_copies(to_ref):
            return [
                pltpu.make_async_copy(
                    downs.at[part],
                    to_ref.at[step % 2, :, pl.ds(hidden + part * model, model)],
                    sems.at[4 + part],
                )
                for part in range(steps)
            ]

        @pl.when(step != 0)
        def _():
            for copy in up_copies() + down_copies(kept_ref):
                copy.wait()

        ups[...] = g_up
        for part in range(steps):
            downs[part] = g_down[:, part].reshape(chunk, model).astype(bf)
        for copy in up_copies():
            copy.start()

        @pl.when(step < steps // 2)
        def _():
            for copy in down_copies(sent_ref):
                copy.start()

        @pl.when(step >= steps // 2)
        def _():
            for copy in down_copies(kept_ref):
                copy.start()

        @pl.when(step == steps - 1)
        def _():
            width = length // peers
            for slot in range(slots):
                y = y_acc[slot * length : (slot + 1) * length] + vec_ref[7:8]
                keep = (tag_ref[slot] & 1).astype(f32)
                result = (keep * (x2_ref[slot] + y)).astype(bf)
                for index, ref in enumerate(out_refs):
                    ref[slot] = result[index * width : (index + 1) * width]
            gh_ref[...] = gh_acc[...].reshape(gh_ref.shape)
            for copy in up_copies() + down_copies(kept_ref):
                copy.wait()

    def at(step, here_ref):
        return 2 * (step % 2) + (here_ref[1] ^ (1 - step // 2))

    full = pl.BlockSpec((slots, length, model), lambda i, h: (0, 0, 0))
    shape = (slots, length, model)
    side = jax.ShapeDtypeStruct((2, chunk, 2 * hidden), bf)
    line = jax.ShapeDtypeStruct((1, model), f32)
    results = pl.pallas_call(
        body,
        grid_spec=pltpu.PrefetchScalarGridSpec(
            num_scalar_prefetch=1,
            grid=(steps,),
            in_specs=[
                full,
                full,
                pl.BlockSpec(tags.shape, lambda i, h: (0, 0, 0)),
                pl.BlockSpec(vec.shape, lambda i, h: (0, 0)),
                pl.BlockSpec((model, model), lambda i, h: (0, 1 + at(i, h))),
                pl.BlockSpec((1, model), lambda i, h: (0, at(i, h))),
            ]
            + [pl.BlockSpec(cot[0].shape, lambda i, h: (0, 0, 0))] * peers
            + [
                pl.BlockSpec((chunk, model), lambda i, h, c=1 + steps + step: (at(i, h), c))
                for step in range(steps)
            ],
            out_specs=[pl.BlockSpec(cot[0].shape, lambda i, h: (0, 0, 0))] * peers
            + [
                full,
                full,
                ANY,
                ANY,
                pl.BlockSpec((1, model), lambda i, h: (0, at(i, h))),
                pl.BlockSpec((1, model), lambda i, h: (0, 0)),
            ],
            scratch_shapes=[
                pltpu.VMEM((rows, model), f32),
                pltpu.VMEM((rows, model), f32),
                pltpu.VMEM((4, chunk, model), bf),
                pltpu.VMEM((steps, chunk, model), bf),
                pltpu.SemaphoreType.DMA((4 + steps,)),
            ],
        ),
        out_shape=[jax.ShapeDtypeStruct(cot[0].shape, bf)] * peers
        + [
            jax.ShapeDtypeStruct(shape, f32),
            jax.ShapeDtypeStruct(shape, bf),
            side,
            side,
            jax.ShapeDtypeStruct((1, hidden), f32),
            line,
        ],
        compiler_params=pltpu.CompilerParams(vmem_limit_bytes=58 * 1024 * 1024),
        cost_estimate=pl.CostEstimate(
            flops=12 * rows * model * hidden, bytes_accessed=30 * rows * model, transcendentals=rows * hidden
        ),
    )(here, h2, x2, tags, vec, rest, up_bias, *cot, *([rest] * steps))
    return [list(results[:peers])] + list(results[peers:])


def norm_back(grad, n, scale, gain):
    gn = grad * gain
    mean = jnp.mean(gn, axis=-1, keepdims=True)
    cross = jnp.mean(gn * n, axis=-1, keepdims=True)
    return (gn - mean - n * cross) * scale


def middle_kernel(gh_ref, wo_ref, x2_ref, gm_ref, vec_ref, gx_ref, ga_ref, go_ref, gg_ref, gb_ref, gob_ref):
    gh = gh_ref[0]
    n, scale = normalize(x2_ref[0])
    add_rows(gg_ref, gh * n)
    add_rows(gb_ref, gh)
    gx = gm_ref[0].astype(jnp.float32) + norm_back(gh, n, scale, vec_ref[5:6])
    gx_ref[0] = gx
    low = gx.astype(jnp.bfloat16)
    ga_ref[0] = low
    add_rows(gob_ref, low.astype(jnp.float32))
    go_ref[0] = dot(low, wo_ref[...], NT).astype(jnp.bfloat16)


def attend_back_kernel(qkv_ref, go_ref, p_ref, o_ref, g_ref, gqb_ref, gvb_ref):
    model = go_ref.shape[-1]
    head = model // HEADS
    turned_go = go_ref[0].T
    turned_q = qkv_ref[0, :, :model].T
    for i in range(HEADS):
        at = slice(i * head, (i + 1) * head)
        k_at = slice(model + i * head, model + (i + 1) * head)
        v_at = slice(2 * model + i * head, 2 * model + (i + 1) * head)
        go = go_ref[0, :, at]
        p = p_ref[0, i]
        dp = dot(go, qkv_ref[0, :, v_at], NT)
        delta = jnp.sum(go.astype(jnp.float32) * o_ref[0, :, at].astype(jnp.float32), axis=-1, keepdims=True)
        ds = (p.astype(jnp.float32) * (dp - delta)).astype(jnp.bfloat16)
        g_ref[0, :, at] = (dot(ds, qkv_ref[0, :, k_at]) * head**-0.5).astype(jnp.bfloat16)
        g_ref[0, :, k_at] = dot(turned_q[at], ds).T.astype(jnp.bfloat16)
        g_ref[0, :, v_at] = dot(turned_go[at], p).T.astype(jnp.bfloat16)
    add_rows(gqb_ref, g_ref[0, :, :model].astype(jnp.float32))
    add_rows(gvb_ref, g_ref[0, :, 2 * model :].astype(jnp.float32))


def input_kernel(g_ref, w_ref, x_ref, gx_ref, vec_ref, out_ref, gg_ref, gb_ref):
    model = x_ref[0].shape[-1]
    gh = dot(g_ref[0], w_ref[:, : 3 * model], NT)
    n, scale = normalize(rows_of(x_ref).astype(jnp.float32))
    add_rows(gg_ref, gh * n)
    add_rows(gb_ref, gh)
    grad = gx_ref[0] + norm_back(gh, n, scale, vec_ref[0:1])
    spread(out_ref, grad.astype(jnp.bfloat16))


def call(kernel, inputs, outputs, slots, flops, first=0, carry=None, after=(), limit=56):
    specs = []
    arrays = []
    groups = []

    def slot_spec(shape):
        return pl.BlockSpec((1,) + shape[1:], lambda i, n=len(shape) - 1: (i + first,) + (0,) * n)

    for array, kind in inputs:
        if kind == "frames":
            groups.append(len(array))
            arrays += array
            specs += [slot_spec(piece.shape) for piece in array]
            continue
        groups.append(0)
        arrays.append(array)
        if kind == "slot":
            specs.append(slot_spec(array.shape))
        elif kind == "whole":
            specs.append(pl.BlockSpec(array.shape, lambda i, n=array.ndim: (0,) * n))
        else:
            rows = array.shape[0]
            specs.append(pl.BlockSpec((rows, rows), lambda i, j=kind: (0, j)))
    used = len(arrays)
    extra = list(after)
    shapes = []
    places = []
    aliases = {}
    for output in outputs:
        parts = output if isinstance(output, list) else [output]
        groups.append(len(parts) if isinstance(output, list) else 0)
        for shape, dtype in parts:
            shapes.append(jax.ShapeDtypeStruct(shape, dtype))
            if len(shape) > 2:
                places.append(slot_spec(shape))
                if carry is not None:
                    aliases[used + len(extra)] = len(shapes) - 1
                    extra.append(carry[len(shapes) - 1])
            else:
                places.append(pl.BlockSpec(shape, lambda i: (0, 0)))
    moved = sum(s.size * s.dtype.itemsize for s in arrays + shapes)
    skip = used + len(extra)

    def run(*refs):
        refs = list(refs[:used]) + list(refs[skip:])
        arguments = []
        for size in groups:
            arguments.append(refs[:size] if size else refs[0])
            refs = refs[size or 1 :]
        kernel(*arguments)

    results = pl.pallas_call(
        run,
        grid=(slots,),
        in_specs=specs + [ANY] * len(extra),
        out_specs=places,
        out_shape=shapes,
        input_output_aliases=aliases,
        compiler_params=pltpu.CompilerParams(vmem_limit_bytes=limit * 1024 * 1024),
        cost_estimate=pl.CostEstimate(flops=flops, bytes_accessed=moved, transcendentals=0),
    )(*arrays, *extra)
    final = []
    for output in outputs:
        size = len(output) if isinstance(output, list) else 0
        final.append(list(results[:size]) if size else results[0])
        results = results[size or 1 :]
    return final


def row_grad(here, products, after):
    slots, length, model = products[0][0].shape
    steps = []
    for index, (_, right) in enumerate(products):
        steps += [index] * (right.shape[2] // model)
    starts = [steps.index(index) for index in range(len(products))]
    chunk = model // 4
    used = 2 * len(products)

    def body(here_ref, *refs):
        sent_ref, kept_ref, value_ref = refs[-3:]
        core = here_ref[1]
        step = pl.program_id(0)
        for index in range(len(products)):
            end = starts[index] + steps.count(index)

            @pl.when((step >= starts[index]) & (step < end))
            def _():
                left, right = refs[2 * index], refs[2 * index + 1]
                value = dot(left[...].reshape(-1, model), right[...].reshape(-1, model), TN)
                value_ref[...] = value.astype(jnp.bfloat16).reshape(value_ref.shape)

        for x in range(2):
            sent_ref[x] = value_ref[2 * x + (1 - core)]
            kept_ref[x] = value_ref[2 * x + core]

    specs = []
    for index, (left, right) in enumerate(products):
        most = right.shape[2] // model - 1
        specs.append(pl.BlockSpec((slots, length, model), lambda i, h: (0, 0, 0)))
        specs.append(
            pl.BlockSpec(
                (slots, length, model),
                lambda i, h, s=starts[index], m=most: (0, 0, jnp.clip(i - s, 0, m)),
            )
        )
    shape = jax.ShapeDtypeStruct((2, chunk, len(steps) * model), jnp.bfloat16)
    out = pl.BlockSpec((2, chunk, model), lambda i, h: (0, 0, i))
    return pl.pallas_call(
        body,
        grid_spec=pltpu.PrefetchScalarGridSpec(
            num_scalar_prefetch=1,
            grid=(len(steps),),
            in_specs=specs + [ANY] * len(after),
            out_specs=[out, out],
            scratch_shapes=[pltpu.VMEM((4, chunk, model), jnp.bfloat16)],
        ),
        out_shape=[shape, shape],
        compiler_params=pltpu.CompilerParams(vmem_limit_bytes=56 * 1024 * 1024),
        cost_estimate=pl.CostEstimate(
            flops=2 * slots * length * model * model * len(steps),
            bytes_accessed=2 * sum(r.size for _, r in products),
            transcendentals=0,
        ),
    )(here, *[array for pair in products for array in pair], *after)


def turned(lines, tail, after):
    width = lines[0].shape[1]
    used = len(lines)

    def body(*refs):
        out = refs[-1]
        value = jnp.concatenate([ref[...] for ref in refs[:used]], axis=0)
        value = jnp.pad(value, ((0, 128 - value.shape[0]), (0, 0))).T
        out[...] = value.astype(jnp.bfloat16)
        out[:, used : used + tail.shape[1]] = refs[used][...].astype(jnp.bfloat16)

    vmem = pl.BlockSpec(memory_space=pltpu.VMEM)
    return pl.pallas_call(
        body,
        in_specs=[vmem] * (used + 1) + [ANY] * len(after),
        out_specs=vmem,
        out_shape=jax.ShapeDtypeStruct((width, 128), jnp.bfloat16),
    )(*lines, tail, *after)


def join(here, pieces, dtype):
    slots, width, model = pieces[0].shape
    count = len(pieces)

    def body(here_ref, *refs):
        for step in range(count):

            @pl.when(pl.program_id(0) == step)
            def _():
                refs[-1][...] = refs[step][...].astype(dtype)

    whole = pl.BlockSpec((slots, width, model), lambda i, h: (0, 0, 0))
    return pl.pallas_call(
        body,
        grid_spec=pltpu.PrefetchScalarGridSpec(
            num_scalar_prefetch=1,
            grid=(count,),
            in_specs=[whole] * count,
            out_specs=pl.BlockSpec((slots, width, model), lambda i, h: ((2 * h[0] + h[1]) ^ i, 0, 0)),
        ),
        out_shape=jax.ShapeDtypeStruct((slots * count, width, model), dtype),
    )(here, *pieces)


def side_by_side(out, up, down):
    rows, width = out.shape
    blocks = down.shape[0] // rows

    def body(out_ref, up_ref, down_ref, to_ref):
        to_ref[:, :width] = out_ref[...]
        to_ref[:, width : width + up.shape[1]] = up_ref[...]
        value = down_ref[...].astype(jnp.float32).reshape(blocks, rows, width)
        for step in range(blocks):
            at = width + up.shape[1] + step * width
            to_ref[:, at : at + width] = value[step].astype(down.dtype)

    total = width + up.shape[1] + blocks * width
    return pl.pallas_call(body, out_shape=jax.ShapeDtypeStruct((rows, total), down.dtype))(out, up, down)


def body(
    sizes,
    tokens,
    cotangent,
    frame_count,
    image_group,
    keep_mask,
    attn_norm_gain,
    attn_norm_bias,
    w_qkv,
    query_bias,
    value_bias,
    w_out,
    out_bias,
    mlp_norm_gain,
    mlp_norm_bias,
    w_up,
    up_bias,
    w_down,
    down_bias,
):
    bf, f32 = jnp.bfloat16, jnp.float32
    here = jnp.stack([lax.axis_index(name) for name in AXES]).astype(jnp.int32)
    peers = sizes[0] * sizes[1]
    frames_here = image_group.shape[1]
    block_width = keep_mask.shape[1] // frames_here
    frame_index = lax.axis_index(FRAME) * frames_here + jnp.arange(frames_here, dtype=jnp.int32)
    segment = jnp.where(frame_index[None, :] < frame_count[:, None], 0, 1 + image_group)
    tags = jnp.repeat(segment, block_width, axis=1) * 2 + keep_mask

    def frame_peer(bits):
        def choose(at):
            at["x"] ^= bits // 2
            at["core"] ^= bits % 2
            return at

        return choose

    def exchange(pieces):
        return list(pieces[:1]) + [swap(sizes, pieces[bits], frame_peer(bits)) for bits in range(1, len(pieces))]

    def slots_for(value):
        own = value.shape[0] // peers
        frame = lax.axis_index(FRAME)
        return [lax.dynamic_slice_in_dim(value, (frame ^ bits) * own, own, 0) for bits in range(peers)]

    rows, model = w_out.shape
    hidden = w_up.shape[1]
    ratio = hidden // model
    vectors = [
        attn_norm_gain, attn_norm_bias, query_bias, value_bias, out_bias, mlp_norm_gain, mlp_norm_bias, down_bias
    ]
    small = columns_of(vectors, up_bias.reshape(rows, ratio))
    slots = tokens.shape[0] // peers
    length = peers * tokens.shape[1]
    here_rows = slots * length
    framed = [((slots, tokens.shape[1], model), bf)] * peers
    full = (slots, length, model)
    wide = (slots, length, hidden)
    scores = 2 * here_rows * length * model
    each = (1,) * slots

    rest = lax.all_gather(side_by_side(w_out, w_up, w_down), AXES, axis=0, tiled=True)
    tags = jnp.pad(tags.astype(bf)[:, None, :], ((0, 0), (0, 7), (0, model - tags.shape[1])))
    x = exchange(slots_for(jnp.concatenate([tokens, tags], axis=1)))
    get_mixed = Gather(sizes, here, jnp.concatenate([w_qkv, small], axis=1))
    get_mixed.stack(x[1:])
    get_mixed.second()
    get_mixed.third()
    mixed, vec = get_mixed.whole(16)
    up_bias_row = vec[8 : 8 + ratio].T.reshape(1, -1)

    attend = (
        attend_kernel,
        [(x, "frames"), (mixed, "whole"), (vec, "whole")],
        [
            (full, bf), ((slots, length, 3 * model), bf), (full, bf), ((slots, HEADS, length, length), bf),
            ((slots, length, 1), jnp.int32),
        ],
    )
    cost = (6 * here_rows * model * model + 8 * scores) // slots
    h1, qkv, o, p, tag_columns = call(*attend, slots, cost * slots)
    cot = exchange(slots_for(copy_after(cotangent, [mixed])))
    x2, h2 = call(
        project_kernel,
        [(x, "frames"), (o, "slot"), (rest, 0), (vec, "whole")],
        [(full, f32), (full, bf)],
        slots,
        2 * here_rows * model * model,
    )
    out, gh, gm, sent, kept, gub, gdb = mlp(here, h2, x2, cot, tag_columns, rest, vec, up_bias_row, rows)
    put_rest = Scatter(sizes, here, sent, kept)
    gx, ga, go, gmg, gmb, gob = call(
        middle_kernel,
        [(gh, "slot"), (rest, 0), (x2, "slot"), (gm, "slot"), (vec, "whole")],
        [(full, f32), (full, bf), (full, bf)] + [((1, model), f32)] * 3,
        slots,
        2 * here_rows * model * model,
    )
    late = out[3:]
    out = exchange(out[:3])
    put_rest.hold([go] + out[1:])
    put_rest.second()
    g_mix, gqb, gvb = call(
        attend_back_kernel,
        [(qkv, "slot"), (go, "slot"), (p, "slot"), (o, "slot")],
        [((slots, length, 3 * model), bf)] + [((1, model), f32)] * 2,
        slots,
        16 * scores,
        after=[put_rest.sent],
    )
    out += [swap(sizes, piece, frame_peer(3 + index)) for index, piece in enumerate(hold(late, [g_mix]))]
    sent, kept = row_grad(here, [(h1, g_mix), (o, ga)], [])
    put_mixed = Scatter(sizes, here, sent, kept)
    put_rest.hold([kept])
    put_rest.third()
    in_grad, gag, gab = call(
        input_kernel,
        [(g_mix, "slot"), (mixed, "whole"), (x, "frames"), (gx, "slot"), (vec, "whole")],
        [framed] + [((1, model), f32)] * 2,
        slots,
        6 * here_rows * model * model,
        after=[put_rest.sent],
    )
    put_mixed.hold([gag])
    put_mixed.second()
    put_rest.hold([put_mixed.sent])
    put_rest.fourth()
    sums = [gag, gab, gqb, gvb, gob, gmg, gmb, gdb]
    pack = turned(sums, gub.reshape(-1, ratio), [put_rest.sent])
    pack = lax.all_to_all(pack.reshape(-1, rows, 128), AXES, 0, 0, tiled=True)
    last = jnp.sum(pack.astype(f32), axis=0)
    put_mixed.hold([put_rest.sent])
    put_mixed.third()
    in_grad = exchange(list(hold(in_grad, [put_mixed.sent])))
    out = list(hold(out, [put_mixed.sent]))
    put_mixed.hold([pack])
    put_mixed.fourth()
    in_grad = list(hold(in_grad, [put_mixed.sent]))
    rest_rows = put_rest.last()
    g_up = rest_rows[:, :hidden]
    g_down = rest_rows[:, hidden:].reshape(rows, ratio, model).transpose(1, 0, 2).reshape(ratio * rows, model)
    mixed_rows = put_mixed.last()
    g_qkv, g_out = mixed_rows[:, : 3 * model], mixed_rows[:, 3 * model :]
    v = [last[:, i] for i in range(8)]
    return (
        join(here, out, bf), join(here, in_grad, f32), v[0], v[1], g_qkv, v[2], v[3], g_out, v[4], v[5], v[6],
        g_up, last[:, 8 : 8 + ratio].reshape(-1), g_down, v[7],
    )


def solution(mesh):
    frames, clips = mesh.shape["frame"], mesh.shape["clip"]
    sizes = (frames // 2, 2, clips // 2, 2)
    mesh = Mesh(mesh.devices.reshape(sizes), AXES)

    def run(*arguments):
        return body(sizes, *arguments)

    placed = (
        P(("z", "y"), FRAME, None),
        P(("z", "y"), FRAME, None),
        P(("z", "y")),
        P(("z", "y"), FRAME),
        P(("z", "y"), FRAME),
        P(AXES),
        P(AXES),
        P(AXES, None),
        P(AXES),
        P(AXES),
        P(AXES, None),
        P(AXES),
        P(AXES),
        P(AXES),
        P(AXES, None),
        P(AXES),
        P(AXES, None),
        P(AXES),
    )
    return jax.shard_map(
        run,
        mesh=mesh,
        in_specs=placed,
        out_specs=(
            P(("z", "y"), FRAME, None),
            P(("z", "y"), FRAME, None),
            P(AXES),
            P(AXES),
            P(AXES, None),
            P(AXES),
            P(AXES),
            P(AXES, None),
            P(AXES),
            P(AXES),
            P(AXES),
            P(AXES, None),
            P(AXES),
            P(AXES, None),
            P(AXES),
        ),
        check_vma=False,
    )
```

```python
import jax
import jax.numpy as jnp
from jax import lax
from jax.experimental import pallas as pl
from jax.experimental.pallas import tpu as pltpu
from jax.sharding import Mesh
from jax.sharding import PartitionSpec as P

HEADS = 12
EPSILON = 1e-06
AXES = ("x", "core", "z", "y")
FRAME = ("x", "core")
ANY = pl.BlockSpec(memory_space=pl.ANY)


def index_of(sizes, at):
    value = 0
    for name, size in zip(AXES, sizes):
        value = value * size + at[name]
    return value


def swap(sizes, value, choose):
    pairs = []
    for x in range(sizes[0]):
        for core in range(sizes[1]):
            for z in range(sizes[2]):
                for y in range(sizes[3]):
                    at = {"x": x, "core": core, "z": z, "y": y}
                    pairs.append((index_of(sizes, at), index_of(sizes, choose(dict(at)))))
    return lax.ppermute(value, AXES, pairs)


def near_peer(at):
    at["y" if at["core"] else "x"] ^= 1
    return at


def far_peer(at):
    at["x" if at["core"] else "y"] ^= 1
    return at


def line_peer(bits):
    def choose(at):
        at["z"] ^= bits
        return at

    return choose


def core_peer(at):
    at["core"] ^= 1
    return at


def cell(core, x, y, near, far):
    return jnp.where(core == 0, x ^ near, x ^ far), jnp.where(core == 0, y ^ far, y ^ near)


def hold(values, after):
    def body(*refs):
        pass

    return pl.pallas_call(
        body,
        in_specs=[ANY] * (len(values) + len(after)),
        out_specs=[ANY] * len(values),
        out_shape=[jax.ShapeDtypeStruct(value.shape, value.dtype) for value in values],
        input_output_aliases={index: index for index in range(len(values))},
    )(*values, *after)


def copy_after(value, after):
    def body(in_ref, *refs):
        refs[-1][...] = in_ref[...]

    return pl.pallas_call(
        body,
        in_specs=[pl.BlockSpec(memory_space=pltpu.VMEM)] + [ANY] * len(after),
        out_specs=pl.BlockSpec(memory_space=pltpu.VMEM),
        out_shape=jax.ShapeDtypeStruct(value.shape, value.dtype),
    )(value, *after)


def columns_of(vectors, tail):
    rows = tail.shape[0]

    def body(*refs):
        out = refs[-1]
        lines = jnp.concatenate([ref[...].astype(jnp.float32) for ref in refs[:-2]], axis=0)
        lines = jnp.pad(lines, ((0, 0), (0, 128 - rows)))
        turned = jnp.pad(lines, ((0, 128 - lines.shape[0]), (0, 0))).T[:rows]
        out[...] = turned.astype(jnp.bfloat16)
        out[:, len(vectors) : len(vectors) + tail.shape[1]] = refs[-2][...]

    return pl.pallas_call(
        body, out_shape=jax.ShapeDtypeStruct((rows, 128), jnp.bfloat16)
    )(*[v.reshape(1, rows) for v in vectors], tail)


class Gather:
    def __init__(self, sizes, here, shard):
        self.sizes, self.here = sizes, here
        self.parts = [shard] + [swap(sizes, shard, line_peer(bits)) for bits in range(1, sizes[2])]

    def stack(self, after=()):
        parts = self.parts[:1] + list(hold(self.parts[1:], after)) if after else self.parts
        self.pieces = {(0, 0): jnp.stack(parts)}
        return [self.pieces[0, 0]]

    def second(self):
        column = self.pieces[0, 0]
        self.pieces[1, 0] = swap(self.sizes, column, near_peer)
        self.pieces[0, 1] = swap(self.sizes, column, far_peer)
        return [self.pieces[1, 0], self.pieces[0, 1]]

    def third(self, after=()):
        (self.pieces[1, 0],) = hold([self.pieces[1, 0]], [self.pieces[0, 1]] + list(after))
        self.pieces[1, 1] = swap(self.sizes, self.pieces[1, 0], far_peer)
        return [self.pieces[1, 1]]

    def whole(self, lines=0, after=()):
        if after:
            (self.pieces[1, 1],) = hold([self.pieces[1, 1]], after)
        keys = sorted(self.pieces)
        mine = [self.pieces[key] for key in keys]
        theirs = [swap(self.sizes, piece, core_peer) for piece in mine]
        count, rows, width = mine[0].shape
        total = 2 * len(keys)
        devices = self.sizes[0] * self.sizes[1] * self.sizes[2] * self.sizes[3]

        def body(here_ref, *refs):
            out, sems = refs[total], refs[-1]
            copies = []
            for side in range(2):
                core = here_ref[1] ^ side
                for index, (near, far) in enumerate(keys):
                    x, y = cell(core, here_ref[0], here_ref[3], near, far)
                    slot = side * len(keys) + index
                    for bits in range(count):
                        to = out.at[x, core, here_ref[2] ^ bits, y]
                        copies.append(pltpu.make_async_copy(refs[slot].at[bits], to, sems.at[slot * count + bits]))
            for copy in copies:
                copy.start()
            for copy in copies:
                copy.wait()
            if lines:
                tail = out[..., width - 128 :].astype(jnp.float32).reshape(devices * rows, 128)
                refs[total + 1][...] = tail.T[:lines]

        vmem = pl.BlockSpec(memory_space=pltpu.VMEM)
        shapes = [jax.ShapeDtypeStruct((self.sizes[0], 2, count, 2, rows, width), mine[0].dtype)]
        if lines:
            shapes.append(jax.ShapeDtypeStruct((lines, devices * rows), jnp.float32))
        results = pl.pallas_call(
            body,
            in_specs=[pl.BlockSpec(memory_space=pltpu.SMEM)] + [ANY] * total,
            out_specs=[vmem] * len(shapes),
            out_shape=shapes,
            scratch_shapes=[pltpu.SemaphoreType.DMA((total * count,))],
        )(self.here, *mine, *theirs)
        full = results[0].reshape(-1, width)
        return (full, results[1]) if lines else full


class Scatter:
    def __init__(self, sizes, here, sent, kept):
        self.sizes, self.here = sizes, here
        rows = kept.shape[1] // (sizes[2] * 2)
        shape = (sizes[0], sizes[2], 2, rows, kept.shape[2])
        self.terms = [kept.reshape(shape), swap(sizes, sent.reshape(shape), core_peer)]

    def hold(self, after):
        self.terms[0] = hold(self.terms[:1], after)[0]

    def add(self, cells):
        _, count, _, rows, width = self.terms[0].shape
        steps = len(cells)
        used = len(self.terms)
        near, first = cells[0]

        def body(here_ref, *refs):
            for bit in range(2):
                z = (here_ref[2] & 1) ^ bit
                value = refs[0][0, z, 0].astype(jnp.float32) + refs[1][0, z, 0].astype(jnp.float32)
                for ref in refs[2:used]:
                    value += ref[0, bit].astype(jnp.float32)
                refs[used][0, bit] = value.astype(jnp.bfloat16)

        def place(step, pair, here_ref):
            far = first if steps == 1 else step
            x, y = cell(here_ref[1], here_ref[0], here_ref[3], near, far)
            return x, (here_ref[2] >> 1) ^ pair, y, 0, 0

        plain = (1, 2, rows, width)
        specs = [pl.BlockSpec((1, 2, 1, rows, width), place)] * 2
        for term in self.terms[2:]:
            many = term.shape[0] > 1
            specs.append(
                pl.BlockSpec(plain, lambda i, b, h, m=many: ((first if steps == 1 else i) if m else 0, b, 0, 0))
            )
        return pl.pallas_call(
            body,
            grid_spec=pltpu.PrefetchScalarGridSpec(
                num_scalar_prefetch=1,
                grid=(steps, count // 2),
                in_specs=specs,
                out_specs=pl.BlockSpec(plain, lambda i, b, h: (i, b, 0, 0)),
            ),
            out_shape=jax.ShapeDtypeStruct((steps, count, rows, width), jnp.bfloat16),
            cost_estimate=pl.CostEstimate(
                flops=0, bytes_accessed=2 * steps * count * rows * width * (used + 1), transcendentals=0
            ),
        )(self.here, *self.terms)

    def second(self):
        self.sent = self.add([(1, 0), (1, 1)])
        self.terms.append(swap(self.sizes, self.sent, near_peer))

    def third(self):
        self.sent = self.add([(0, 1)])
        self.terms.append(swap(self.sizes, self.sent, far_peer))

    def fourth(self):
        value = self.add([(0, 0)])[0]
        self.sent = value
        self.parts = [value[0]]
        for bits in range(1, self.sizes[2]):
            self.parts.append(swap(self.sizes, value[bits], line_peer(bits)))

    def last(self):
        return sum(part.astype(jnp.float32) for part in self.parts)


ROOT_HALF = 0.7071067811865476
DENSITY = 0.3989422804014327
NT = (((1,), (1,)), ((), ()))
NN = (((1,), (0,)), ((), ()))
TN = (((0,), (0,)), ((), ()))


def dot(left, right, dims=NN):
    return lax.dot_general(left, right, dims, preferred_element_type=jnp.float32)


def normalize(values):
    center = values - jnp.mean(values, axis=-1, keepdims=True)
    spread = jnp.mean(center * center, axis=-1, keepdims=True)
    scale = lax.rsqrt(spread + EPSILON)
    return center * scale, scale


def gelu_parts(u):
    size = jnp.abs(u)
    bell = jnp.exp(-0.5 * (u * u))
    t = 1.0 / (1.0 + (0.3275911 * ROOT_HALF) * size)
    poly = t * (
        0.5 * 0.254829592
        + t * (0.5 * -0.284496736 + t * (0.5 * 1.421413741 + t * (0.5 * -1.453152027 + t * (0.5 * 1.061405429))))
    )
    tail = poly * bell
    value = jnp.maximum(u, 0.0) - size * tail
    slope = jnp.where(u > 0, 1.0 - tail, tail) + DENSITY * (u * bell)
    return value, slope


def add_rows(ref, values):
    total = jnp.sum(values, axis=0, keepdims=True)

    @pl.when(pl.program_id(0) == 0)
    def _():
        ref[...] = total

    @pl.when(pl.program_id(0) != 0)
    def _():
        ref[...] += total


def rows_of(refs):
    return jnp.concatenate([ref[0, : ref.shape[1] - 8] for ref in refs], axis=0)


def tags_of(refs):
    width = refs[0].shape[1] - 8
    rows = width * len(refs)
    column, line = None, None
    for index, ref in enumerate(refs):
        tags = ref[0, width:, :128]
        row = lax.broadcasted_iota(jnp.int32, (rows, 128), 0)
        place = lax.broadcasted_iota(jnp.int32, (rows, 128), 1) + index * width
        chosen = jnp.where(row == place, 1.0, 0.0).astype(jnp.bfloat16)
        one, other = dot(chosen, tags, NT), dot(tags, chosen, NT)
        column = one if column is None else column + one
        line = other if line is None else line + other
    return column[:, :1].astype(jnp.int32), line[:1].astype(jnp.int32)


def spread(refs, rows):
    width = refs[0].shape[1]
    for index, ref in enumerate(refs):
        ref[0] = rows[index * width : (index + 1) * width]


def attend_kernel(x_ref, w_ref, vec_ref, h_ref, qkv_ref, o_ref, p_ref, tag_ref):
    model = x_ref[0].shape[-1]
    head = model // HEADS
    n, _ = normalize(rows_of(x_ref).astype(jnp.float32))
    low = (n * vec_ref[0:1] + vec_ref[1:2]).astype(jnp.bfloat16)
    h_ref[0] = low
    q = dot(low, w_ref[:, :model]) + vec_ref[2:3]
    qkv_ref[0, :, :model] = q.astype(jnp.bfloat16) * jnp.bfloat16(head**-0.5)
    qkv_ref[0, :, model : 2 * model] = dot(low, w_ref[:, model : 2 * model]).astype(jnp.bfloat16)
    v = dot(low, w_ref[:, 2 * model : 3 * model]) + vec_ref[3:4]
    qkv_ref[0, :, 2 * model :] = v.astype(jnp.bfloat16)
    column, line = tags_of(x_ref)
    tag_ref[0] = column
    code = jnp.where(line & 1 == 1, line >> 1, -1)
    bias = jnp.where(column >> 1 == code, 0.0, -1e30)
    for i in range(HEADS):
        at = slice(i * head, (i + 1) * head)
        k_at = slice(model + i * head, model + (i + 1) * head)
        v_at = slice(2 * model + i * head, 2 * model + (i + 1) * head)
        s = dot(qkv_ref[0, :, at], qkv_ref[0, :, k_at], NT) + bias
        e = jnp.exp(s - jnp.max(s, axis=-1, keepdims=True))
        p = (e * (1.0 / jnp.sum(e, axis=-1, keepdims=True))).astype(jnp.bfloat16)
        p_ref[0, i] = p
        o_ref[0, :, at] = dot(p, qkv_ref[0, :, v_at]).astype(jnp.bfloat16)


def project_kernel(x_ref, o_ref, wo_ref, vec_ref, x2_ref, h2_ref):
    x2 = rows_of(x_ref).astype(jnp.float32) + (dot(o_ref[0], wo_ref[...]) + vec_ref[4:5])
    x2_ref[0] = x2
    n, _ = normalize(x2)
    h2_ref[0] = (n * vec_ref[5:6] + vec_ref[6:7]).astype(jnp.bfloat16)


def mlp(here, h2, x2, cot, tags, rest, vec, up_bias, shard):
    slots, length, model = h2.shape
    rows = slots * length
    hidden = up_bias.shape[1]
    steps = hidden // model
    peers = len(cot)
    chunk = model // peers
    bf, f32 = jnp.bfloat16, jnp.float32

    def body(here_ref, h2_ref, x2_ref, tag_ref, vec_ref, u_ref, b_ref, *refs):
        cot_refs = refs[:peers]
        down_refs = refs[peers : peers + steps]
        out_refs = refs[peers + steps : 2 * peers + steps]
        gh_ref, gm_ref, sent_ref, kept_ref, gub_ref, gdb_ref, y_acc, gh_acc, ups, downs, sems = refs[
            2 * peers + steps :
        ]
        step = pl.program_id(0)
        core = here_ref[1]

        @pl.when(step == 0)
        def _():
            total = jnp.zeros((1, model), f32)
            for slot in range(slots):
                keep = (tag_ref[slot] & 1).astype(f32)
                gy = keep * jnp.concatenate([ref[slot] for ref in cot_refs], axis=0).astype(f32)
                gm_ref[slot] = gy.astype(bf)
                total += jnp.sum(gy, axis=0, keepdims=True)
            gdb_ref[...] = total

        h2 = h2_ref[...].reshape(rows, model)
        gm = gm_ref[...].reshape(rows, model)
        up = u_ref[...]
        parts = [ref[...].astype(f32).reshape(-1, 1, shard, model) for ref in down_refs]
        down = jnp.concatenate(parts, axis=1).reshape(model, model).astype(bf)
        value, slope = gelu_parts(dot(h2, up) + b_ref[...])
        a = value.astype(bf)
        y = dot(a, down)
        gu32 = dot(gm, down, NT) * slope
        gu = gu32.astype(bf)
        gub_ref[...] = jnp.sum(gu.astype(f32), axis=0, keepdims=True)
        gh = dot(gu, up, NT)

        @pl.when(step == 0)
        def _():
            y_acc[...] = y
            gh_acc[...] = gh

        @pl.when(step != 0)
        def _():
            y_acc[...] += y
            gh_acc[...] += gh

        g_down = dot(a, gm, TN).reshape(-1, steps, shard, model)
        g_up = dot(h2, gu, TN).astype(bf).reshape(ups.shape)
        up_at = pl.ds(pl.multiple_of(at(step, here_ref) * model, 128), model)

        def up_copies():
            found = []
            for x in range(2):
                found.append(pltpu.make_async_copy(ups.at[2 * x + (1 - core)], sent_ref.at[x, :, up_at], sems.at[2 * x]))
                found.append(pltpu.make_async_copy(ups.at[2 * x + core], kept_ref.at[x, :, up_at], sems.at[2 * x + 1]))
            return found

        def down_copies(to_ref):
            return [
                pltpu.make_async_copy(
                    downs.at[part],
                    to_ref.at[step % 2, :, pl.ds(hidden + part * model, model)],
                    sems.at[4 + part],
                )
                for part in range(steps)
            ]

        @pl.when(step != 0)
        def _():
            for copy in up_copies() + down_copies(kept_ref):
                copy.wait()

        ups[...] = g_up
        for part in range(steps):
            downs[part] = g_down[:, part].reshape(chunk, model).astype(bf)
        for copy in up_copies():
            copy.start()

        @pl.when(step < steps // 2)
        def _():
            for copy in down_copies(sent_ref):
                copy.start()

        @pl.when(step >= steps // 2)
        def _():
            for copy in down_copies(kept_ref):
                copy.start()

        @pl.when(step == steps - 1)
        def _():
            width = length // peers
            for slot in range(slots):
                y = y_acc[slot * length : (slot + 1) * length] + vec_ref[7:8]
                keep = (tag_ref[slot] & 1).astype(f32)
                result = (keep * (x2_ref[slot] + y)).astype(bf)
                for index, ref in enumerate(out_refs):
                    ref[slot] = result[index * width : (index + 1) * width]
            gh_ref[...] = gh_acc[...].reshape(gh_ref.shape)
            for copy in up_copies() + down_copies(kept_ref):
                copy.wait()

    def at(step, here_ref):
        return 2 * (step % 2) + (here_ref[1] ^ (1 - step // 2))

    full = pl.BlockSpec((slots, length, model), lambda i, h: (0, 0, 0))
    shape = (slots, length, model)
    side = jax.ShapeDtypeStruct((2, chunk, 2 * hidden), bf)
    line = jax.ShapeDtypeStruct((1, model), f32)
    results = pl.pallas_call(
        body,
        grid_spec=pltpu.PrefetchScalarGridSpec(
            num_scalar_prefetch=1,
            grid=(steps,),
            in_specs=[
                full,
                full,
                pl.BlockSpec(tags.shape, lambda i, h: (0, 0, 0)),
                pl.BlockSpec(vec.shape, lambda i, h: (0, 0)),
                pl.BlockSpec((model, model), lambda i, h: (0, 1 + at(i, h))),
                pl.BlockSpec((1, model), lambda i, h: (0, at(i, h))),
            ]
            + [pl.BlockSpec(cot[0].shape, lambda i, h: (0, 0, 0))] * peers
            + [
                pl.BlockSpec((chunk, model), lambda i, h, c=1 + steps + step: (at(i, h), c))
                for step in range(steps)
            ],
            out_specs=[pl.BlockSpec(cot[0].shape, lambda i, h: (0, 0, 0))] * peers
            + [
                full,
                full,
                ANY,
                ANY,
                pl.BlockSpec((1, model), lambda i, h: (0, at(i, h))),
                pl.BlockSpec((1, model), lambda i, h: (0, 0)),
            ],
            scratch_shapes=[
                pltpu.VMEM((rows, model), f32),
                pltpu.VMEM((rows, model), f32),
                pltpu.VMEM((4, chunk, model), bf),
                pltpu.VMEM((steps, chunk, model), bf),
                pltpu.SemaphoreType.DMA((4 + steps,)),
            ],
        ),
        out_shape=[jax.ShapeDtypeStruct(cot[0].shape, bf)] * peers
        + [
            jax.ShapeDtypeStruct(shape, f32),
            jax.ShapeDtypeStruct(shape, bf),
            side,
            side,
            jax.ShapeDtypeStruct((1, hidden), f32),
            line,
        ],
        compiler_params=pltpu.CompilerParams(vmem_limit_bytes=58 * 1024 * 1024),
        cost_estimate=pl.CostEstimate(
            flops=12 * rows * model * hidden, bytes_accessed=30 * rows * model, transcendentals=rows * hidden
        ),
    )(here, h2, x2, tags, vec, rest, up_bias, *cot, *([rest] * steps))
    return [list(results[:peers])] + list(results[peers:])


def norm_back(grad, n, scale, gain):
    gn = grad * gain
    mean = jnp.mean(gn, axis=-1, keepdims=True)
    cross = jnp.mean(gn * n, axis=-1, keepdims=True)
    return (gn - mean - n * cross) * scale


def middle_kernel(gh_ref, wo_ref, x2_ref, gm_ref, vec_ref, gx_ref, ga_ref, go_ref, gg_ref, gb_ref, gob_ref):
    gh = gh_ref[0]
    n, scale = normalize(x2_ref[0])
    add_rows(gg_ref, gh * n)
    add_rows(gb_ref, gh)
    gx = gm_ref[0].astype(jnp.float32) + norm_back(gh, n, scale, vec_ref[5:6])
    gx_ref[0] = gx
    low = gx.astype(jnp.bfloat16)
    ga_ref[0] = low
    add_rows(gob_ref, low.astype(jnp.float32))
    go_ref[0] = dot(low, wo_ref[...], NT).astype(jnp.bfloat16)


def attend_back_kernel(qkv_ref, go_ref, p_ref, o_ref, g_ref, gqb_ref, gvb_ref):
    model = go_ref.shape[-1]
    head = model // HEADS
    turned_go = go_ref[0].T
    turned_q = qkv_ref[0, :, :model].T
    for i in range(HEADS):
        at = slice(i * head, (i + 1) * head)
        k_at = slice(model + i * head, model + (i + 1) * head)
        v_at = slice(2 * model + i * head, 2 * model + (i + 1) * head)
        go = go_ref[0, :, at]
        p = p_ref[0, i]
        dp = dot(go, qkv_ref[0, :, v_at], NT)
        delta = jnp.sum(go.astype(jnp.float32) * o_ref[0, :, at].astype(jnp.float32), axis=-1, keepdims=True)
        ds = (p.astype(jnp.float32) * (dp - delta)).astype(jnp.bfloat16)
        g_ref[0, :, at] = (dot(ds, qkv_ref[0, :, k_at]) * head**-0.5).astype(jnp.bfloat16)
        g_ref[0, :, k_at] = dot(turned_q[at], ds).T.astype(jnp.bfloat16)
        g_ref[0, :, v_at] = dot(turned_go[at], p).T.astype(jnp.bfloat16)
    add_rows(gqb_ref, g_ref[0, :, :model].astype(jnp.float32))
    add_rows(gvb_ref, g_ref[0, :, 2 * model :].astype(jnp.float32))


def input_kernel(g_ref, w_ref, x_ref, gx_ref, vec_ref, out_ref, gg_ref, gb_ref):
    model = x_ref[0].shape[-1]
    gh = dot(g_ref[0], w_ref[:, : 3 * model], NT)
    n, scale = normalize(rows_of(x_ref).astype(jnp.float32))
    add_rows(gg_ref, gh * n)
    add_rows(gb_ref, gh)
    grad = gx_ref[0] + norm_back(gh, n, scale, vec_ref[0:1])
    spread(out_ref, grad.astype(jnp.bfloat16))


def call(kernel, inputs, outputs, slots, flops, first=0, carry=None, after=(), limit=56):
    specs = []
    arrays = []
    groups = []

    def slot_spec(shape):
        return pl.BlockSpec((1,) + shape[1:], lambda i, n=len(shape) - 1: (i + first,) + (0,) * n)

    for array, kind in inputs:
        if kind == "frames":
            groups.append(len(array))
            arrays += array
            specs += [slot_spec(piece.shape) for piece in array]
            continue
        groups.append(0)
        arrays.append(array)
        if kind == "slot":
            specs.append(slot_spec(array.shape))
        elif kind == "whole":
            specs.append(pl.BlockSpec(array.shape, lambda i, n=array.ndim: (0,) * n))
        else:
            rows = array.shape[0]
            specs.append(pl.BlockSpec((rows, rows), lambda i, j=kind: (0, j)))
    used = len(arrays)
    extra = list(after)
    shapes = []
    places = []
    aliases = {}
    for output in outputs:
        parts = output if isinstance(output, list) else [output]
        groups.append(len(parts) if isinstance(output, list) else 0)
        for shape, dtype in parts:
            shapes.append(jax.ShapeDtypeStruct(shape, dtype))
            if len(shape) > 2:
                places.append(slot_spec(shape))
                if carry is not None:
                    aliases[used + len(extra)] = len(shapes) - 1
                    extra.append(carry[len(shapes) - 1])
            else:
                places.append(pl.BlockSpec(shape, lambda i: (0, 0)))
    moved = sum(s.size * s.dtype.itemsize for s in arrays + shapes)
    skip = used + len(extra)

    def run(*refs):
        refs = list(refs[:used]) + list(refs[skip:])
        arguments = []
        for size in groups:
            arguments.append(refs[:size] if size else refs[0])
            refs = refs[size or 1 :]
        kernel(*arguments)

    results = pl.pallas_call(
        run,
        grid=(slots,),
        in_specs=specs + [ANY] * len(extra),
        out_specs=places,
        out_shape=shapes,
        input_output_aliases=aliases,
        compiler_params=pltpu.CompilerParams(vmem_limit_bytes=limit * 1024 * 1024),
        cost_estimate=pl.CostEstimate(flops=flops, bytes_accessed=moved, transcendentals=0),
    )(*arrays, *extra)
    final = []
    for output in outputs:
        size = len(output) if isinstance(output, list) else 0
        final.append(list(results[:size]) if size else results[0])
        results = results[size or 1 :]
    return final


def row_grad(here, products, after):
    slots, length, model = products[0][0].shape
    steps = []
    for index, (_, right) in enumerate(products):
        steps += [index] * (right.shape[2] // model)
    starts = [steps.index(index) for index in range(len(products))]
    chunk = model // 4
    used = 2 * len(products)

    def body(here_ref, *refs):
        sent_ref, kept_ref, value_ref = refs[-3:]
        core = here_ref[1]
        step = pl.program_id(0)
        for index in range(len(products)):
            end = starts[index] + steps.count(index)

            @pl.when((step >= starts[index]) & (step < end))
            def _():
                left, right = refs[2 * index], refs[2 * index + 1]
                value = dot(left[...].reshape(-1, model), right[...].reshape(-1, model), TN)
                value_ref[...] = value.astype(jnp.bfloat16).reshape(value_ref.shape)

        for x in range(2):
            sent_ref[x] = value_ref[2 * x + (1 - core)]
            kept_ref[x] = value_ref[2 * x + core]

    specs = []
    for index, (left, right) in enumerate(products):
        most = right.shape[2] // model - 1
        specs.append(pl.BlockSpec((slots, length, model), lambda i, h: (0, 0, 0)))
        specs.append(
            pl.BlockSpec(
                (slots, length, model),
                lambda i, h, s=starts[index], m=most: (0, 0, jnp.clip(i - s, 0, m)),
            )
        )
    shape = jax.ShapeDtypeStruct((2, chunk, len(steps) * model), jnp.bfloat16)
    out = pl.BlockSpec((2, chunk, model), lambda i, h: (0, 0, i))
    return pl.pallas_call(
        body,
        grid_spec=pltpu.PrefetchScalarGridSpec(
            num_scalar_prefetch=1,
            grid=(len(steps),),
            in_specs=specs + [ANY] * len(after),
            out_specs=[out, out],
            scratch_shapes=[pltpu.VMEM((4, chunk, model), jnp.bfloat16)],
        ),
        out_shape=[shape, shape],
        compiler_params=pltpu.CompilerParams(vmem_limit_bytes=56 * 1024 * 1024),
        cost_estimate=pl.CostEstimate(
            flops=2 * slots * length * model * model * len(steps),
            bytes_accessed=2 * sum(r.size for _, r in products),
            transcendentals=0,
        ),
    )(here, *[array for pair in products for array in pair], *after)


def turned(lines, tail, after):
    width = lines[0].shape[1]
    used = len(lines)

    def body(*refs):
        out = refs[-1]
        value = jnp.concatenate([ref[...] for ref in refs[:used]], axis=0)
        value = jnp.pad(value, ((0, 128 - value.shape[0]), (0, 0))).T
        out[...] = value.astype(jnp.bfloat16)
        out[:, used : used + tail.shape[1]] = refs[used][...].astype(jnp.bfloat16)

    vmem = pl.BlockSpec(memory_space=pltpu.VMEM)
    return pl.pallas_call(
        body,
        in_specs=[vmem] * (used + 1) + [ANY] * len(after),
        out_specs=vmem,
        out_shape=jax.ShapeDtypeStruct((width, 128), jnp.bfloat16),
    )(*lines, tail, *after)


def join(here, pieces, dtype):
    slots, width, model = pieces[0].shape
    count = len(pieces)

    def body(here_ref, *refs):
        for step in range(count):

            @pl.when(pl.program_id(0) == step)
            def _():
                refs[-1][...] = refs[step][...].astype(dtype)

    whole = pl.BlockSpec((slots, width, model), lambda i, h: (0, 0, 0))
    return pl.pallas_call(
        body,
        grid_spec=pltpu.PrefetchScalarGridSpec(
            num_scalar_prefetch=1,
            grid=(count,),
            in_specs=[whole] * count,
            out_specs=pl.BlockSpec((slots, width, model), lambda i, h: ((2 * h[0] + h[1]) ^ i, 0, 0)),
        ),
        out_shape=jax.ShapeDtypeStruct((slots * count, width, model), dtype),
    )(here, *pieces)


def side_by_side(out, up, down):
    rows, width = out.shape
    blocks = down.shape[0] // rows

    def body(out_ref, up_ref, down_ref, to_ref):
        to_ref[:, :width] = out_ref[...]
        to_ref[:, width : width + up.shape[1]] = up_ref[...]
        value = down_ref[...].astype(jnp.float32).reshape(blocks, rows, width)
        for step in range(blocks):
            at = width + up.shape[1] + step * width
            to_ref[:, at : at + width] = value[step].astype(down.dtype)

    total = width + up.shape[1] + blocks * width
    return pl.pallas_call(body, out_shape=jax.ShapeDtypeStruct((rows, total), down.dtype))(out, up, down)


def body(
    sizes,
    tokens,
    cotangent,
    frame_count,
    image_group,
    keep_mask,
    attn_norm_gain,
    attn_norm_bias,
    w_qkv,
    query_bias,
    value_bias,
    w_out,
    out_bias,
    mlp_norm_gain,
    mlp_norm_bias,
    w_up,
    up_bias,
    w_down,
    down_bias,
):
    bf, f32 = jnp.bfloat16, jnp.float32
    here = jnp.stack([lax.axis_index(name) for name in AXES]).astype(jnp.int32)
    peers = sizes[0] * sizes[1]
    frames_here = image_group.shape[1]
    block_width = keep_mask.shape[1] // frames_here
    frame_index = lax.axis_index(FRAME) * frames_here + jnp.arange(frames_here, dtype=jnp.int32)
    segment = jnp.where(frame_index[None, :] < frame_count[:, None], 0, 1 + image_group)
    tags = jnp.repeat(segment, block_width, axis=1) * 2 + keep_mask

    def frame_peer(bits):
        def choose(at):
            at["x"] ^= bits // 2
            at["core"] ^= bits % 2
            return at

        return choose

    def exchange(pieces):
        return list(pieces[:1]) + [swap(sizes, pieces[bits], frame_peer(bits)) for bits in range(1, len(pieces))]

    def slots_for(value):
        own = value.shape[0] // peers
        frame = lax.axis_index(FRAME)
        return [lax.dynamic_slice_in_dim(value, (frame ^ bits) * own, own, 0) for bits in range(peers)]

    rows, model = w_out.shape
    hidden = w_up.shape[1]
    ratio = hidden // model
    vectors = [
        attn_norm_gain, attn_norm_bias, query_bias, value_bias, out_bias, mlp_norm_gain, mlp_norm_bias, down_bias
    ]
    small = columns_of(vectors, up_bias.reshape(rows, ratio))
    slots = tokens.shape[0] // peers
    length = peers * tokens.shape[1]
    here_rows = slots * length
    framed = [((slots, tokens.shape[1], model), bf)] * peers
    full = (slots, length, model)
    wide = (slots, length, hidden)
    scores = 2 * here_rows * length * model
    each = (1,) * slots

    rest = lax.all_gather(side_by_side(w_out, w_up, w_down), AXES, axis=0, tiled=True)
    tags = jnp.pad(tags.astype(bf)[:, None, :], ((0, 0), (0, 7), (0, model - tags.shape[1])))
    x = exchange(slots_for(jnp.concatenate([tokens, tags], axis=1)))
    get_mixed = Gather(sizes, here, jnp.concatenate([w_qkv, small], axis=1))
    get_mixed.stack(x[1:])
    get_mixed.second()
    get_mixed.third()
    mixed, vec = get_mixed.whole(16)
    up_bias_row = vec[8 : 8 + ratio].T.reshape(1, -1)

    attend = (
        attend_kernel,
        [(x, "frames"), (mixed, "whole"), (vec, "whole")],
        [
            (full, bf), ((slots, length, 3 * model), bf), (full, bf), ((slots, HEADS, length, length), bf),
            ((slots, length, 1), jnp.int32),
        ],
    )
    cost = (6 * here_rows * model * model + 8 * scores) // slots
    h1, qkv, o, p, tag_columns = call(*attend, slots, cost * slots)
    cot = exchange(slots_for(copy_after(cotangent, [mixed])))
    x2, h2 = call(
        project_kernel,
        [(x, "frames"), (o, "slot"), (rest, 0), (vec, "whole")],
        [(full, f32), (full, bf)],
        slots,
        2 * here_rows * model * model,
    )
    out, gh, gm, sent, kept, gub, gdb = mlp(here, h2, x2, cot, tag_columns, rest, vec, up_bias_row, rows)
    put_rest = Scatter(sizes, here, sent, kept)
    gx, ga, go, gmg, gmb, gob = call(
        middle_kernel,
        [(gh, "slot"), (rest, 0), (x2, "slot"), (gm, "slot"), (vec, "whole")],
        [(full, f32), (full, bf), (full, bf)] + [((1, model), f32)] * 3,
        slots,
        2 * here_rows * model * model,
    )
    late = out[3:]
    out = exchange(out[:3])
    put_rest.hold([go] + out[1:])
    put_rest.second()
    g_mix, gqb, gvb = call(
        attend_back_kernel,
        [(qkv, "slot"), (go, "slot"), (p, "slot"), (o, "slot")],
        [((slots, length, 3 * model), bf)] + [((1, model), f32)] * 2,
        slots,
        16 * scores,
        after=[put_rest.sent],
    )
    out += [swap(sizes, piece, frame_peer(3 + index)) for index, piece in enumerate(hold(late, [g_mix]))]
    sent, kept = row_grad(here, [(h1, g_mix), (o, ga)], [])
    put_mixed = Scatter(sizes, here, sent, kept)
    put_rest.hold([kept])
    put_rest.third()
    in_grad, gag, gab = call(
        input_kernel,
        [(g_mix, "slot"), (mixed, "whole"), (x, "frames"), (gx, "slot"), (vec, "whole")],
        [framed] + [((1, model), f32)] * 2,
        slots,
        6 * here_rows * model * model,
        after=[put_rest.sent],
    )
    put_mixed.hold([gag])
    put_mixed.second()
    put_rest.hold([put_mixed.sent])
    put_rest.fourth()
    sums = [gag, gab, gqb, gvb, gob, gmg, gmb, gdb]
    pack = turned(sums, gub.reshape(-1, ratio), [put_rest.sent])
    pack = lax.all_to_all(pack.reshape(-1, rows, 128), AXES, 0, 0, tiled=True)
    last = jnp.sum(pack.astype(f32), axis=0)
    put_mixed.hold([put_rest.sent])
    put_mixed.third()
    in_grad = exchange(list(hold(in_grad, [put_mixed.sent])))
    out = list(hold(out, [put_mixed.sent]))
    put_mixed.fourth()
    in_grad = list(hold(in_grad, [put_mixed.sent]))
    rest_rows = put_rest.last()
    g_up = rest_rows[:, :hidden]
    g_down = rest_rows[:, hidden:].reshape(rows, ratio, model).transpose(1, 0, 2).reshape(ratio * rows, model)
    mixed_rows = put_mixed.last()
    g_qkv, g_out = mixed_rows[:, : 3 * model], mixed_rows[:, 3 * model :]
    v = [last[:, i] for i in range(8)]
    return (
        join(here, out, bf), join(here, in_grad, f32), v[0], v[1], g_qkv, v[2], v[3], g_out, v[4], v[5], v[6],
        g_up, last[:, 8 : 8 + ratio].reshape(-1), g_down, v[7],
    )


def solution(mesh):
    frames, clips = mesh.shape["frame"], mesh.shape["clip"]
    sizes = (frames // 2, 2, clips // 2, 2)
    mesh = Mesh(mesh.devices.reshape(sizes), AXES)

    def run(*arguments):
        return body(sizes, *arguments)

    placed = (
        P(("z", "y"), FRAME, None),
        P(("z", "y"), FRAME, None),
        P(("z", "y")),
        P(("z", "y"), FRAME),
        P(("z", "y"), FRAME),
        P(AXES),
        P(AXES),
        P(AXES, None),
        P(AXES),
        P(AXES),
        P(AXES, None),
        P(AXES),
        P(AXES),
        P(AXES),
        P(AXES, None),
        P(AXES),
        P(AXES, None),
        P(AXES),
    )
    return jax.shard_map(
        run,
        mesh=mesh,
        in_specs=placed,
        out_specs=(
            P(("z", "y"), FRAME, None),
            P(("z", "y"), FRAME, None),
            P(AXES),
            P(AXES),
            P(AXES, None),
            P(AXES),
            P(AXES),
            P(AXES, None),
            P(AXES),
            P(AXES),
            P(AXES),
            P(AXES, None),
            P(AXES),
            P(AXES, None),
            P(AXES),
        ),
        check_vma=False,
    )
```
